32 devices in a mesh: dp: 8 (over z, x), tensor: 4 (over y, core).
Axes of the slice: x: 2, y: 2, z: 4, core: 2. Of those that a mesh axis runs over, the one named last changes fastest.
Arguments:
- hidden_in: bfloat16 [12288, 768], P('dp'), may hold values from -6 to 6
- token_mask: int32 [12288], P('dp'), may hold values from 0 to 1, as said below
- bucket: int32 [24], P('dp'), may hold values from 0 to 1, as said below
- positive: int32 [192], P('dp'), may hold values from 0 to 47, as said below
- qkv_weight: bfloat16 [3, 768, 768], P(None, None, 'tensor'), may hold values from -0.21875 to 0.21875
- qv_bias: bfloat16 [2, 768], P(None, 'tensor'), may hold values from -3 to 3
- out_weight: bfloat16 [768, 768], P('tensor'), may hold values from -1.25 to 1.25
- out_bias: bfloat16 [768], replicated, may hold values from -3 to 3
- norm1_gain: bfloat16 [768], replicated, may hold values from 0.25 to 1.75
- norm1_bias: bfloat16 [768], replicated, may hold values from -2 to 2
- ffn_in: bfloat16 [768, 3072], P(None, 'tensor'), may hold values from -0.21875 to 0.21875
- ffn_in_bias: bfloat16 [3072], P('tensor'), may hold values from -3 to 3
- ffn_out: bfloat16 [3072, 768], P('tensor'), may hold values from -0.15625 to 0.15625
- ffn_out_bias: bfloat16 [768], replicated, may hold values from -3 to 3
- norm2_gain: bfloat16 [768], replicated, may hold values from 0.25 to 1.75
- norm2_bias: bfloat16 [768], replicated, may hold values from -2 to 2
- upstream: bfloat16 [12288, 768], P('dp'), may hold values from -6 to 6
Outputs:
- layer_out: bfloat16 [12288, 768], P('dp')
- query_emb: bfloat16 [192, 768], P('dp')
- passage_emb: bfloat16 [48, 768], P('dp')
- loss: float32 [], replicated
- grad_in: float32 [12288, 768], P('dp')
- grad_qkv: float32 [3, 768, 768], P(None, None, 'tensor')
- grad_qv_bias: float32 [2, 768], P(None, 'tensor')
- grad_out_weight: float32 [768, 768], P('tensor')
- grad_out_bias: float32 [768], replicated
- grad_norm1_gain: float32 [768], replicated
- grad_norm1_bias: float32 [768], replicated
- grad_ffn_in: float32 [768, 3072], P(None, 'tensor')
- grad_ffn_in_bias: float32 [3072], P('tensor')
- grad_ffn_out: float32 [3072, 768], P('tensor')
- grad_ffn_out_bias: float32 [768], replicated
- grad_norm2_gain: float32 [768], replicated
- grad_norm2_bias: float32 [768], replicated
The draws below stay inside these ranges and needn't reach their ends.
Inputs may be any that keep to these rules, and one draw needn't show every extreme that they name: `token_mask`: each block of 1536 rows holds 3 slots of 256 rows, then 24 queries of 32 rows. The real tokens of every sequence are a prefix of it: a bucket 1 slot has more than half of 256 real tokens, each half of a bucket 0 slot has from a quarter to a half of 256, a query has a quarter of 32 or more. The first slot has bucket 1 and the last slot bucket 0. `positive`: always a live candidate: 2 * s for some slot s, or 2 * s + 1 for a slot s of bucket 0.
All inputs are finite; a program needn't handle non-finite values.
Results may differ from the reference program's by a relative error of at most 0.015.
Values may be sent and summed in bfloat16 or wider, within the bound.
A program may use at most 128 MiB of HBM per device.

```python
import math
import jax
import jax.numpy as jnp
from jax import lax

HEADS = 12
HEAD_DIM = 64
FF = 3072
D = 768
SLOT_LEN = 256
QRY_LEN = 32
SLOT_DEV = 3
QRY_DEV = 24
TOK_DEV = 1536
TOKENS = 12288
SLOTS = 24
QUERIES = 192
CANDS = 48
N_DP = 8


def shared_buckets(key):
    drawn = jax.random.randint(jax.random.fold_in(key, 17), (SLOTS,), 0, 2, dtype=jnp.int32)
    drawn = drawn.at[0].set(1)
    return drawn.at[SLOTS - 1].set(0).astype(jnp.int32)


def draw_bucket(key, part):
    return shared_buckets(key)


def draw_token_mask(key, part):
    buckets = shared_buckets(key)
    key = jax.random.fold_in(key, 2)
    key_long, key_short, key_query = jax.random.split(key, 3)
    half_len = SLOT_LEN // 2
    long_len = jax.random.randint(key_long, (SLOTS,), half_len + 1, SLOT_LEN + 1, dtype=jnp.int32)
    short_len = jax.random.randint(key_short, (SLOTS, 2), SLOT_LEN // 4, half_len + 1, dtype=jnp.int32)
    query_len = jax.random.randint(key_query, (QUERIES,), QRY_LEN // 4, QRY_LEN + 1, dtype=jnp.int32)
    slot_place = jnp.arange(half_len, dtype=jnp.int32)
    short_mask = slot_place[None, None, :] < short_len[:, :, None]
    long_mask = slot_place[None, None, :] + half_len * jnp.arange(2, dtype=jnp.int32)[None, :, None] < long_len[:, None, None]
    slot_mask = jnp.where(buckets[:, None, None] == 1, long_mask, short_mask).reshape(N_DP, SLOT_DEV * SLOT_LEN)
    query_mask = (jnp.arange(QRY_LEN, dtype=jnp.int32)[None, :] < query_len[:, None]).reshape(N_DP, QRY_DEV * QRY_LEN)
    return jnp.concatenate([slot_mask, query_mask], axis=1).reshape(TOKENS).astype(jnp.int32)


def draw_positive(key, part):
    buckets = shared_buckets(key)
    key = jax.random.fold_in(key, 3)
    key_slot, key_half, key_order = jax.random.split(key, 3)
    slot_pick = jax.random.randint(key_slot, (QUERIES,), 0, SLOTS, dtype=jnp.int32)
    half_pick = jax.random.randint(key_half, (QUERIES,), 0, 2, dtype=jnp.int32)
    picks = (2 * slot_pick + half_pick * (1 - buckets[slot_pick])).astype(jnp.int32)
    order = jax.random.permutation(key_order, QUERIES)
    picks = picks.at[order[0]].set(0)
    picks = picks.at[order[1]].set(CANDS - 1)
    return picks.astype(jnp.int32)


def block_scale(key, extent, shards, smallest, high):
    def one(dim, shards_of):
        steps = jax.random.uniform(jax.random.fold_in(jax.random.fold_in(key, 6), dim), (shards_of,), jnp.float32, smallest / len(shards), high / len(shards))
        return jnp.repeat(jnp.exp(steps), extent[dim] // shards_of).reshape((-1,) + (1,) * (len(extent) - dim - 1))

    loudness = one(*shards[0])
    for cut in shards[1:]:
        loudness = loudness * one(*cut)
    return loudness


def bell_draw(stream_key, extent, width, most, shards=(), kind=jnp.bfloat16):
    values = width * jax.random.normal(stream_key, extent, jnp.float32)
    if shards:
        values = values * block_scale(stream_key, extent, shards, -0.22, 0.18)
    return jnp.clip(values, -most, most).astype(kind)


def setup_inputs(seed: int = 0) -> dict:
    key_of = jax.random.split(jax.random.key(seed), 18)
    hidden_in = bell_draw(key_of[0], (TOKENS, D), 1.0, 6.0, ((0, 8),))
    token_mask = draw_token_mask(jax.random.fold_in(key_of[17], 71), 0)
    bucket = draw_bucket(jax.random.fold_in(key_of[17], 71), 0)
    positive = draw_positive(jax.random.fold_in(key_of[17], 71), 0)
    qkv_weight = bell_draw(key_of[4], (3, D, D), D ** -0.5, 0.21875, ((2, 4),))
    qv_bias = bell_draw(key_of[5], (2, D), 0.5, 3.0, ((1, 4),))
    out_weight = bell_draw(key_of[6], (D, D), (D // 32) ** -0.5, 1.25, ((0, 4),))
    out_bias = bell_draw(key_of[7], (D,), 0.5, 3.0)
    norm1_gain = jnp.clip(1.0 + 0.15 * jax.random.normal(key_of[8], (D,), jnp.float32), 0.25, 1.75).astype(jnp.bfloat16)
    norm1_bias = bell_draw(key_of[9], (D,), 0.3, 2.0)
    ffn_in = bell_draw(key_of[10], (D, FF), D ** -0.5, 0.21875, ((1, 4),))
    ffn_in_bias = bell_draw(key_of[11], (FF,), 0.5, 3.0, ((0, 4),))
    ffn_out = bell_draw(key_of[12], (FF, D), (FF // 2) ** -0.5, 0.15625, ((0, 4),))
    ffn_out_bias = bell_draw(key_of[13], (D,), 0.5, 3.0)
    norm2_gain = jnp.clip(1.0 + 0.15 * jax.random.normal(key_of[14], (D,), jnp.float32), 0.25, 1.75).astype(jnp.bfloat16)
    norm2_bias = bell_draw(key_of[15], (D,), 0.3, 2.0)
    upstream = bell_draw(key_of[16], (TOKENS, D), 1.0, 6.0, ((0, 8),))
    return {"hidden_in": hidden_in, "token_mask": token_mask, "bucket": bucket, "positive": positive, "qkv_weight": qkv_weight, "qv_bias": qv_bias, "out_weight": out_weight, "out_bias": out_bias, "norm1_gain": norm1_gain, "norm1_bias": norm1_bias, "ffn_in": ffn_in, "ffn_in_bias": ffn_in_bias, "ffn_out": ffn_out, "ffn_out_bias": ffn_out_bias, "norm2_gain": norm2_gain, "norm2_bias": norm2_bias, "upstream": upstream}


PRECISE = lax.Precision.HIGHEST
NORM_EPS = 1e-12

@jax.custom_vjp
def low(v):
    return lax.optimization_barrier(v.astype(jnp.bfloat16)).astype(jnp.float32)

@jax.custom_vjp
def low_back(v):
    return v

def low_keep(v):
    return (low(v), None)

def low_pass(kept, grad):
    return (grad,)

def back_keep(v):
    return (v, None)

def back_low(kept, grad):
    return (low(grad),)
low.defvjp(low_keep, low_pass)
low_back.defvjp(back_keep, back_low)

def layer_norm(values, gain_row, bias_row):
    centre = values - lax.optimization_barrier(jnp.mean(values, axis=-1, keepdims=True))
    spread = lax.optimization_barrier(jnp.mean(centre * centre, axis=-1, keepdims=True))
    return centre * lax.rsqrt(spread + NORM_EPS) * gain_row + bias_row

def segment_ids(bucket):
    row_index = jnp.arange(TOKENS, dtype=jnp.int32)
    device_of = row_index // TOK_DEV
    within = row_index % TOK_DEV
    slot_of = within // SLOT_LEN
    slot_place = within % SLOT_LEN
    slot_rows = SLOT_DEV * SLOT_LEN
    global_slot = jnp.minimum(device_of * SLOT_DEV + slot_of, SLOTS - 1).astype(jnp.int32)
    slot_kind = bucket[global_slot]
    in_slot = 2 * slot_of + jnp.where(slot_place >= SLOT_LEN // 2, 1 - slot_kind, 0)
    in_query = 2 * SLOT_DEV + (within - slot_rows) // QRY_LEN
    local_ids = jnp.where(within < slot_rows, in_slot, in_query)
    return device_of * (2 * SLOT_DEV + QRY_DEV) + local_ids

def split_heads(values):
    block_rows = 2 * SLOT_LEN
    return values.reshape(TOKENS // block_rows, block_rows, HEADS, HEAD_DIM)

def attention(queries, keys_in, values_in, segment, keep):
    block_rows = 2 * SLOT_LEN
    head_scale = 1.0 / math.sqrt(HEAD_DIM)

    def one_block(pieces):
        query_blk, key_blk, value_blk, seg_blk, keep_blk = pieces
        scores = low_back(jnp.einsum('qhd,khd->hqk', query_blk, key_blk, precision=PRECISE) * head_scale)
        allowed = (seg_blk[:, None] == seg_blk[None, :]) & (keep_blk[None, :] == 1)
        scores = jnp.where(allowed[None], scores, -1e+30)
        probs = jax.nn.softmax(scores, axis=-1)
        return jnp.einsum('hqk,khd->qhd', low(probs), value_blk, precision=PRECISE)
    context = lax.map(jax.checkpoint(one_block), (split_heads(queries), split_heads(keys_in), split_heads(values_in), segment.reshape(-1, block_rows), keep.reshape(-1, block_rows)))
    return context.reshape(TOKENS, D)

def reference(hidden_in, token_mask, bucket, positive, qkv_weight, qv_bias, out_weight, out_bias, norm1_gain, norm1_bias, ffn_in, ffn_in_bias, ffn_out, ffn_out_bias, norm2_gain, norm2_bias, upstream):
    segment = segment_ids(bucket)
    cand_valid = jnp.stack([bucket >= 0, bucket == 0], axis=1).reshape(CANDS)
    device_ids = jnp.arange(N_DP, dtype=jnp.int32)[:, None]
    passage_rows = (device_ids * TOK_DEV + (jnp.arange(2 * SLOT_DEV, dtype=jnp.int32) * (SLOT_LEN // 2))[None]).reshape(-1)
    query_rows = (device_ids * TOK_DEV + SLOT_DEV * SLOT_LEN + (jnp.arange(QRY_DEV, dtype=jnp.int32) * QRY_LEN)[None]).reshape(-1)
    loss_scale = 2.0 / math.sqrt(D)

    def forward(x_in, w_qkv, b_qv, w_attn, b_attn, gain_one, bias_one, w_first, b_first, w_second, b_second, gain_two, bias_two):
        projected = jnp.einsum('rd,kde->kre', x_in, w_qkv, precision=PRECISE)
        queries = low_back(low(projected[0] + b_qv[0]))
        keys_in = low_back(low(projected[1]))
        values_in = low_back(low(projected[2] + b_qv[1]))
        context = low_back(low(attention(queries, keys_in, values_in, segment, token_mask)))
        attended = low_back(jnp.dot(context, w_attn, precision=PRECISE) + b_attn)
        first_norm = layer_norm(x_in + attended, gain_one, bias_one)
        inner = low_back(jnp.dot(low(first_norm), w_first, precision=PRECISE) + b_first)
        branch = low_back(jnp.dot(low(jax.nn.gelu(inner, approximate=False)), w_second, precision=PRECISE) + b_second)
        out_value = layer_norm(first_norm + branch, gain_two, bias_two)
        query_vecs = low(out_value[query_rows])
        passage_vecs = low(out_value[passage_rows])
        logits = low_back(jnp.dot(query_vecs, passage_vecs.T, precision=PRECISE) * loss_scale)
        logits = jnp.where(cand_valid[None], logits, -1e+30)
        log_total = jax.nn.logsumexp(logits, axis=1)
        picked = jnp.take_along_axis(logits, positive[:, None], axis=1)[:, 0]
        return ((out_value, jnp.sum(log_total - picked)), (query_vecs, passage_vecs))
    f32 = jnp.float32
    (out_value, ce_total), back_fn, (query_vecs, passage_vecs) = jax.vjp(forward, hidden_in.astype(f32), qkv_weight.astype(f32), qv_bias.astype(f32), out_weight.astype(f32), out_bias.astype(f32), norm1_gain.astype(f32), norm1_bias.astype(f32), ffn_in.astype(f32), ffn_in_bias.astype(f32), ffn_out.astype(f32), ffn_out_bias.astype(f32), norm2_gain.astype(f32), norm2_bias.astype(f32), has_aux=True)
    grads = back_fn((upstream.astype(f32), jnp.ones((), f32)))
    return (out_value.astype(jnp.bfloat16), query_vecs.astype(jnp.bfloat16), passage_vecs.astype(jnp.bfloat16), ce_total / QUERIES, grads[0], grads[1], grads[2], grads[3], grads[4], grads[5], grads[6], grads[7], grads[8], grads[9], grads[10], grads[11], grads[12])
```

```python
import math
from types import SimpleNamespace

import jax
import jax.numpy as jnp
from jax import lax
from jax.experimental import pallas as pl
from jax.experimental.pallas import tpu as pltpu
from jax.sharding import PartitionSpec as P

f32 = jnp.float32
bf16 = jnp.bfloat16
MESH = pl.DeviceIdType.MESH

HEAD_DIM = 64
SLOT_LEN = 256
QRY_LEN = 32
NORM_EPS = 1e-12
BLK = 256
PIECE = 64
RING = 8
DEAD = -1e30


def dot(a, b):
    return lax.dot_general(a, b, (((1,), (0,)), ((), ())), preferred_element_type=f32)


def dot_t(a, b):
    return lax.dot_general(a, b, (((1,), (1,)), ((), ())), preferred_element_type=f32)


def dot_l(a, b):
    return lax.dot_general(a, b, (((0,), (0,)), ((), ())), preferred_element_type=f32)


def loop(n, body, lo=0):
    def step(i, carry):
        body(i)
        return carry

    lax.fori_loop(lo, n, step, 0)


def layer_kernel(n_dp, dims, names, *refs):
    R = SimpleNamespace(**dict(zip(names, refs)))
    rows, width, slots, queries, local_width = dims
    blocks = rows // BLK
    heads = local_width // HEAD_DIM
    groups = n_dp // RING
    cands = 8 * n_dp
    loss_scale = 2.0 / math.sqrt(width)
    quarter = width
    own = blocks * PIECE
    part_rows = own // 2

    dp = lax.axis_index("dp")
    t = lax.axis_index("tensor")
    y = lax.div(t, 2)
    c = lax.rem(t, 2)
    t1 = 2 * y + (1 - c)
    t2 = 2 * (1 - y) + c
    t3 = 2 * (1 - y) + (1 - c)
    core = (dp, t1)
    ypeer = (dp, t2)
    mates = ((dp, t1), (dp, t2), (dp, t3))

    group = lax.div(dp, RING)
    place = lax.rem(dp, RING)

    def place_of(r):
        return jnp.where(r < 4, 2 * r, 2 * (7 - r) + 1)

    r = jnp.where(lax.rem(place, 2) == 0, lax.div(place, 2), 7 - lax.div(place, 2))
    ring_to = (
        (group * RING + place_of(lax.rem(r + 1, RING)), t),
        (group * RING + place_of(lax.rem(r + RING - 1, RING)), t),
    )

    def dp_at(k):
        return lax.rem(dp + k, n_dp)

    (S_SHARE, S_WCORE, S_WRING, S_WON, S_BIAS, S_CORE0, S_Y0, S_CORE1, S_Y1, S_X1, S_FIRST, S_DF, S_DA, S_OUT, S_MAIL,
     S_BACK, S_VEC, S_TSUM, S_RING, S_GATHER, S_LOCAL, S_GLOCAL, S_GCORE, S_OUTL) = range(24)

    def cp(src, dst, kind, rsem, dev):
        return pltpu.make_async_remote_copy(
            src_ref=src, dst_ref=dst, send_sem=R.ss.at[kind], recv_sem=rsem, device_id=dev, device_id_type=MESH
        )

    def arrived(ref, rsem):
        cp(ref, ref, S_SHARE, rsem, core).wait_recv()

    def sent(ref, kind):
        cp(ref, ref, kind, R.wc_r.at[0], core).wait_send()

    loads = [
        pltpu.make_async_copy(R.wqkv_in, R.wqkv, R.load_sem.at[0]),
        pltpu.make_async_copy(R.hid_in, R.hid, R.load_sem.at[1]),
        pltpu.make_async_copy(R.wo_in, R.wo, R.load_sem.at[2]),
        pltpu.make_async_copy(R.w1, R.wf1.at[t], R.load_sem.at[3]),
        pltpu.make_async_copy(R.w2, R.wf2.at[t], R.load_sem.at[4]),
        pltpu.make_async_copy(R.upstream.at[:, t], R.up, R.load_sem.at[5]),
    ]
    for one in loads:
        one.start()

    barrier = pltpu.get_barrier_semaphore()
    for mate in mates:
        pl.semaphore_signal(barrier, inc=1, device_id=mate, device_id_type=MESH)

    def greet(k):
        pl.semaphore_signal(barrier, inc=1, device_id=(dp_at(k), t), device_id_type=MESH)

    loop(n_dp, greet, 1)
    pl.semaphore_wait(barrier, 3 + n_dp - 1)

    share = quarter // RING
    half = share // 2
    wfs = (R.wf1, R.wf2)
    wins = (R.w1, R.w2)
    rb = R.rb

    def unit(chunk, sub):
        return pl.ds(pl.multiple_of(chunk * share + sub * half, half), half)

    def from_here(d, s):
        return lax.rem(r - s + 2 * RING, RING) if d == 0 else lax.rem(r + s + 2 * RING, RING)

    def w_share(k):
        at = pl.ds(pl.multiple_of(r * share, share), share)
        return cp(wins[k].at[at], wfs[k].at[t, at], S_SHARE, R.wy_r.at[k], ypeer)

    def w_send(k, at, d, idx):
        ref = wfs[k].at[t2, at]
        cp(ref, ref, S_WRING, R.wr_r.at[idx], ring_to[d]).start()

    def w_on(k, at):
        ref = wfs[k].at[t2, at]
        cp(ref, ref, S_WON, R.wf_r.at[0], core).start()

    def w_start():
        for k in range(2):
            at = pl.ds(pl.multiple_of(r * share, share), share)
            arrived(wfs[k].at[t2, at], R.wy_r.at[k])
            for d in range(2):
                w_send(k, unit(r, d), d, 0)
                w_send(k, unit(r, 1 - d), d, 4)
            w_on(k, at)

    def w_lead(s):
        arrived(rb.at[0:2, :, 0], R.wr_r.at[s - 1])
        for k in range(2):
            for d in range(2):
                at = unit(from_here(d, s), d)
                if s < 4:
                    w_send(k, at, d, s)
                w_on(k, at)

    def w_trail(s):
        arrived(rb.at[0:2, :, 0], R.wr_r.at[3 + s])
        for k in range(2):
            for d in range(2):
                at = unit(from_here(d, s), 1 - d)
                if s < 3:
                    w_send(k, at, d, 4 + s)
                w_on(k, at)

    for k in range(2):
        w_share(k).start()
    for k in range(2):
        cp(wins[k], wfs[k].at[t], S_WCORE, R.wc_r.at[0], core).start()
    R.bias1[t] = jnp.broadcast_to(R.b1[...].astype(f32).reshape(1, quarter), (8, quarter))
    for mate in mates:
        cp(R.bias1.at[t], R.bias1.at[t], S_BIAS, R.bi_r.at[0], mate).start()

    part = R.part
    keep, send1, got1, send2, got2 = R.keep, R.send1, R.got1, R.send2, R.got2

    def rs0(e, i):
        for yy in range(2):
            mine = pl.ds(pl.multiple_of((2 * yy + c) * PIECE, PIECE), PIECE)
            other = pl.ds(pl.multiple_of((2 * yy + 1 - c) * PIECE, PIECE), PIECE)
            keep[i, yy] = part[mine].astype(bf16)
            send1[i, yy] = part[other].astype(bf16)
        cp(send1.at[i], got1.at[i], (S_CORE0, S_CORE1)[e], R.rc_r.at[e, i], core).start()

    def rs1(i):
        arrived(got1.at[i], R.rc_r.at[0, i])
        send2[i, 0] = (keep[i, 1 - y].astype(f32) + got1[i, 1 - y].astype(f32)).astype(bf16)
        cp(send2.at[i, 0], got2.at[i, 0], S_Y0, R.ry_r.at[0, i], ypeer).start()

    def rs2(i):
        arrived(got2.at[i, 0], R.ry_r.at[0, i])
        return keep[i, y].astype(f32) + got1[i, y].astype(f32) + got2[i, 0].astype(f32)

    def ag0(mine, kind, ysem, csem):
        cp(mine, mine, kind, ysem, ypeer).start()
        cp(mine, mine, kind, csem, core).start()

    def ag1(theirs, kind, ysem, csem):
        arrived(theirs, ysem)
        cp(theirs, theirs, kind, csem, core).start()

    def ag2(first, second, csem):
        arrived(first, csem)

    hid, wqkv, wo = R.hid, R.wqkv, R.wo
    lane = lax.broadcasted_iota(jnp.int32, (1, local_width), 1)
    head_f = [jnp.where(lax.shift_right_logical(lane, 6) == h, 1.0, 0.0).astype(f32) for h in range(heads)]
    head_b = [m.astype(bf16) for m in head_f]
    q_bias = R.qv_bias[0:1].astype(f32)
    v_bias = R.qv_bias[1:2].astype(f32)
    head_scale = 1.0 / math.sqrt(HEAD_DIM)

    def allowed_of(i):
        row = lax.broadcasted_iota(jnp.int32, (BLK, 1), 0)
        col = lax.broadcasted_iota(jnp.int32, (1, BLK), 1)
        split = 1 - R.bucket[jnp.minimum(i, slots - 1)]
        is_query = jnp.where(i >= slots, 1, 0)

        def seg(at):
            in_query = lax.shift_right_logical(at, 5)
            in_slot = lax.shift_right_logical(at, 7) * split
            return in_query * is_query + in_slot * (1 - is_query)

        return (seg(row) == seg(col)) & (R.mask[blk(i)].reshape(1, BLK) == 1)

    def blk(i):
        return pl.ds(pl.multiple_of(i * BLK, BLK), BLK)

    def attend(i):
        h_in = hid[blk(i)]
        q = (dot_t(h_in, wqkv[0]) + q_bias).astype(bf16)
        k = dot_t(h_in, wqkv[1]).astype(bf16)
        v = (dot_t(h_in, wqkv[2]) + v_bias).astype(bf16)
        R.q[blk(i)] = q
        R.k[blk(i)] = k
        R.v[blk(i)] = v
        allowed = allowed_of(i)
        context = jnp.zeros((BLK, local_width), f32)
        for h in range(heads):
            s = jnp.where(allowed, dot_t(q * head_b[h], k) * head_scale, DEAD)
            e = jnp.exp(s - jnp.max(s, axis=-1, keepdims=True))
            p = (e / jnp.sum(e, axis=-1, keepdims=True)).astype(bf16)
            R.pb[i, h] = p
            context = context + dot(p, v) * head_f[h]
        low = context.astype(bf16)
        R.ctx[blk(i)] = low
        part[...] = dot(low, wo[...])

    def norm_fwd(v, gain, bias):
        centre = v - jnp.mean(v, axis=-1, keepdims=True)
        rstd = lax.rsqrt(jnp.mean(centre * centre, axis=-1, keepdims=True) + NORM_EPS)
        n = centre * rstd
        return n, rstd, n * gain + bias

    def norm_bwd(dy, n, rstd, gain):
        e = dy * gain
        return (e - jnp.mean(e, axis=-1, keepdims=True) - n * jnp.mean(e * n, axis=-1, keepdims=True)) * rstd

    def vec_of(ref):
        return ref[...].astype(f32).reshape(1, width)

    vec = SimpleNamespace(
        ob=vec_of(R.ob), g1=vec_of(R.g1), n1b=vec_of(R.n1b), fb=vec_of(R.fb), g2=vec_of(R.g2), n2b=vec_of(R.n2b)
    )
    x1 = R.x1
    h1, n1, n2 = R.h1, R.n1, R.n2
    rstd1, rstd2 = R.rstd1, R.rstd2

    def own_rows(i):
        return pl.ds(pl.multiple_of(i * BLK + t * PIECE, PIECE), PIECE)

    def part_at(b, i):
        return pl.ds(pl.multiple_of(b * part_rows + i * 32, 32), 32)

    def first_norm(i):
        v = hid[own_rows(i)].astype(f32) + rs2(i) + vec.ob
        n, rstd, out = norm_fwd(v, vec.g1, vec.n1b)
        wide_rstd = jnp.broadcast_to(rstd, (PIECE, 128)).reshape(2, 2, 16, 128)
        n = n.reshape(2, 2, 16, width)
        low = out.astype(bf16)
        out = out.reshape(2, 2, 16, width)
        low4 = low.reshape(2, 2, 16, width)
        for b in range(2):
            n1[part_at(b, i)] = n[:, b].reshape(32, width)
            rstd1[part_at(b, i)] = wide_rstd[:, b].reshape(32, 128)
            h1[part_at(b, i)] = out[:, b].reshape(32, width)
            R.x1_own[part_at(b, i)] = low4[:, b].reshape(32, width)
        x1[i, t] = low
        ag0(x1.at[i, t], S_X1, R.gy_r.at[i], R.gc_r.at[i])

    def at_step(s, jobs):
        for i, job in jobs.items():
            pl.when(s == i)(job)

    def fwd_step(s):
        attend(s)
        rs0(0, s)

        @pl.when(s >= 1)
        def _():
            rs1(s - 1)

        at_step(s, {3: w_start})

        @pl.when(s >= 3)
        def _():
            first_norm(s - 3)

    for one in loads[:3]:
        one.wait()
    loop(blocks, fwd_step)
    rs1(blocks - 1)
    w_lead(1)
    first_norm(blocks - 3)
    w_trail(1)
    first_norm(blocks - 2)
    first_norm(blocks - 1)
    w_lead(2)

    for one in loads[3:]:
        one.wait()
    arrived(R.bias1.at[0:3], R.bi_r.at[0])
    arrived(R.wf1.at[0:2], R.wc_r.at[0])
    act, slope = R.act, R.slope

    def gelu(u):
        cdf = 0.5 * (1.0 + lax.erf(u * (1.0 / math.sqrt(2.0))))
        pdf = jnp.exp(-0.5 * u * u) * (1.0 / math.sqrt(2.0 * math.pi))
        return (u * cdf).astype(bf16), (cdf + u * pdf).astype(bf16)

    wide = R.wide
    wide[...] = jnp.zeros((own, width), f32)

    def own_fwd(j):
        q = jnp.where(j == 0, t, jnp.where(j == 1, t1, jnp.where(j == 2, t2, t3)))
        u = dot(R.x1_own[...], wfs[0][q]) + R.bias1[q, 0:1]
        a, sl = gelu(u)
        R.slope_own[q] = sl
        wide[...] += dot(a, wfs[1][q])

    def quarter_fwd(i):
        ag1(x1.at[i, t2], S_X1, R.gy_r.at[i], R.gc_r.at[i])
        arrived(x1.at[i, 0:2], R.gc_r.at[i])
        u = dot(x1[i].reshape(BLK, width), wfs[0][t]) + R.bias1[t, 0:1]
        a, sl = gelu(u)
        act[i] = a.reshape(4, 2, 2, 16, width)
        slope[i] = sl.reshape(4, 2, 2, 16, width)

    def middle(s):
        @pl.when(s < 2)
        def _():
            own_fwd(s)

        @pl.when((s >= 2) & (s < blocks + 2))
        def _():
            quarter_fwd(s - 2)

        at_step(s, {0: lambda: w_trail(2), 1: lambda: w_lead(3), 3: lambda: w_trail(3), 5: lambda: w_lead(4)})

        @pl.when(s >= blocks + 2)
        def _():
            @pl.when(s == blocks + 3)
            def _():
                arrived(R.wf1.at[0:2], R.wf_r.at[0])

            own_fwd(s - blocks)

    loop(blocks + 4, middle)

    low_out = R.low

    def second_norm(j):
        at = pl.ds(pl.multiple_of(j * PIECE, PIECE), PIECE)
        n, rstd, out = norm_fwd(h1[at] + wide[at] + vec.fb, vec.g2, vec.n2b)
        n2[at] = n
        rstd2[at] = jnp.broadcast_to(rstd, (PIECE, 128))
        h1[at] = out
        b = lax.div(j, blocks // 2)
        i = 2 * lax.rem(j, blocks // 2)
        low_out[pl.ds(i, 2), :, b] = out.astype(bf16).reshape(2, 2, 16, width)

    loop(blocks, second_norm)

    firsts = R.firsts
    stage = R.stage
    stage[...] = jnp.zeros((16, width), f32)
    for b in range(blocks - slots):
        for k in range(2):
            at = (slots + b) * 32 + 16 * k
            stage[2 * b + k : 2 * b + k + 1] = h1[at : at + 1]
    for s in range(slots):
        stage[6 + s : 7 + s] = h1[32 * s : 32 * s + 1]
    firsts[t] = stage[...].astype(bf16)
    for mate in mates:
        cp(firsts.at[t], firsts.at[t], S_FIRST, R.fi_r.at[0], mate).start()

    sums = R.sums
    sums[...] = jnp.zeros((16, width), f32)
    adds = R.adds
    up, dv2, df, da = R.up, R.n2, R.df, R.da
    dv1 = R.h1

    def colsum(v):
        return jnp.sum(v, axis=0, keepdims=True)

    def second_back(b):
        def one(i):
            at = part_at(b, i)
            dy = up[i, :, b].reshape(32, width).astype(f32)
            if b == 0:
                row = lax.broadcasted_iota(jnp.int32, (32, 1), 0)
                dy = dy + jnp.where(row == 0, adds[i, 0:1], 0.0) + jnp.where(row == 16, adds[i, 1:2], 0.0)
            n = n2[at]
            sums[0:1] += colsum(dy * n)
            sums[1:2] += colsum(dy)
            dv = norm_bwd(dy, n, rstd2[at][:, 0:1], vec.g2)
            dv2[at] = dv
            low = dv.astype(bf16)
            sums[2:3] += colsum(low.astype(f32))
            df[i, t, :, b] = low.reshape(2, 16, width)

        loop(blocks, one)
        ag0(df.at[:, t, :, b], S_DF, R.fy_r.at[b], R.fc_r.at[b])

    def own_bwd(b):
        at = pl.ds(b * part_rows, part_rows)
        wide[at] = dv2[at]

        def one(q):
            dg = dot_t(df[:, t, :, b].reshape(part_rows, width), wfs[1][q])
            du = (dg * R.slope_own[q, at].astype(f32)).astype(bf16)
            wide[at] += dot_t(du, wfs[0][q])

        loop(4, one)

        def first_back(i):
            at = part_at(b, i)
            dy = wide[at]
            n = n1[at]
            sums[3:4] += colsum(dy * n)
            sums[4:5] += colsum(dy)
            dv = norm_bwd(dy, n, rstd1[at][:, 0:1], vec.g1)
            dv1[at] = dv
            low = dv.astype(bf16)
            sums[5:6] += colsum(low.astype(f32))
            da[i, t, :, b] = low.reshape(2, 16, width)

        loop(blocks, first_back)
        ag0(da.at[:, t, :, b], S_DA, R.ay_r.at[b], R.ac_r.at[b])

    def df_on(b):
        ag1(df.at[:, t2, :, b], S_DF, R.fy_r.at[b], R.fc_r.at[b])

    def da_on(b):
        ag1(da.at[:, t2, :, b], S_DA, R.ay_r.at[b], R.ac_r.at[b])

    du_all = slope

    def quarter_bwd(b):
        arrived(df.at[:, 0:2, :, b], R.fc_r.at[b])

        def one(j):
            at = pl.ds(2 * j, 2)
            dg = dot_t(df[at, :, :, b].reshape(BLK, width), wfs[1][t])
            du = (dg * slope[at, :, :, b].reshape(BLK, width).astype(f32)).astype(bf16)
            sums[8:9] += colsum(du.astype(f32))
            du_all[at, :, :, b] = du.reshape(2, 4, 2, 16, width)

        loop(blocks // 2, one)

    second_back(1)

    arrived(firsts.at[0:3], R.fi_r.at[0])
    hw = width // 2
    pack = R.pack
    pack[...] = jnp.zeros((16, hw + 128), f32)
    cand_rows = [firsts[0].astype(f32), firsts[2].astype(f32)]
    for k in range(2):
        pack[3 * k : 3 * k + 3, 0:hw] = cand_rows[k][6:9, 0:hw]
        pack[8 + 3 * k : 11 + 3 * k, 0:hw] = cand_rows[k][6:9, hw:width]
    for s in range(slots):
        pack[3 + s : 4 + s, hw : hw + 128] = jnp.zeros((1, 128), f32) + R.bucket[s].astype(f32)
    pack[6:8, hw : hw + 128] = jnp.ones((2, 128), f32)
    mail = R.mail
    mail[dp] = pack[...].astype(bf16)
    loop(n_dp, lambda k: cp(mail.at[dp], mail.at[dp], S_MAIL, R.dp_r.at[0], (dp_at(k), t)).start(), 1)

    qe = R.qe
    qe[...] = jnp.zeros(qe.shape, f32)
    for tt in range(4):
        qe[8 * tt : 8 * tt + 6, 0:width] = firsts[tt].astype(f32)[0:6]
    lane_e = lax.broadcasted_iota(jnp.int32, (32, 128), 1)
    qe[:, width : width + 128] = jnp.where(lane_e == 0, DEAD, 0.0)
    row_q = lax.broadcasted_iota(jnp.int32, (32, 1), 0)
    target_at = jnp.full((32, 1), -1, jnp.int32)
    for tt in range(4):
        for b in range(blocks - slots):
            for k in range(2):
                pos = R.positive[b * 8 + tt * 2 + k]
                slot = lax.div(pos, 2)
                at = lax.div(slot, slots) * 8 + lax.rem(pos, 2) * 3 + lax.rem(slot, slots)
                target_at = jnp.where(row_q == 8 * tt + 2 * b + k, at, target_at)

    own_bwd(1)

    arrived(mail.at[1:], R.dp_r.at[0])
    pe = R.pe

    def unpack(n):
        got = mail[n].astype(f32)
        at = pl.ds(pl.multiple_of(n * 8, 8), 8)
        pe[at, 0:hw] = got[0:8, 0:hw]
        pe[at, hw:width] = got[8:16, 0:hw]
        pe[at, width : width + 128] = got[0:8, hw : hw + 128]

    loop(n_dp, unpack)
    pe_low = pe[...].astype(bf16)
    qe_low = qe[...].astype(bf16)
    z = dot_t(qe_low, pe_low) * loss_scale
    peak = jnp.max(z, axis=1, keepdims=True)
    total = peak + jnp.log(jnp.sum(jnp.exp(z - peak), axis=1, keepdims=True))
    target = lax.broadcasted_iota(jnp.int32, (32, cands), 1) == target_at
    live = target_at >= 0
    picked = jnp.sum(jnp.where(target, z, 0.0), axis=1, keepdims=True)
    ce = jnp.where(live, total - picked, 0.0)
    loss = jnp.sum(ce, axis=0, keepdims=True)
    dz = jnp.where(live, jnp.exp(z - total) - jnp.where(target, 1.0, 0.0), 0.0).astype(bf16)
    dqe = R.dqe
    dqe[...] = dot(dz, pe_low[:, 0:width]) * loss_scale
    dpe = R.dpe
    dpe[...] = (dot_l(dz, qe_low[:, 0:width]) * loss_scale).reshape(n_dp, 8, width)
    back = R.back

    @pl.when(c == 0)
    def _():
        loop(n_dp, lambda k: cp(dpe.at[dp_at(k)], back.at[dp], S_BACK, R.dp_r.at[1], (dp_at(k), t)).start(), 1)

    back[dp] = dpe[dp]

    df_on(1)
    da_on(1)
    quarter_bwd(1)

    @pl.when(c == 0)
    def _():
        arrived(back.at[1:], R.dp_r.at[1])
        stage[0:8] = back[0]

        def add(n):
            stage[0:8] += back[n]

        loop(n_dp, add, 1)

    mine_q = dqe[pl.ds(pl.multiple_of(t * 8, 8), 8)]
    is_c0 = jnp.where(c == 0, 1.0, 0.0).astype(f32)
    adds[...] = jnp.zeros(adds.shape, f32)
    for s in range(slots):
        adds[s, 0:1] = jnp.where(y == 0, stage[s : s + 1], stage[3 + s : 4 + s]) * is_c0
    for b in range(blocks - slots):
        adds[slots + b, 0:2] = mine_q[2 * b : 2 * b + 2]
    second_back(0)
    own_bwd(0)

    out = R.layer_out
    out_own = pltpu.make_async_copy(low_out, out.at[:, t], R.ss.at[S_OUTL])
    out_own.start()
    cp(low_out, out.at[:, t], S_OUT, R.lo_r.at[0], ypeer).start()
    cp(low_out, out.at[:, t], S_OUT, R.lo_r.at[1], core).start()

    sums[6:7] = jnp.where(t == 0, loss, 0.0) + jnp.zeros((1, width), f32)
    tsum = R.tsum
    tsum[t] = sums[0:8]
    for mate in mates:
        cp(tsum.at[t], tsum.at[t], S_TSUM, R.ts_r.at[0], mate).start()
    df_on(0)
    quarter_bwd(0)

    grads = (R.ga1, R.ga2, R.ga3)
    outs = (R.o1, R.o2, R.o3)

    def to_owner(d, s):
        return from_here(1 - d, 4 - s)

    def ring_send(k, d, src, idx):
        cp(src, rb.at[k, d, idx], S_RING, R.rr_r.at[k, idx], ring_to[d]).start()

    def ring_start(k):
        for d in range(2):
            ring_send(k, d, grads[k].at[unit(to_owner(d, 0), d)], 0)
            ring_send(k, d, grads[k].at[unit(to_owner(d, 1), 1 - d)], 4)

    def ring_add(k, s, lead):
        idx = s - 1 if lead else s + 2
        arrived(rb.at[k, :, idx], R.rr_r.at[k, idx])
        for d in range(2):
            slot = rb.at[k, d, idx]
            mine = grads[k][unit(to_owner(d, s), d if lead else 1 - d)]
            slot[...] = (slot[...].astype(f32) + mine.astype(f32)).astype(bf16)
            ring_send(k, d, slot, idx + 1)

    def gather_send(k, d, src, at, idx):
        cp(src, outs[k].at[at], S_GATHER, R.rg_r.at[k, idx], ring_to[d]).start()

    def ring_turn(k):
        for idx in (3, 6):
            arrived(rb.at[k, :, idx], R.rr_r.at[k, idx])
        for a in range(2):
            mine = grads[k][unit(r, a)].astype(f32)
            rb[k, a, 3] = (rb[k, a, 3].astype(f32) + rb[k, 1 - a, 6].astype(f32) + mine).astype(bf16)
        if groups > 1:

            def swap(a, g):
                at = (k * 2 + a) * (groups - 1) + g - 1
                dev = (lax.rem(group + g, groups) * RING + place, t)
                return pltpu.make_async_remote_copy(
                    src_ref=rb.at[k, a, 3], dst_ref=R.gb.at[at], send_sem=R.gr_s.at[at], recv_sem=R.gr_r.at[at],
                    device_id=dev, device_id_type=MESH,
                )

            both = [(a, g) for a in range(2) for g in range(1, groups)]
            for a, g in both:
                swap(a, g).start()
            for a, g in both:
                swap(a, g).wait()
            for a in range(2):
                tot = rb[k, a, 3].astype(f32)
                for g in range(1, groups):
                    tot = tot + R.gb[(k * 2 + a) * (groups - 1) + g - 1].astype(f32)
                rb[k, a, 3] = tot.astype(bf16)
        for d in range(2):
            gather_send(k, d, rb.at[k, d, 3], unit(r, d), 0)
            gather_send(k, d, rb.at[k, 1 - d, 3], unit(r, 1 - d), 4)
        for a in range(2):
            pltpu.make_async_copy(rb.at[k, a, 3], outs[k].at[unit(r, a)], R.ss.at[S_LOCAL]).start()

    def gather_on(k, s, lead):
        idx = s - 1 if lead else s + 3
        arrived(rb.at[k, :, 0], R.rg_r.at[k, idx])
        if s < (4 if lead else 3):
            for d in range(2):
                at = unit(from_here(d, s), d if lead else 1 - d)
                gather_send(k, d, outs[k].at[at], at, idx + 1)

    def ring_jobs(k):
        return [
            lambda: ring_add(k, 1, True), lambda: ring_add(k, 2, False), lambda: ring_add(k, 2, True),
            lambda: ring_add(k, 3, False), lambda: ring_add(k, 3, True), lambda: ring_turn(k),
            lambda: gather_on(k, 1, True), lambda: gather_on(k, 1, False), lambda: gather_on(k, 2, True),
            lambda: gather_on(k, 2, False), lambda: gather_on(k, 3, True), lambda: gather_on(k, 3, False),
            lambda: gather_on(k, 4, True),
        ]

    tile = BLK

    def grad2(j):
        at = pl.ds(pl.multiple_of(j * tile, tile), tile)
        grads[1][at] = dot_l(act[..., at].reshape(rows, tile), df[...].reshape(rows, width)).astype(bf16)

    loop(quarter // tile, grad2)
    ring_start(1)
    da_on(0)

    def grad1(j):
        at = pl.ds(pl.multiple_of(j * tile, tile), tile)
        grads[0][:, at] = dot_l(x1[...].reshape(rows, width), du_all[..., at].reshape(rows, tile)).astype(bf16)

    loop(quarter // tile, grad1)
    ring_start(0)

    dq_all, dk_all, dv_all = R.q, R.k, R.v

    def attend_back(i):
        da_i = da[i].reshape(BLK, width)
        dc = dot_t(da_i, wo[...]).astype(bf16)
        q = R.q[blk(i)]
        k = R.k[blk(i)]
        v = R.v[blk(i)]
        dq = jnp.zeros((BLK, local_width), f32)
        dk = jnp.zeros((BLK, local_width), f32)
        dv = jnp.zeros((BLK, local_width), f32)
        for h in range(heads):
            dch = dc * head_b[h]
            p = R.pb[i, h]
            pf = p.astype(f32)
            dp_h = dot_t(dch, v)
            ds = (pf * (dp_h - jnp.sum(pf * dp_h, axis=-1, keepdims=True))).astype(bf16)
            dq = dq + dot(ds, k) * head_f[h]
            dk = dk + dot_l(ds, q * head_b[h])
            dv = dv + dot_l(p, dch)
        dq = (dq * head_scale).astype(bf16)
        dk = (dk * head_scale).astype(bf16)
        dv = dv.astype(bf16)
        dq_all[blk(i)] = dq
        dk_all[blk(i)] = dk
        dv_all[blk(i)] = dv
        sums[9:10, 0:local_width] += colsum(dq.astype(f32))
        sums[10:11, 0:local_width] += colsum(dv.astype(f32))
        part[...] = dot(dq, wqkv[0]) + dot(dk, wqkv[1]) + dot(dv, wqkv[2])

    gin = R.grad_in

    def gin1(i):
        arrived(got1.at[i], R.rc_r.at[1, i])
        mine = [dv1[part_at(b, i)].reshape(2, 16, width) for b in range(2)]
        mine = jnp.stack(mine, axis=1).reshape(PIECE, width)
        for yy in range(2):
            has = jnp.where(y == yy, 1.0, 0.0).astype(f32)
            send2[i, yy] = (keep[i, yy].astype(f32) + got1[i, yy].astype(f32) + mine * has).astype(bf16)
        cp(send2.at[i], got2.at[i], S_Y1, R.ry_r.at[1, i], ypeer).start()

    def gin2(i):
        arrived(got2.at[i], R.ry_r.at[1, i])
        for yy in range(2):
            got2[i, yy] = (send2[i, yy].astype(f32) + got2[i, yy].astype(f32)).astype(bf16)
            dst = gin.at[i, 2 * yy + c]
            pltpu.make_async_copy(got2.at[i, yy], dst, R.ss.at[S_GLOCAL]).start()
            cp(got2.at[i, yy], dst, S_GCORE, R.go_r.at[0], core).start()

    sent(send1, S_CORE0)
    sent(send2.at[:, 0], S_Y0)
    for b in range(2):
        arrived(da.at[:, 0:2, :, b], R.ac_r.at[b])

    jobs1, jobs0, jobs2 = ring_jobs(1), ring_jobs(0), ring_jobs(2)
    n_early = blocks

    def back_step(s):
        attend_back(s)
        rs0(1, s)

        @pl.when(s >= 1)
        def _():
            gin1(s - 1)

        at_step(s, dict(enumerate(jobs1[:n_early])))
        at_step(s, dict(enumerate(jobs0[:n_early])))

        @pl.when(s >= 3)
        def _():
            gin2(s - 3)

    loop(blocks, back_step)

    grads[2][0:local_width] = dot_l(dq_all[...], hid[...]).astype(bf16)
    grads[2][local_width : 2 * local_width] = dot_l(dk_all[...], hid[...]).astype(bf16)
    grads[2][2 * local_width : 3 * local_width] = dot_l(dv_all[...], hid[...]).astype(bf16)
    grads[2][3 * local_width : 4 * local_width] = dot_l(R.ctx[...], da[...].reshape(rows, width)).astype(bf16)
    ring_start(2)

    arrived(tsum.at[0:3], R.ts_r.at[0])
    sums[0:8] = tsum[0] + tsum[1] + tsum[2] + tsum[3]
    loss_low = sums[6:7].astype(bf16).astype(f32)
    sums[7:8] = sums[6:7] - loss_low
    vmail = R.vmail
    vmail[dp] = sums[...].astype(bf16)
    loop(n_dp, lambda k: cp(vmail.at[dp], vmail.at[dp], S_VEC, R.dp_r.at[2], (dp_at(k), t)).start(), 1)

    extra = [lambda: gin1(blocks - 1)] + [lambda i=i: gin2(i) for i in range(blocks - 3, blocks)]
    late1, late0 = jobs1[n_early:], jobs0[n_early:]
    for i in range(max(len(jobs2), len(late1), len(extra))):
        for jobs in (late1, late0, jobs2, extra):
            if i < len(jobs):
                jobs[i]()

    arrived(vmail.at[1:], R.dp_r.at[2])
    sums[...] = vmail[0].astype(f32)

    def vec_add(n):
        sums[...] += vmail[n].astype(f32)

    loop(n_dp, vec_add, 1)
    R.vec_out[...] = sums[...]
    piece = x1.at[:, 0]
    arrived(piece, R.lo_r.at[0])
    cp(out.at[:, t2], out.at[:, t2], S_OUT, R.lo_r.at[1], core).start()
    arrived(x1.at[:, 0:2], R.lo_r.at[1])
    arrived(send1, R.go_r.at[0])

    out_own.wait()
    sent(x1.at[0, 0:3], S_SHARE)
    sent(R.wf1.at[0:2], S_WCORE)
    sent(rb.at[0:2], S_WRING)
    sent(R.wf1.at[0:2], S_WON)
    sent(R.bias1.at[0:3], S_BIAS)
    sent(send1, S_CORE1)
    sent(send2, S_Y1)
    for kind in (S_X1, S_DF, S_DA, S_OUT):
        sent(x1.at[:, 0:3], kind)
    sent(firsts.at[0:3], S_FIRST)
    sent(mail.at[1:], S_MAIL)
    sent(vmail.at[1:], S_VEC)
    sent(tsum.at[0:3], S_TSUM)

    @pl.when(c == 0)
    def _():
        sent(back.at[1:], S_BACK)

    sent(rb, S_RING)
    sent(rb, S_GATHER)
    sent(send1, S_GCORE)
    pltpu.make_async_copy(rb.at[0, 0, 0:6], rb.at[0, 0, 0:6], R.ss.at[S_LOCAL]).wait()
    pltpu.make_async_copy(send1, send1, R.ss.at[S_GLOCAL]).wait()


def run_layer(n_dp, ins, dims):
    rows, width, slots, queries, local_width = dims
    blocks = rows // BLK
    heads = local_width // HEAD_DIM
    own = blocks * PIECE
    groups = n_dp // RING
    share = width // RING // 2
    dma = pltpu.SemaphoreType.DMA
    vm = pltpu.VMEM
    any_ = pl.BlockSpec(memory_space=pl.ANY)
    vmem = pl.BlockSpec(memory_space=pltpu.VMEM)
    smem = pl.BlockSpec(memory_space=pltpu.SMEM)
    ins_at = dict(
        hid_in=any_, mask=vmem, bucket=smem, positive=smem, wqkv_in=any_, qv_bias=vmem, wo_in=any_, ob=vmem, g1=vmem,
        n1b=vmem, w1=any_, b1=vmem, w2=any_, fb=vmem, g2=vmem, n2b=vmem, upstream=any_,
    )
    pieces = (blocks, 4, 2, 2, 16, width)
    pairs = (blocks, 2, PIECE, width)
    outs = dict(
        layer_out=(any_, pieces, bf16),
        grad_in=(any_, (blocks, 4, PIECE, width), bf16),
        o1=(any_, (width, width), bf16),
        o2=(any_, (width, width), bf16),
        o3=(any_, (width, width), bf16),
        vec_out=(vmem, (16, width), f32),
    )
    scratch = dict(
        hid=vm((rows, width), bf16),
        wqkv=vm((3, local_width, width), bf16),
        wo=vm((local_width, width), bf16),
        wf1=vm((4, width, width), bf16),
        wf2=vm((4, width, width), bf16),
        up=vm((blocks, 2, 2, 16, width), bf16),
        bias1=vm((4, 8, width), f32),
        part=vm((BLK, width), f32),
        keep=vm(pairs, bf16),
        send1=vm(pairs, bf16),
        got1=vm(pairs, bf16),
        send2=vm(pairs, bf16),
        got2=vm(pairs, bf16),
        q=vm((rows, local_width), bf16),
        k=vm((rows, local_width), bf16),
        v=vm((rows, local_width), bf16),
        ctx=vm((rows, local_width), bf16),
        pb=vm((blocks, heads, BLK, BLK), bf16),
        x1=vm((blocks, 4, PIECE, width), bf16),
        x1_own=vm((own, width), bf16),
        h1=vm((own, width), f32),
        n1=vm((own, width), f32),
        n2=vm((own, width), f32),
        rstd1=vm((own, 128), f32),
        rstd2=vm((own, 128), f32),
        act=vm(pieces, bf16),
        slope=vm(pieces, bf16),
        wide=vm((own, width), f32),
        slope_own=vm((4, own, width), bf16),
        low=vm((blocks, 2, 2, 16, width), bf16),
        firsts=vm((4, 16, width), bf16),
        stage=vm((16, width), f32),
        adds=vm((blocks, 8, width), f32),
        pack=vm((16, width // 2 + 128), f32),
        mail=vm((n_dp, 16, width // 2 + 128), bf16),
        qe=vm((32, width + 128), f32),
        pe=vm((n_dp * 8, width + 128), f32),
        dqe=vm((32, width), f32),
        dpe=vm((n_dp, 8, width), f32),
        back=vm((n_dp, 8, width), f32),
        sums=vm((16, width), f32),
        tsum=vm((4, 8, width), f32),
        vmail=vm((n_dp, 16, width), bf16),
        df=vm(pieces, bf16),
        da=vm(pieces, bf16),
        ga1=vm((width, width), bf16),
        ga2=vm((width, width), bf16),
        ga3=vm((width, width), bf16),
        rb=vm((3, 2, RING - 1, share, width), bf16),
        load_sem=dma((6,)),
        ss=dma((24,)),
        wc_r=dma((1,)), wy_r=dma((2,)), wf_r=dma((1,)), wr_r=dma((7,)), bi_r=dma((1,)),
        rc_r=dma((2, blocks)), ry_r=dma((2, blocks)),
        gy_r=dma((blocks,)), gc_r=dma((blocks,)),
        fy_r=dma((2,)), fc_r=dma((2,)), ay_r=dma((2,)), ac_r=dma((2,)),
        fi_r=dma((1,)), lo_r=dma((2,)), dp_r=dma((3,)), ts_r=dma((1,)),
        rr_r=dma((3, 7)), rg_r=dma((3, 7)), go_r=dma((1,)),
    )
    if groups > 1:
        n = 6 * (groups - 1)
        scratch.update(gb=vm((n, share, width), bf16), gr_s=dma((n,)), gr_r=dma((n,)))
    names = [*ins_at, *outs, *scratch]

    def kernel(*refs):
        layer_kernel(n_dp, dims, names, *refs)

    return pl.pallas_call(
        kernel,
        name="layer",
        out_shape=[jax.ShapeDtypeStruct(shape, kind) for _, shape, kind in outs.values()],
        in_specs=list(ins_at.values()),
        out_specs=[spec for spec, _, _ in outs.values()],
        scratch_shapes=list(scratch.values()),
        compiler_params=pltpu.CompilerParams(
            collective_id=0, has_side_effects=True, vmem_limit_bytes=64 * 2**20
        ),
    )(*[ins[n] for n in ins_at])


def local(
    hidden_in, token_mask, bucket, positive, qkv_weight, qv_bias, out_weight, out_bias, norm1_gain, norm1_bias,
    ffn_in, ffn_in_bias, ffn_out, ffn_out_bias, norm2_gain, norm2_bias, upstream,
):
    rows, width = hidden_in.shape
    blocks = rows // BLK
    slots = bucket.shape[0]
    queries = positive.shape[0]
    local_width = qkv_weight.shape[2]
    n_dp = lax.axis_size("dp")
    ins = dict(
        hid_in=hidden_in, mask=token_mask, bucket=bucket, positive=positive, wqkv_in=qkv_weight.transpose(0, 2, 1),
        qv_bias=qv_bias, wo_in=out_weight, ob=out_bias, g1=norm1_gain, n1b=norm1_bias, w1=ffn_in, b1=ffn_in_bias,
        w2=ffn_out, fb=ffn_out_bias, g2=norm2_gain, n2b=norm2_bias,
        upstream=upstream.reshape(blocks, 4, 2, 2, 16, width),
    )
    lout, gin, o1, o2, o3, sums = run_layer(n_dp, ins, (rows, width, slots, queries, local_width))
    lout = lout.reshape(rows, width)
    slot_rows = slots * SLOT_LEN
    passage = lout[:slot_rows].reshape(2 * slots, SLOT_LEN // 2, width)[:, 0]
    query = lout[slot_rows:].reshape(queries, QRY_LEN, width)[:, 0]
    qkv = o3[: 3 * local_width].reshape(3, local_width, width)
    loss = (sums[6, 0] + sums[7, 0]) / (queries * n_dp)
    return (
        lout, query, passage, loss, gin.reshape(rows, width).astype(f32),
        qkv.transpose(0, 2, 1).astype(f32), sums[9:11, :local_width], o3[3 * local_width :].astype(f32),
        sums[5], sums[3], sums[4], o1.astype(f32), sums[8], o2.astype(f32), sums[2], sums[0], sums[1],
    )


def solution(mesh):
    one, two = P("dp"), P("dp", None)
    col, row = P(None, "tensor"), P("tensor", None)
    return jax.shard_map(
        local,
        mesh=mesh,
        in_specs=(
            two, one, one, one, P(None, None, "tensor"), col, row, P(), P(), P(), col, P("tensor"), row, P(), P(), P(),
            two,
        ),
        out_specs=(
            two, two, two, P(), two, P(None, None, "tensor"), col, row, P(), P(), P(), col, P("tensor"), row, P(), P(),
            P(),
        ),
        check_vma=False,
    )
```

```python
import math
from types import SimpleNamespace

import jax
import jax.numpy as jnp
from jax import lax
from jax.experimental import pallas as pl
from jax.experimental.pallas import tpu as pltpu
from jax.sharding import PartitionSpec as P

f32 = jnp.float32
bf16 = jnp.bfloat16
MESH = pl.DeviceIdType.MESH

HEAD_DIM = 64
SLOT_LEN = 256
QRY_LEN = 32
NORM_EPS = 1e-12
BLK = 256
PIECE = 64
RING = 8
DEAD = -1e30


def dot(a, b):
    return lax.dot_general(a, b, (((1,), (0,)), ((), ())), preferred_element_type=f32)


def dot_t(a, b):
    return lax.dot_general(a, b, (((1,), (1,)), ((), ())), preferred_element_type=f32)


def dot_l(a, b):
    return lax.dot_general(a, b, (((0,), (0,)), ((), ())), preferred_element_type=f32)


def loop(n, body, lo=0):
    def step(i, carry):
        body(i)
        return carry

    lax.fori_loop(lo, n, step, 0)


def layer_kernel(n_dp, dims, names, *refs):
    R = SimpleNamespace(**dict(zip(names, refs)))
    rows, width, slots, queries, local_width = dims
    blocks = rows // BLK
    heads = local_width // HEAD_DIM
    groups = n_dp // RING
    cands = 8 * n_dp
    loss_scale = 2.0 / math.sqrt(width)
    quarter = width
    own = blocks * PIECE
    part_rows = own // 2

    dp = lax.axis_index("dp")
    t = lax.axis_index("tensor")
    y = lax.div(t, 2)
    c = lax.rem(t, 2)
    t1 = 2 * y + (1 - c)
    t2 = 2 * (1 - y) + c
    t3 = 2 * (1 - y) + (1 - c)
    core = (dp, t1)
    ypeer = (dp, t2)
    mates = ((dp, t1), (dp, t2), (dp, t3))

    group = lax.div(dp, RING)
    place = lax.rem(dp, RING)

    def place_of(r):
        return jnp.where(r < 4, 2 * r, 2 * (7 - r) + 1)

    r = jnp.where(lax.rem(place, 2) == 0, lax.div(place, 2), 7 - lax.div(place, 2))
    ring_to = (
        (group * RING + place_of(lax.rem(r + 1, RING)), t),
        (group * RING + place_of(lax.rem(r + RING - 1, RING)), t),
    )

    def dp_at(k):
        return lax.rem(dp + k, n_dp)

    (S_SHARE, S_WCORE, S_WRING, S_WON, S_BIAS, S_CORE0, S_Y0, S_CORE1, S_Y1, S_X1, S_FIRST, S_DF, S_DA, S_OUT, S_MAIL,
     S_BACK, S_VEC, S_TSUM, S_RING, S_GATHER, S_LOCAL, S_GLOCAL, S_GCORE, S_OUTL) = range(24)

    def cp(src, dst, kind, rsem, dev):
        return pltpu.make_async_remote_copy(
            src_ref=src, dst_ref=dst, send_sem=R.ss.at[kind], recv_sem=rsem, device_id=dev, device_id_type=MESH
        )

    def arrived(ref, rsem):
        cp(ref, ref, S_SHARE, rsem, core).wait_recv()

    def sent(ref, kind):
        cp(ref, ref, kind, R.wc_r.at[0], core).wait_send()

    loads = [
        pltpu.make_async_copy(R.wqkv_in, R.wqkv, R.load_sem.at[0]),
        pltpu.make_async_copy(R.hid_in, R.hid, R.load_sem.at[1]),
        pltpu.make_async_copy(R.wo_in, R.wo, R.load_sem.at[2]),
        pltpu.make_async_copy(R.w1, R.wf1.at[t], R.load_sem.at[3]),
        pltpu.make_async_copy(R.w2, R.wf2.at[t], R.load_sem.at[4]),
        pltpu.make_async_copy(R.upstream.at[:, t], R.up, R.load_sem.at[5]),
    ]
    for one in loads:
        one.start()

    barrier = pltpu.get_barrier_semaphore()
    for mate in mates:
        pl.semaphore_signal(barrier, inc=1, device_id=mate, device_id_type=MESH)

    def greet(k):
        pl.semaphore_signal(barrier, inc=1, device_id=(dp_at(k), t), device_id_type=MESH)

    loop(n_dp, greet, 1)
    pl.semaphore_wait(barrier, 3 + n_dp - 1)

    share = quarter // RING
    half = share // 2
    wfs = (R.wf1, R.wf2)
    wins = (R.w1, R.w2)
    rb = R.rb

    def unit(chunk, sub):
        return pl.ds(pl.multiple_of(chunk * share + sub * half, half), half)

    def from_here(d, s):
        return lax.rem(r - s + 2 * RING, RING) if d == 0 else lax.rem(r + s + 2 * RING, RING)

    def w_share(k):
        at = pl.ds(pl.multiple_of(r * share, share), share)
        return cp(wins[k].at[at], wfs[k].at[t, at], S_SHARE, R.wy_r.at[k], ypeer)

    def w_send(k, at, d, idx):
        ref = wfs[k].at[t2, at]
        cp(ref, ref, S_WRING, R.wr_r.at[k, idx], ring_to[d]).start()

    def w_on(k, at):
        ref = wfs[k].at[t2, at]
        cp(ref, ref, S_WON, R.wf_r.at[k], core).start()

    def w_start(k):
        at = pl.ds(pl.multiple_of(r * share, share), share)
        arrived(wfs[k].at[t2, at], R.wy_r.at[k])
        for d in range(2):
            w_send(k, unit(r, d), d, 0)
            w_send(k, unit(r, 1 - d), d, 4)
        w_on(k, at)

    def w_pass(k, s, lead):
        idx = s - 1 if lead else s + 3
        arrived(rb.at[0, :, 0], R.wr_r.at[k, idx])
        for d in range(2):
            at = unit(from_here(d, s), d if lead else 1 - d)
            if s < (4 if lead else 3):
                w_send(k, at, d, idx + 1)
            w_on(k, at)

    def w_jobs(k):
        return [lambda: w_start(k)] + [
            lambda s=s, lead=lead: w_pass(k, s, lead)
            for s, lead in ((1, True), (1, False), (2, True), (2, False), (3, True), (3, False), (4, True))
        ]

    wa, wb = w_jobs(0), w_jobs(1)

    for k in range(2):
        w_share(k).start()
    for k in range(2):
        cp(wins[k], wfs[k].at[t], S_WCORE, R.wc_r.at[0], core).start()
    R.bias1[t] = jnp.broadcast_to(R.b1[...].astype(f32).reshape(1, quarter), (8, quarter))
    for mate in mates:
        cp(R.bias1.at[t], R.bias1.at[t], S_BIAS, R.bi_r.at[0], mate).start()

    part = R.part
    keep, send1, got1, send2, got2 = R.keep, R.send1, R.got1, R.send2, R.got2

    def rs0(e, i):
        for yy in range(2):
            mine = pl.ds(pl.multiple_of((2 * yy + c) * PIECE, PIECE), PIECE)
            other = pl.ds(pl.multiple_of((2 * yy + 1 - c) * PIECE, PIECE), PIECE)
            keep[i, yy] = part[mine].astype(bf16)
            send1[i, yy] = part[other].astype(bf16)
        cp(send1.at[i], got1.at[i], (S_CORE0, S_CORE1)[e], R.rc_r.at[e, i], core).start()

    def rs1(i):
        arrived(got1.at[i], R.rc_r.at[0, i])
        send2[i, 0] = (keep[i, 1 - y].astype(f32) + got1[i, 1 - y].astype(f32)).astype(bf16)
        cp(send2.at[i, 0], got2.at[i, 0], S_Y0, R.ry_r.at[0, i], ypeer).start()

    def rs2(i):
        arrived(got2.at[i, 0], R.ry_r.at[0, i])
        return keep[i, y].astype(f32) + got1[i, y].astype(f32) + got2[i, 0].astype(f32)

    def ag0(mine, kind, ysem, csem):
        cp(mine, mine, kind, ysem, ypeer).start()
        cp(mine, mine, kind, csem, core).start()

    def ag1(theirs, kind, ysem, csem):
        arrived(theirs, ysem)
        cp(theirs, theirs, kind, csem, core).start()

    def ag2(first, second, csem):
        arrived(first, csem)

    hid, wqkv, wo = R.hid, R.wqkv, R.wo
    lane = lax.broadcasted_iota(jnp.int32, (1, local_width), 1)
    head_f = [jnp.where(lax.shift_right_logical(lane, 6) == h, 1.0, 0.0).astype(f32) for h in range(heads)]
    head_b = [m.astype(bf16) for m in head_f]
    q_bias = R.qv_bias[0:1].astype(f32)
    v_bias = R.qv_bias[1:2].astype(f32)
    head_scale = 1.0 / math.sqrt(HEAD_DIM)

    def allowed_of(i):
        row = lax.broadcasted_iota(jnp.int32, (BLK, 1), 0)
        col = lax.broadcasted_iota(jnp.int32, (1, BLK), 1)
        split = 1 - R.bucket[jnp.minimum(i, slots - 1)]
        is_query = jnp.where(i >= slots, 1, 0)

        def seg(at):
            in_query = lax.shift_right_logical(at, 5)
            in_slot = lax.shift_right_logical(at, 7) * split
            return in_query * is_query + in_slot * (1 - is_query)

        return (seg(row) == seg(col)) & (R.mask[blk(i)].reshape(1, BLK) == 1)

    def blk(i):
        return pl.ds(pl.multiple_of(i * BLK, BLK), BLK)

    def attend(i):
        h_in = hid[blk(i)]
        q = (dot_t(h_in, wqkv[0]) + q_bias).astype(bf16)
        k = dot_t(h_in, wqkv[1]).astype(bf16)
        v = (dot_t(h_in, wqkv[2]) + v_bias).astype(bf16)
        R.q[blk(i)] = q
        R.k[blk(i)] = k
        R.v[blk(i)] = v
        allowed = allowed_of(i)
        context = jnp.zeros((BLK, local_width), f32)
        for h in range(heads):
            s = jnp.where(allowed, dot_t(q * head_b[h], k) * head_scale, DEAD)
            e = jnp.exp(s - jnp.max(s, axis=-1, keepdims=True))
            p = (e / jnp.sum(e, axis=-1, keepdims=True)).astype(bf16)
            R.pb[i, h] = p
            context = context + dot(p, v) * head_f[h]
        low = context.astype(bf16)
        R.ctx[blk(i)] = low
        part[...] = dot(low, wo[...])

    def norm_fwd(v, gain, bias):
        centre = v - jnp.mean(v, axis=-1, keepdims=True)
        rstd = lax.rsqrt(jnp.mean(centre * centre, axis=-1, keepdims=True) + NORM_EPS)
        n = centre * rstd
        return n, rstd, n * gain + bias

    def norm_bwd(dy, n, rstd, gain):
        e = dy * gain
        return (e - jnp.mean(e, axis=-1, keepdims=True) - n * jnp.mean(e * n, axis=-1, keepdims=True)) * rstd

    def vec_of(ref):
        return ref[...].astype(f32).reshape(1, width)

    vec = SimpleNamespace(
        ob=vec_of(R.ob), g1=vec_of(R.g1), n1b=vec_of(R.n1b), fb=vec_of(R.fb), g2=vec_of(R.g2), n2b=vec_of(R.n2b)
    )
    x1 = R.x1
    h1, n1, n2 = R.h1, R.n1, R.n2
    rstd1, rstd2 = R.rstd1, R.rstd2

    def own_rows(i):
        return pl.ds(pl.multiple_of(i * BLK + t * PIECE, PIECE), PIECE)

    def part_at(b, i):
        return pl.ds(pl.multiple_of(b * part_rows + i * 32, 32), 32)

    def first_norm(i):
        v = hid[own_rows(i)].astype(f32) + rs2(i) + vec.ob
        n, rstd, out = norm_fwd(v, vec.g1, vec.n1b)
        wide_rstd = jnp.broadcast_to(rstd, (PIECE, 128)).reshape(2, 2, 16, 128)
        n = n.reshape(2, 2, 16, width)
        low = out.astype(bf16)
        out = out.reshape(2, 2, 16, width)
        low4 = low.reshape(2, 2, 16, width)
        for b in range(2):
            n1[part_at(b, i)] = n[:, b].reshape(32, width)
            rstd1[part_at(b, i)] = wide_rstd[:, b].reshape(32, 128)
            h1[part_at(b, i)] = out[:, b].reshape(32, width)
            R.x1_own[part_at(b, i)] = low4[:, b].reshape(32, width)
        x1[i, t] = low

    def at_step(s, jobs):
        for i, job in jobs.items():
            pl.when(s == i)(job)

    def both(*jobs):
        def run():
            for job in jobs:
                job()

        return run

    def fwd_step(s):
        attend(s)
        rs0(0, s)

        @pl.when(s >= 1)
        def _():
            rs1(s - 1)

        at_step(s, {1: wa[0], 4: both(wa[1], wb[0]), 5: wa[2]})

    for one in loads[:3]:
        one.wait()
    loop(blocks, fwd_step)
    rs1(blocks - 1)

    wa[3]()

    def norm_step(s):
        first_norm(s)
        at_step(s, {0: wb[1], 1: wa[4], 2: both(wb[2], wa[5]), 3: wb[3], 4: both(wa[6], wb[4]), 5: wa[7]})

    loop(blocks, norm_step)
    def x1_out(i):
        ag0(x1.at[i, t], S_X1, R.gy_r.at[i], R.gc_r.at[i])

    loop(blocks - 2, x1_out)

    for one in loads[3:]:
        one.wait()
    arrived(R.bias1.at[0:3], R.bi_r.at[0])
    arrived(R.wf1.at[0:2], R.wc_r.at[0])
    act, slope = R.act, R.slope

    def gelu(u):
        cdf = 0.5 * (1.0 + lax.erf(u * (1.0 / math.sqrt(2.0))))
        pdf = jnp.exp(-0.5 * u * u) * (1.0 / math.sqrt(2.0 * math.pi))
        return (u * cdf).astype(bf16), (cdf + u * pdf).astype(bf16)

    wide = R.wide
    act_own = R.da

    def nth(j):
        return jnp.where(j == 0, t, jnp.where(j == 1, t1, jnp.where(j == 2, t2, t3)))

    def own_in(j):
        q = nth(j)
        u = dot(R.x1_own[...], wfs[0][q]) + R.bias1[q, 0:1]
        a, sl = gelu(u)
        R.slope_own[q] = sl
        act_own[:, q] = a.reshape(blocks, 2, 2, 16, width)

    def own_out(j):
        q = nth(j)
        wide[...] += dot(act_own[:, q].reshape(own, width), wfs[1][q])

    def x1_on(i):
        ag1(x1.at[i, t2], S_X1, R.gy_r.at[i], R.gc_r.at[i])

    def quarter_fwd(i):
        arrived(x1.at[i, 0:2], R.gc_r.at[i])
        u = dot(x1[i].reshape(BLK, width), wfs[0][t]) + R.bias1[t, 0:1]
        a, sl = gelu(u)
        act[i] = a.reshape(4, 2, 2, 16, width)
        slope[i] = sl.reshape(4, 2, 2, 16, width)

    def own_step(s):
        own_in(s)
        at_step(
            s, {0: wb[5], 1: both(wb[6], lambda: arrived(R.wf1.at[0], R.wf_r.at[0])), 2: wb[7]}
        )

    loop(4, own_step)
    wide[...] = jnp.zeros((own, width), f32)

    def out_step(s):
        at_step(s, {3: lambda: arrived(R.wf2.at[0], R.wf_r.at[1])})
        own_out(s)

    loop(4, out_step)

    low_out = R.low

    def second_norm(j):
        at = pl.ds(pl.multiple_of(j * PIECE, PIECE), PIECE)
        n, rstd, out = norm_fwd(h1[at] + wide[at] + vec.fb, vec.g2, vec.n2b)
        n2[at] = n
        rstd2[at] = jnp.broadcast_to(rstd, (PIECE, 128))
        h1[at] = out
        b = lax.div(j, blocks // 2)
        i = 2 * lax.rem(j, blocks // 2)
        low_out[pl.ds(i, 2), :, b] = out.astype(bf16).reshape(2, 2, 16, width)

    loop(blocks, second_norm)

    firsts = R.firsts
    stage = R.stage
    stage[...] = jnp.zeros((16, width), f32)
    for b in range(blocks - slots):
        for k in range(2):
            at = (slots + b) * 32 + 16 * k
            stage[2 * b + k : 2 * b + k + 1] = h1[at : at + 1]
    for s in range(slots):
        stage[6 + s : 7 + s] = h1[32 * s : 32 * s + 1]
    firsts[t] = stage[...].astype(bf16)
    for mate in mates:
        cp(firsts.at[t], firsts.at[t], S_FIRST, R.fi_r.at[0], mate).start()

    sums = R.sums
    sums[...] = jnp.zeros((16, width), f32)
    adds = R.adds
    up, dv2, df, da = R.up, R.n2, R.df, R.da
    dv1 = R.h1

    def colsum(v):
        return jnp.sum(v, axis=0, keepdims=True)

    def second_back(b):
        def one(i):
            at = part_at(b, i)
            dy = up[i, :, b].reshape(32, width).astype(f32)
            if b == 0:
                row = lax.broadcasted_iota(jnp.int32, (32, 1), 0)
                dy = dy + jnp.where(row == 0, adds[i, 0:1], 0.0) + jnp.where(row == 16, adds[i, 1:2], 0.0)
            n = n2[at]
            sums[0:1] += colsum(dy * n)
            sums[1:2] += colsum(dy)
            dv = norm_bwd(dy, n, rstd2[at][:, 0:1], vec.g2)
            dv2[at] = dv
            low = dv.astype(bf16)
            sums[2:3] += colsum(low.astype(f32))
            df[i, t, :, b] = low.reshape(2, 16, width)

        loop(blocks, one)
        ag0(df.at[:, t, :, b], S_DF, R.fy_r.at[b], R.fc_r.at[b])

    def own_bwd(b):
        at = pl.ds(b * part_rows, part_rows)
        wide[at] = dv2[at]

        def one(q):
            dg = dot_t(df[:, t, :, b].reshape(part_rows, width), wfs[1][q])
            du = (dg * R.slope_own[q, at].astype(f32)).astype(bf16)
            wide[at] += dot_t(du, wfs[0][q])

        loop(4, one)

        def first_back(i):
            at = part_at(b, i)
            dy = wide[at]
            n = n1[at]
            sums[3:4] += colsum(dy * n)
            sums[4:5] += colsum(dy)
            dv = norm_bwd(dy, n, rstd1[at][:, 0:1], vec.g1)
            dv1[at] = dv
            low = dv.astype(bf16)
            sums[5:6] += colsum(low.astype(f32))
            da[i, t, :, b] = low.reshape(2, 16, width)

        loop(blocks, first_back)
        ag0(da.at[:, t, :, b], S_DA, R.ay_r.at[b], R.ac_r.at[b])

    def df_on(b):
        ag1(df.at[:, t2, :, b], S_DF, R.fy_r.at[b], R.fc_r.at[b])

    def da_on(b):
        ag1(da.at[:, t2, :, b], S_DA, R.ay_r.at[b], R.ac_r.at[b])

    du_all = slope

    def quarter_bwd(b):
        def one(j):
            at = pl.ds(2 * j, 2)
            dg = dot_t(df[at, :, :, b].reshape(BLK, width), wfs[1][t])
            du = (dg * slope[at, :, :, b].reshape(BLK, width).astype(f32)).astype(bf16)
            sums[8:9] += colsum(du.astype(f32))
            du_all[at, :, :, b] = du.reshape(2, 4, 2, 16, width)

        loop(blocks // 2, one)

    second_back(1)
    loop(blocks, x1_out, blocks - 2)

    arrived(firsts.at[0:3], R.fi_r.at[0])
    hw = width // 2
    pack = R.pack
    pack[...] = jnp.zeros((16, hw + 128), f32)
    cand_rows = [firsts[0].astype(f32), firsts[2].astype(f32)]
    for k in range(2):
        pack[3 * k : 3 * k + 3, 0:hw] = cand_rows[k][6:9, 0:hw]
        pack[8 + 3 * k : 11 + 3 * k, 0:hw] = cand_rows[k][6:9, hw:width]
    for s in range(slots):
        pack[3 + s : 4 + s, hw : hw + 128] = jnp.zeros((1, 128), f32) + R.bucket[s].astype(f32)
    pack[6:8, hw : hw + 128] = jnp.ones((2, 128), f32)
    mail = R.mail
    mail[dp] = pack[...].astype(bf16)
    loop(n_dp, lambda k: cp(mail.at[dp], mail.at[dp], S_MAIL, R.dp_r.at[0], (dp_at(k), t)).start(), 1)

    qe = R.qe
    qe[...] = jnp.zeros(qe.shape, f32)
    for tt in range(4):
        qe[8 * tt : 8 * tt + 6, 0:width] = firsts[tt].astype(f32)[0:6]
    lane_e = lax.broadcasted_iota(jnp.int32, (32, 128), 1)
    qe[:, width : width + 128] = jnp.where(lane_e == 0, DEAD, 0.0)
    row_q = lax.broadcasted_iota(jnp.int32, (32, 1), 0)
    target_at = jnp.full((32, 1), -1, jnp.int32)
    for tt in range(4):
        for b in range(blocks - slots):
            for k in range(2):
                pos = R.positive[b * 8 + tt * 2 + k]
                slot = lax.div(pos, 2)
                at = lax.div(slot, slots) * 8 + lax.rem(pos, 2) * 3 + lax.rem(slot, slots)
                target_at = jnp.where(row_q == 8 * tt + 2 * b + k, at, target_at)

    own_bwd(1)
    loop(blocks - 2, x1_on)

    arrived(mail.at[1:], R.dp_r.at[0])
    pe = R.pe

    def unpack(n):
        got = mail[n].astype(f32)
        at = pl.ds(pl.multiple_of(n * 8, 8), 8)
        pe[at, 0:hw] = got[0:8, 0:hw]
        pe[at, hw:width] = got[8:16, 0:hw]
        pe[at, width : width + 128] = got[0:8, hw : hw + 128]

    loop(n_dp, unpack)
    pe_low = pe[...].astype(bf16)
    qe_low = qe[...].astype(bf16)
    z = dot_t(qe_low, pe_low) * loss_scale
    peak = jnp.max(z, axis=1, keepdims=True)
    total = peak + jnp.log(jnp.sum(jnp.exp(z - peak), axis=1, keepdims=True))
    target = lax.broadcasted_iota(jnp.int32, (32, cands), 1) == target_at
    live = target_at >= 0
    picked = jnp.sum(jnp.where(target, z, 0.0), axis=1, keepdims=True)
    ce = jnp.where(live, total - picked, 0.0)
    loss = jnp.sum(ce, axis=0, keepdims=True)
    dz = jnp.where(live, jnp.exp(z - total) - jnp.where(target, 1.0, 0.0), 0.0).astype(bf16)
    dqe = R.dqe
    dqe[...] = dot(dz, pe_low[:, 0:width]) * loss_scale
    dpe = R.dpe
    dpe[...] = (dot_l(dz, qe_low[:, 0:width]) * loss_scale).reshape(n_dp, 8, width)
    back = R.back

    @pl.when(c == 0)
    def _():
        loop(n_dp, lambda k: cp(dpe.at[dp_at(k)], back.at[dp], S_BACK, R.dp_r.at[1], (dp_at(k), t)).start(), 1)

    back[dp] = dpe[dp]

    df_on(1)
    loop(blocks - 2, quarter_fwd)
    loop(blocks, x1_on, blocks - 2)
    loop(blocks, quarter_fwd, blocks - 2)
    arrived(df.at[:, 0:2, :, 1], R.fc_r.at[1])
    quarter_bwd(1)

    @pl.when(c == 0)
    def _():
        arrived(back.at[1:], R.dp_r.at[1])
        stage[0:8] = back[0]

        def add(n):
            stage[0:8] += back[n]

        loop(n_dp, add, 1)

    mine_q = dqe[pl.ds(pl.multiple_of(t * 8, 8), 8)]
    is_c0 = jnp.where(c == 0, 1.0, 0.0).astype(f32)
    adds[...] = jnp.zeros(adds.shape, f32)
    for s in range(slots):
        adds[s, 0:1] = jnp.where(y == 0, stage[s : s + 1], stage[3 + s : 4 + s]) * is_c0
    for b in range(blocks - slots):
        adds[slots + b, 0:2] = mine_q[2 * b : 2 * b + 2]
    second_back(0)
    own_bwd(0)

    sums[6:7] = jnp.where(t == 0, loss, 0.0) + jnp.zeros((1, width), f32)
    tsum = R.tsum
    tsum[t] = sums[0:8]
    for mate in mates:
        cp(tsum.at[t], tsum.at[t], S_TSUM, R.ts_r.at[0], mate).start()

    grads = (R.ga1, R.ga2, R.ga3)
    outs = (R.o1, R.o2, R.o3)

    def to_owner(d, s):
        return from_here(1 - d, 4 - s)

    def ring_send(k, d, src, idx):
        cp(src, rb.at[k, d, idx], S_RING, R.rr_r.at[k, idx], ring_to[d]).start()

    def ring_start(k):
        for d in range(2):
            ring_send(k, d, grads[k].at[unit(to_owner(d, 0), d)], 0)
            ring_send(k, d, grads[k].at[unit(to_owner(d, 1), 1 - d)], 4)

    def ring_add(k, s, lead):
        idx = s - 1 if lead else s + 2
        arrived(rb.at[k, :, idx], R.rr_r.at[k, idx])
        for d in range(2):
            slot = rb.at[k, d, idx]
            mine = grads[k][unit(to_owner(d, s), d if lead else 1 - d)]
            slot[...] = (slot[...].astype(f32) + mine.astype(f32)).astype(bf16)
            ring_send(k, d, slot, idx + 1)

    def gather_send(k, d, src, at, idx):
        cp(src, outs[k].at[at], S_GATHER, R.rg_r.at[k, idx], ring_to[d]).start()

    def ring_turn(k):
        for idx in (3, 6):
            arrived(rb.at[k, :, idx], R.rr_r.at[k, idx])
        for a in range(2):
            mine = grads[k][unit(r, a)].astype(f32)
            rb[k, a, 3] = (rb[k, a, 3].astype(f32) + rb[k, 1 - a, 6].astype(f32) + mine).astype(bf16)
        if groups > 1:

            def swap(a, g):
                at = (k * 2 + a) * (groups - 1) + g - 1
                dev = (lax.rem(group + g, groups) * RING + place, t)
                return pltpu.make_async_remote_copy(
                    src_ref=rb.at[k, a, 3], dst_ref=R.gb.at[at], send_sem=R.gr_s.at[at], recv_sem=R.gr_r.at[at],
                    device_id=dev, device_id_type=MESH,
                )

            both = [(a, g) for a in range(2) for g in range(1, groups)]
            for a, g in both:
                swap(a, g).start()
            for a, g in both:
                swap(a, g).wait()
            for a in range(2):
                tot = rb[k, a, 3].astype(f32)
                for g in range(1, groups):
                    tot = tot + R.gb[(k * 2 + a) * (groups - 1) + g - 1].astype(f32)
                rb[k, a, 3] = tot.astype(bf16)
        for d in range(2):
            gather_send(k, d, rb.at[k, d, 3], unit(r, d), 0)
            gather_send(k, d, rb.at[k, 1 - d, 3], unit(r, 1 - d), 4)
        for a in range(2):
            pltpu.make_async_copy(rb.at[k, a, 3], outs[k].at[unit(r, a)], R.ss.at[S_LOCAL]).start()

    def gather_on(k, s, lead):
        idx = s - 1 if lead else s + 3
        arrived(rb.at[k, :, 0], R.rg_r.at[k, idx])
        if s < (4 if lead else 3):
            for d in range(2):
                at = unit(from_here(d, s), d if lead else 1 - d)
                gather_send(k, d, outs[k].at[at], at, idx + 1)

    def ring_jobs(k):
        return [
            lambda: ring_add(k, 1, True), lambda: ring_add(k, 2, False), lambda: ring_add(k, 2, True),
            lambda: ring_add(k, 3, False), lambda: ring_add(k, 3, True), lambda: ring_turn(k),
            lambda: gather_on(k, 1, True), lambda: gather_on(k, 1, False), lambda: gather_on(k, 2, True),
            lambda: gather_on(k, 2, False), lambda: gather_on(k, 3, True), lambda: gather_on(k, 3, False),
            lambda: gather_on(k, 4, True),
        ]

    da_on(1)
    part_all = rows // 2

    def grad2(b):
        def one(j):
            at = pl.ds(pl.multiple_of(j * BLK, BLK), BLK)
            new = dot_l(act[:, :, :, b, :, at].reshape(part_all, BLK), df[:, :, :, b].reshape(part_all, width))
            if b == 0:
                new = new + grads[1][at].astype(f32)
            grads[1][at] = new.astype(bf16)

        loop(quarter // BLK, one)

    def grad1(b):
        def one(j):
            at = pl.ds(pl.multiple_of(j * BLK, BLK), BLK)
            x1_part = x1[...].reshape(blocks, 4, 2, 2, 16, width)[:, :, :, b].reshape(part_all, width)
            new = dot_l(x1_part, du_all[:, :, :, b, :, at].reshape(part_all, BLK))
            if b == 0:
                new = new + grads[0][:, at].astype(f32)
            grads[0][:, at] = new.astype(bf16)

        loop(quarter // BLK, one)

    grad2(1)
    grad1(1)
    df_on(0)
    arrived(df.at[:, 0:2, :, 0], R.fc_r.at[0])
    grad2(0)
    ring_start(1)
    quarter_bwd(0)
    grad1(0)
    ring_start(0)
    da_on(0)

    dq_all, dk_all, dv_all = R.q, R.k, R.v

    def attend_back(i):
        da_i = da[i].reshape(BLK, width)
        dc = dot_t(da_i, wo[...]).astype(bf16)
        q = R.q[blk(i)]
        k = R.k[blk(i)]
        v = R.v[blk(i)]
        dq = jnp.zeros((BLK, local_width), f32)
        dk = jnp.zeros((BLK, local_width), f32)
        dv = jnp.zeros((BLK, local_width), f32)
        for h in range(heads):
            dch = dc * head_b[h]
            p = R.pb[i, h]
            pf = p.astype(f32)
            dp_h = dot_t(dch, v)
            ds = (pf * (dp_h - jnp.sum(pf * dp_h, axis=-1, keepdims=True))).astype(bf16)
            dq = dq + dot(ds, k) * head_f[h]
            dk = dk + dot_l(ds, q * head_b[h])
            dv = dv + dot_l(p, dch)
        dq = (dq * head_scale).astype(bf16)
        dk = (dk * head_scale).astype(bf16)
        dv = dv.astype(bf16)
        dq_all[blk(i)] = dq
        dk_all[blk(i)] = dk
        dv_all[blk(i)] = dv
        sums[9:10, 0:local_width] += colsum(dq.astype(f32))
        sums[10:11, 0:local_width] += colsum(dv.astype(f32))
        part[...] = dot(dq, wqkv[0]) + dot(dk, wqkv[1]) + dot(dv, wqkv[2])

    gin = R.grad_in

    def gin1(i):
        arrived(got1.at[i], R.rc_r.at[1, i])
        mine = [dv1[part_at(b, i)].reshape(2, 16, width) for b in range(2)]
        mine = jnp.stack(mine, axis=1).reshape(PIECE, width)
        for yy in range(2):
            has = jnp.where(y == yy, 1.0, 0.0).astype(f32)
            send2[i, yy] = (keep[i, yy].astype(f32) + got1[i, yy].astype(f32) + mine * has).astype(bf16)
        cp(send2.at[i], got2.at[i], S_Y1, R.ry_r.at[1, i], ypeer).start()

    def gin2(i):
        arrived(got2.at[i], R.ry_r.at[1, i])
        for yy in range(2):
            got2[i, yy] = (send2[i, yy].astype(f32) + got2[i, yy].astype(f32)).astype(bf16)
            dst = gin.at[i, 2 * yy + c]
            pltpu.make_async_copy(got2.at[i, yy], dst, R.ss.at[S_GLOCAL]).start()
            cp(got2.at[i, yy], dst, S_GCORE, R.go_r.at[0], core).start()

    sent(send1, S_CORE0)
    sent(send2.at[:, 0], S_Y0)
    for b in range(2):
        arrived(da.at[:, 0:2, :, b], R.ac_r.at[b])

    jobs1, jobs0, jobs2 = ring_jobs(1), ring_jobs(0), ring_jobs(2)
    n_early = blocks

    def back_step(s):
        attend_back(s)
        rs0(1, s)

        @pl.when(s >= 1)
        def _():
            gin1(s - 1)

        at_step(s, dict(enumerate(jobs1[:n_early])))
        at_step(s, dict(enumerate(jobs0[:n_early])))

        @pl.when(s >= 3)
        def _():
            gin2(s - 3)

    loop(blocks, back_step)

    out = R.layer_out
    out_own = pltpu.make_async_copy(low_out, out.at[:, t], R.ss.at[S_OUTL])
    out_own.start()
    cp(low_out, out.at[:, t], S_OUT, R.lo_r.at[0], ypeer).start()
    cp(low_out, out.at[:, t], S_OUT, R.lo_r.at[1], core).start()

    grads[2][0:local_width] = dot_l(dq_all[...], hid[...]).astype(bf16)
    grads[2][local_width : 2 * local_width] = dot_l(dk_all[...], hid[...]).astype(bf16)
    grads[2][2 * local_width : 3 * local_width] = dot_l(dv_all[...], hid[...]).astype(bf16)
    grads[2][3 * local_width : 4 * local_width] = dot_l(R.ctx[...], da[...].reshape(rows, width)).astype(bf16)
    ring_start(2)

    arrived(tsum.at[0:3], R.ts_r.at[0])
    sums[0:8] = tsum[0] + tsum[1] + tsum[2] + tsum[3]
    loss_low = sums[6:7].astype(bf16).astype(f32)
    sums[7:8] = sums[6:7] - loss_low
    vmail = R.vmail
    vmail[dp] = sums[...].astype(bf16)
    loop(n_dp, lambda k: cp(vmail.at[dp], vmail.at[dp], S_VEC, R.dp_r.at[2], (dp_at(k), t)).start(), 1)

    extra = [lambda: gin1(blocks - 1)] + [lambda i=i: gin2(i) for i in range(blocks - 3, blocks)]
    late1, late0 = jobs1[n_early:], jobs0[n_early:]
    for i in range(max(len(jobs2), len(late1), len(extra))):
        for jobs in (late1, late0, jobs2, extra):
            if i < len(jobs):
                jobs[i]()

    arrived(vmail.at[1:], R.dp_r.at[2])
    sums[...] = vmail[0].astype(f32)

    def vec_add(n):
        sums[...] += vmail[n].astype(f32)

    loop(n_dp, vec_add, 1)
    R.vec_out[...] = sums[...]
    R.firsts_out[...] = firsts[...]
    piece = x1.at[:, 0]
    arrived(piece, R.lo_r.at[0])
    cp(out.at[:, t2], out.at[:, t2], S_OUT, R.lo_r.at[1], core).start()
    arrived(x1.at[:, 0:2], R.lo_r.at[1])
    arrived(send1, R.go_r.at[0])

    out_own.wait()
    sent(x1.at[0, 0:3], S_SHARE)
    sent(R.wf1.at[0:2], S_WCORE)
    sent(rb.at[0:2], S_WRING)
    sent(R.wf1.at[0:2], S_WON)
    sent(R.bias1.at[0:3], S_BIAS)
    sent(send1, S_CORE1)
    sent(send2, S_Y1)
    for kind in (S_X1, S_DF, S_DA, S_OUT):
        sent(x1.at[:, 0:3], kind)
    sent(firsts.at[0:3], S_FIRST)
    sent(mail.at[1:], S_MAIL)
    sent(vmail.at[1:], S_VEC)
    sent(tsum.at[0:3], S_TSUM)

    @pl.when(c == 0)
    def _():
        sent(back.at[1:], S_BACK)

    sent(rb, S_RING)
    sent(rb, S_GATHER)
    sent(send1, S_GCORE)
    pltpu.make_async_copy(rb.at[0, 0, 0:6], rb.at[0, 0, 0:6], R.ss.at[S_LOCAL]).wait()
    pltpu.make_async_copy(send1, send1, R.ss.at[S_GLOCAL]).wait()


def run_layer(n_dp, ins, dims):
    rows, width, slots, queries, local_width = dims
    blocks = rows // BLK
    heads = local_width // HEAD_DIM
    own = blocks * PIECE
    groups = n_dp // RING
    share = width // RING // 2
    dma = pltpu.SemaphoreType.DMA
    vm = pltpu.VMEM
    any_ = pl.BlockSpec(memory_space=pl.ANY)
    vmem = pl.BlockSpec(memory_space=pltpu.VMEM)
    smem = pl.BlockSpec(memory_space=pltpu.SMEM)
    ins_at = dict(
        hid_in=any_, mask=vmem, bucket=smem, positive=smem, wqkv_in=any_, qv_bias=vmem, wo_in=any_, ob=vmem, g1=vmem,
        n1b=vmem, w1=any_, b1=vmem, w2=any_, fb=vmem, g2=vmem, n2b=vmem, upstream=any_,
    )
    pieces = (blocks, 4, 2, 2, 16, width)
    pairs = (blocks, 2, PIECE, width)
    outs = dict(
        layer_out=(any_, pieces, bf16),
        grad_in=(any_, (blocks, 4, PIECE, width), bf16),
        o1=(any_, (width, width), bf16),
        o2=(any_, (width, width), bf16),
        o3=(any_, (width, width), bf16),
        vec_out=(vmem, (16, width), f32),
        firsts_out=(vmem, (4, 16, width), bf16),
    )
    scratch = dict(
        hid=vm((rows, width), bf16),
        wqkv=vm((3, local_width, width), bf16),
        wo=vm((local_width, width), bf16),
        wf1=vm((4, width, width), bf16),
        wf2=vm((4, width, width), bf16),
        up=vm((blocks, 2, 2, 16, width), bf16),
        bias1=vm((4, 8, width), f32),
        part=vm((BLK, width), f32),
        keep=vm(pairs, bf16),
        send1=vm(pairs, bf16),
        got1=vm(pairs, bf16),
        send2=vm(pairs, bf16),
        got2=vm(pairs, bf16),
        q=vm((rows, local_width), bf16),
        k=vm((rows, local_width), bf16),
        v=vm((rows, local_width), bf16),
        ctx=vm((rows, local_width), bf16),
        pb=vm((blocks, heads, BLK, BLK), bf16),
        x1=vm((blocks, 4, PIECE, width), bf16),
        x1_own=vm((own, width), bf16),
        h1=vm((own, width), f32),
        n1=vm((own, width), f32),
        n2=vm((own, width), f32),
        rstd1=vm((own, 128), f32),
        rstd2=vm((own, 128), f32),
        act=vm(pieces, bf16),
        slope=vm(pieces, bf16),
        wide=vm((own, width), f32),
        slope_own=vm((4, own, width), bf16),
        low=vm((blocks, 2, 2, 16, width), bf16),
        firsts=vm((4, 16, width), bf16),
        stage=vm((16, width), f32),
        adds=vm((blocks, 8, width), f32),
        pack=vm((16, width // 2 + 128), f32),
        mail=vm((n_dp, 16, width // 2 + 128), bf16),
        qe=vm((32, width + 128), f32),
        pe=vm((n_dp * 8, width + 128), f32),
        dqe=vm((32, width), f32),
        dpe=vm((n_dp, 8, width), f32),
        back=vm((n_dp, 8, width), f32),
        sums=vm((16, width), f32),
        tsum=vm((4, 8, width), f32),
        vmail=vm((n_dp, 16, width), bf16),
        df=vm(pieces, bf16),
        da=vm(pieces, bf16),
        ga1=vm((width, width), bf16),
        ga2=vm((width, width), bf16),
        ga3=vm((width, width), bf16),
        rb=vm((3, 2, RING - 1, share, width), bf16),
        load_sem=dma((6,)),
        ss=dma((24,)),
        wc_r=dma((1,)), wy_r=dma((2,)), wf_r=dma((2,)), wr_r=dma((2, 7)), bi_r=dma((1,)),
        rc_r=dma((2, blocks)), ry_r=dma((2, blocks)),
        gy_r=dma((blocks,)), gc_r=dma((blocks,)),
        fy_r=dma((2,)), fc_r=dma((2,)), ay_r=dma((2,)), ac_r=dma((2,)),
        fi_r=dma((1,)), lo_r=dma((2,)), dp_r=dma((3,)), ts_r=dma((1,)),
        rr_r=dma((3, 7)), rg_r=dma((3, 7)), go_r=dma((1,)),
    )
    if groups > 1:
        n = 6 * (groups - 1)
        scratch.update(gb=vm((n, share, width), bf16), gr_s=dma((n,)), gr_r=dma((n,)))
    names = [*ins_at, *outs, *scratch]

    def kernel(*refs):
        layer_kernel(n_dp, dims, names, *refs)

    return pl.pallas_call(
        kernel,
        name="layer",
        out_shape=[jax.ShapeDtypeStruct(shape, kind) for _, shape, kind in outs.values()],
        in_specs=list(ins_at.values()),
        out_specs=[spec for spec, _, _ in outs.values()],
        scratch_shapes=list(scratch.values()),
        compiler_params=pltpu.CompilerParams(
            collective_id=0, has_side_effects=True, vmem_limit_bytes=64 * 2**20
        ),
    )(*[ins[n] for n in ins_at])


def run_finish(lout, gin, o1, o2, o3, sums, firsts, slots, queries, local_width, n_dp):
    rows, width = lout.shape
    steps = rows // BLK
    shapes = (
        ((rows, width), bf16), ((queries, width), bf16), ((2 * slots, width), bf16), ((1, 1), f32),
        ((rows, width), f32), ((3 * local_width, width), f32), ((2, local_width), f32), ((local_width, width), f32),
        ((width,), f32), ((width,), f32), ((width,), f32), ((width, width), f32), ((width,), f32),
        ((width, width), f32), ((width,), f32), ((width,), f32), ((width,), f32),
    )
    big = (0, 4, 5, 7, 11, 13)

    def whole(shape):
        return pl.BlockSpec(shape, lambda i: (0,) * len(shape))

    def cut(count, offset=0):
        return pl.BlockSpec((count // steps, width), lambda i: (i + offset, 0))

    def kernel(lout, gin, o1, o2, o3a, o3b, sums, firsts, *outs):
        outs[0][...] = lout[...]
        outs[4][...] = gin[...].astype(f32)
        outs[5][...] = o3a[...].astype(f32)
        outs[7][...] = o3b[...].astype(f32)
        outs[11][...] = o1[...].astype(f32)
        outs[13][...] = o2[...].astype(f32)

        @pl.when(pl.program_id(0) == 0)
        def _():
            tiles = [firsts[k].astype(f32) for k in range(4)]
            query = [tiles[q % 8 // 2][2 * (q // 8) + q % 2 : 2 * (q // 8) + q % 2 + 1] for q in range(queries)]
            outs[1][...] = jnp.concatenate(query, axis=0).astype(bf16)
            passage = [tiles[2 * (p % 2)][6 + p // 2 : 7 + p // 2] for p in range(2 * slots)]
            outs[2][...] = jnp.concatenate(passage, axis=0).astype(bf16)
            outs[3][...] = (sums[6:7, 0:1] + sums[7:8, 0:1]) * (1.0 / (queries * n_dp))
            outs[6][...] = sums[9:11, 0:local_width]
            for at, row in ((8, 5), (9, 3), (10, 4), (12, 8), (14, 2), (15, 0), (16, 1)):
                outs[at][...] = sums[row : row + 1].reshape(width)

    specs = [whole(shape) for shape, _ in shapes]
    for at in big:
        specs[at] = cut(shapes[at][0][0])
    return pl.pallas_call(
        kernel,
        name="finish",
        grid=(steps,),
        out_shape=[jax.ShapeDtypeStruct(shape, kind) for shape, kind in shapes],
        in_specs=[
            cut(rows), cut(rows), cut(width), cut(width), cut(3 * local_width),
            cut(local_width, 3 * local_width // (local_width // steps)), whole((16, width)), whole((4, 16, width)),
        ],
        out_specs=specs,
    )(lout, gin, o1, o2, o3, o3, sums, firsts)


def local(
    hidden_in, token_mask, bucket, positive, qkv_weight, qv_bias, out_weight, out_bias, norm1_gain, norm1_bias,
    ffn_in, ffn_in_bias, ffn_out, ffn_out_bias, norm2_gain, norm2_bias, upstream,
):
    rows, width = hidden_in.shape
    blocks = rows // BLK
    slots = bucket.shape[0]
    queries = positive.shape[0]
    local_width = qkv_weight.shape[2]
    n_dp = lax.axis_size("dp")
    ins = dict(
        hid_in=hidden_in, mask=token_mask, bucket=bucket, positive=positive, wqkv_in=qkv_weight.transpose(0, 2, 1),
        qv_bias=qv_bias, wo_in=out_weight, ob=out_bias, g1=norm1_gain, n1b=norm1_bias, w1=ffn_in, b1=ffn_in_bias,
        w2=ffn_out, fb=ffn_out_bias, g2=norm2_gain, n2b=norm2_bias,
        upstream=upstream.reshape(blocks, 4, 2, 2, 16, width),
    )
    lout, gin, o1, o2, o3, sums, firsts = run_layer(n_dp, ins, (rows, width, slots, queries, local_width))
    lout, gin = lout.reshape(rows, width), gin.reshape(rows, width)
    outs = run_finish(lout, gin, o1, o2, o3, sums, firsts, slots, queries, local_width, n_dp)
    lout, query, passage, loss, gin, qkv, qv, gout, gob, gg1, gn1b, gf1, gb1, gf2, gfb, gg2, gn2b = outs
    qkv = qkv.reshape(3, local_width, width).transpose(0, 2, 1)
    return (
        lout, query, passage, loss.reshape(()), gin, qkv, qv, gout, gob, gg1, gn1b, gf1, gb1, gf2, gfb, gg2, gn2b
    )


def solution(mesh):
    one, two = P("dp"), P("dp", None)
    col, row = P(None, "tensor"), P("tensor", None)
    return jax.shard_map(
        local,
        mesh=mesh,
        in_specs=(
            two, one, one, one, P(None, None, "tensor"), col, row, P(), P(), P(), col, P("tensor"), row, P(), P(), P(),
            two,
        ),
        out_specs=(
            two, two, two, P(), two, P(None, None, "tensor"), col, row, P(), P(), P(), col, P("tensor"), row, P(), P(),
            P(),
        ),
        check_vma=False,
    )
```

```python
import math
from types import SimpleNamespace

import jax
import jax.numpy as jnp
from jax import lax
from jax.experimental import pallas as pl
from jax.experimental.pallas import tpu as pltpu
from jax.sharding import PartitionSpec as P

f32 = jnp.float32
bf16 = jnp.bfloat16
MESH = pl.DeviceIdType.MESH

HEAD_DIM = 64
SLOT_LEN = 256
QRY_LEN = 32
NORM_EPS = 1e-12
BLK = 256
PIECE = 64
RING = 8
DEAD = -1e30


def dot(a, b):
    return lax.dot_general(a, b, (((1,), (0,)), ((), ())), preferred_element_type=f32)


def dot_t(a, b):
    return lax.dot_general(a, b, (((1,), (1,)), ((), ())), preferred_element_type=f32)


def dot_l(a, b):
    return lax.dot_general(a, b, (((0,), (0,)), ((), ())), preferred_element_type=f32)


def loop(n, body, lo=0):
    def step(i, carry):
        body(i)
        return carry

    lax.fori_loop(lo, n, step, 0)


def layer_kernel(n_dp, dims, names, *refs):
    R = SimpleNamespace(**dict(zip(names, refs)))
    rows, width, slots, queries, local_width = dims
    blocks = rows // BLK
    heads = local_width // HEAD_DIM
    groups = n_dp // RING
    cands = 8 * n_dp
    loss_scale = 2.0 / math.sqrt(width)
    quarter = width
    own = blocks * PIECE

    dp = lax.axis_index("dp")
    t = lax.axis_index("tensor")
    y = lax.div(t, 2)
    c = lax.rem(t, 2)
    t1 = 2 * y + (1 - c)
    t2 = 2 * (1 - y) + c
    t3 = 2 * (1 - y) + (1 - c)
    core = (dp, t1)
    ypeer = (dp, t2)
    mates = ((dp, t1), (dp, t2), (dp, t3))

    group = lax.div(dp, RING)
    place = lax.rem(dp, RING)

    def place_of(r):
        return jnp.where(r < 4, 2 * r, 2 * (7 - r) + 1)

    r = jnp.where(lax.rem(place, 2) == 0, lax.div(place, 2), 7 - lax.div(place, 2))
    ring_to = (
        (group * RING + place_of(lax.rem(r + 1, RING)), t),
        (group * RING + place_of(lax.rem(r + RING - 1, RING)), t),
    )

    def dp_at(k):
        return lax.rem(dp + k, n_dp)

    (S_SHARE, S_WCORE, S_WRING, S_WON, S_BIAS, S_CORE0, S_Y0, S_CORE1, S_Y1, S_X1, S_FIRST, S_DF, S_DA, S_OUT, S_MAIL,
     S_BACK, S_VEC, S_TSUM, S_RING, S_GATHER, S_LOCAL, S_GLOCAL, S_GCORE, S_OUTL, S_PART) = range(25)

    def cp(src, dst, kind, rsem, dev):
        return pltpu.make_async_remote_copy(
            src_ref=src, dst_ref=dst, send_sem=R.ss.at[kind], recv_sem=rsem, device_id=dev, device_id_type=MESH
        )

    def arrived(ref, rsem):
        cp(ref, ref, S_SHARE, rsem, core).wait_recv()

    def sent(ref, kind):
        cp(ref, ref, kind, R.wc_r.at[0], core).wait_send()

    loads = [
        pltpu.make_async_copy(R.wqkv_in, R.wqkv, R.load_sem.at[0]),
        pltpu.make_async_copy(R.hid_in, R.hid, R.load_sem.at[1]),
        pltpu.make_async_copy(R.wo_in, R.wo, R.load_sem.at[2]),
        pltpu.make_async_copy(R.w1, R.wf1.at[t], R.load_sem.at[3]),
        pltpu.make_async_copy(R.w2, R.wf2.at[t], R.load_sem.at[4]),
        pltpu.make_async_copy(R.upstream.at[:, t], R.up, R.load_sem.at[5]),
    ]
    for one in loads:
        one.start()

    barrier = pltpu.get_barrier_semaphore()
    for mate in mates:
        pl.semaphore_signal(barrier, inc=1, device_id=mate, device_id_type=MESH)

    def greet(k):
        pl.semaphore_signal(barrier, inc=1, device_id=(dp_at(k), t), device_id_type=MESH)

    loop(n_dp, greet, 1)
    pl.semaphore_wait(barrier, 3 + n_dp - 1)

    share = quarter // RING
    half = share // 2
    wfs = (R.wf1, R.wf2)
    wins = (R.w1, R.w2)
    rb = R.rb

    def unit(chunk, sub):
        return pl.ds(pl.multiple_of(chunk * share + sub * half, half), half)

    def from_here(d, s):
        return lax.rem(r - s + 2 * RING, RING) if d == 0 else lax.rem(r + s + 2 * RING, RING)

    def w_share(k):
        at = pl.ds(pl.multiple_of(r * share, share), share)
        return cp(wins[k].at[at], wfs[k].at[t, at], S_SHARE, R.wy_r.at[k], ypeer)

    def w_send(k, at, d, idx):
        ref = wfs[k].at[t2, at]
        cp(ref, ref, S_WRING, R.wr_r.at[k, idx], ring_to[d]).start()

    def w_on(k, at):
        ref = wfs[k].at[t2, at]
        cp(ref, ref, S_WON, R.wf_r.at[k], core).start()

    def w_start(k):
        at = pl.ds(pl.multiple_of(r * share, share), share)
        arrived(wfs[k].at[t2, at], R.wy_r.at[k])
        for d in range(2):
            w_send(k, unit(r, d), d, 0)
            w_send(k, unit(r, 1 - d), d, 4)
        w_on(k, at)

    def w_pass(k, s, lead):
        idx = s - 1 if lead else s + 3
        arrived(rb.at[0, :, 0], R.wr_r.at[k, idx])
        for d in range(2):
            at = unit(from_here(d, s), d if lead else 1 - d)
            if s < (4 if lead else 3):
                w_send(k, at, d, idx + 1)
            w_on(k, at)

    def w_jobs(k):
        return [lambda: w_start(k)] + [
            lambda s=s, lead=lead: w_pass(k, s, lead)
            for s, lead in ((1, True), (1, False), (2, True), (2, False), (3, True), (3, False), (4, True))
        ]

    wa, wb = w_jobs(0), w_jobs(1)

    for k in range(2):
        w_share(k).start()
    for k in range(2):
        cp(wins[k], wfs[k].at[t], S_WCORE, R.wc_r.at[0], core).start()
    R.bias1[t] = jnp.broadcast_to(R.b1[...].astype(f32).reshape(1, quarter), (8, quarter))
    for mate in mates:
        cp(R.bias1.at[t], R.bias1.at[t], S_BIAS, R.bi_r.at[0], mate).start()

    part = R.part
    keep, send1, got1, send2, got2 = R.keep, R.send1, R.got1, R.send2, R.got2

    def rs0(e, i):
        for yy in range(2):
            mine = pl.ds(pl.multiple_of((2 * yy + c) * PIECE, PIECE), PIECE)
            other = pl.ds(pl.multiple_of((2 * yy + 1 - c) * PIECE, PIECE), PIECE)
            keep[i, yy] = part[mine].astype(bf16)
            send1[i, yy] = part[other].astype(bf16)
        cp(send1.at[i], got1.at[i], (S_CORE0, S_CORE1)[e], R.rc_r.at[e, i], core).start()

    def rs1(i):
        arrived(got1.at[i], R.rc_r.at[0, i])
        send2[i, 0] = (keep[i, 1 - y].astype(f32) + got1[i, 1 - y].astype(f32)).astype(bf16)
        cp(send2.at[i, 0], got2.at[i, 0], S_Y0, R.ry_r.at[0, i], ypeer).start()

    def rs2(i):
        arrived(got2.at[i, 0], R.ry_r.at[0, i])
        return keep[i, y].astype(f32) + got1[i, y].astype(f32) + got2[i, 0].astype(f32)

    def ag0(mine, kind, ysem, csem):
        cp(mine, mine, kind, ysem, ypeer).start()
        cp(mine, mine, kind, csem, core).start()

    def ag1(theirs, kind, ysem, csem):
        arrived(theirs, ysem)
        cp(theirs, theirs, kind, csem, core).start()

    def ag2(first, second, csem):
        arrived(first, csem)

    hid, wqkv, wo = R.hid, R.wqkv, R.wo
    lane = lax.broadcasted_iota(jnp.int32, (1, local_width), 1)
    head_f = [jnp.where(lax.shift_right_logical(lane, 6) == h, 1.0, 0.0).astype(f32) for h in range(heads)]
    head_b = [m.astype(bf16) for m in head_f]
    q_bias = R.qv_bias[0:1].astype(f32)
    v_bias = R.qv_bias[1:2].astype(f32)
    head_scale = 1.0 / math.sqrt(HEAD_DIM)

    def allowed_of(i):
        row = lax.broadcasted_iota(jnp.int32, (BLK, 1), 0)
        col = lax.broadcasted_iota(jnp.int32, (1, BLK), 1)
        split = 1 - R.bucket[jnp.minimum(i, slots - 1)]
        is_query = jnp.where(i >= slots, 1, 0)

        def seg(at):
            in_query = lax.shift_right_logical(at, 5)
            in_slot = lax.shift_right_logical(at, 7) * split
            return in_query * is_query + in_slot * (1 - is_query)

        return (seg(row) == seg(col)) & (R.mask[blk(i)].reshape(1, BLK) == 1)

    def blk(i):
        return pl.ds(pl.multiple_of(i * BLK, BLK), BLK)

    def attend(i):
        h_in = hid[blk(i)]
        q = (dot_t(h_in, wqkv[0]) + q_bias).astype(bf16)
        k = dot_t(h_in, wqkv[1]).astype(bf16)
        v = (dot_t(h_in, wqkv[2]) + v_bias).astype(bf16)
        R.q[blk(i)] = q
        R.k[blk(i)] = k
        R.v[blk(i)] = v
        allowed = allowed_of(i)
        context = jnp.zeros((BLK, local_width), f32)
        for h in range(heads):
            s = jnp.where(allowed, dot_t(q * head_b[h], k) * head_scale, DEAD)
            e = jnp.exp(s - jnp.max(s, axis=-1, keepdims=True))
            p = (e / jnp.sum(e, axis=-1, keepdims=True)).astype(bf16)
            R.pb[i, h] = p
            context = context + dot(p, v) * head_f[h]
        low = context.astype(bf16)
        R.ctx[blk(i)] = low
        part[...] = dot(low, wo[...])

    def norm_fwd(v, gain, bias):
        centre = v - jnp.mean(v, axis=-1, keepdims=True)
        rstd = lax.rsqrt(jnp.mean(centre * centre, axis=-1, keepdims=True) + NORM_EPS)
        n = centre * rstd
        return n, rstd, n * gain + bias

    def norm_bwd(dy, n, rstd, gain):
        e = dy * gain
        return (e - jnp.mean(e, axis=-1, keepdims=True) - n * jnp.mean(e * n, axis=-1, keepdims=True)) * rstd

    def vec_of(ref):
        return ref[...].astype(f32).reshape(1, width)

    vec = SimpleNamespace(
        ob=vec_of(R.ob), g1=vec_of(R.g1), n1b=vec_of(R.n1b), fb=vec_of(R.fb), g2=vec_of(R.g2), n2b=vec_of(R.n2b)
    )
    first_at = [(slots + b) * PIECE + 32 * k for b in range(blocks - slots) for k in range(2)]
    first_at += [s * PIECE for s in range(slots)]

    def pick(ref):
        rows_of = [ref[at : at + 1] for at in first_at]
        return jnp.concatenate(rows_of + [jnp.zeros((16 - len(first_at), ref.shape[1]), f32)], axis=0)

    def pick_low(ref):
        rows_of = [ref[at : at + 16].astype(f32)[0:1] for at in first_at]
        return jnp.concatenate(rows_of + [jnp.zeros((16 - len(first_at), ref.shape[1]), f32)], axis=0)

    x1 = R.x1
    h1, n1, n2 = R.h1, R.n1, R.n2
    rstd1, rstd2 = R.rstd1, R.rstd2

    def own_rows(i):
        return pl.ds(pl.multiple_of(i * BLK + t * PIECE, PIECE), PIECE)

    def piece_at(i):
        return pl.ds(pl.multiple_of(i * PIECE, PIECE), PIECE)

    def first_norm(i):
        v = hid[own_rows(i)].astype(f32) + rs2(i) + vec.ob
        n, rstd, out = norm_fwd(v, vec.g1, vec.n1b)
        n1[piece_at(i)] = n
        rstd1[piece_at(i)] = jnp.broadcast_to(rstd, (PIECE, 128))
        h1[piece_at(i)] = out
        x1[i, t] = out.astype(bf16)

    def at_step(s, jobs):
        for i, job in jobs.items():
            pl.when(s == i)(job)

    def both(*jobs):
        def run():
            for job in jobs:
                job()

        return run

    def fwd_step(s):
        attend(s)
        rs0(0, s)

        @pl.when(s >= 1)
        def _():
            rs1(s - 1)

        at_step(s, {1: wa[0], 4: both(wa[1], wb[0]), 5: wa[2]})

    for one in loads[:3]:
        one.wait()
    loop(blocks, fwd_step)
    rs1(blocks - 1)

    wa[3]()

    def norm_step(s):
        first_norm(s)
        at_step(s, {0: wb[1], 1: wa[4], 2: both(wb[2], wa[5]), 3: wb[3], 4: both(wa[6], wb[4]), 5: wa[7]})

    loop(blocks, norm_step)
    def x1_out(i):
        ag0(x1.at[i, t], S_X1, R.gy_r.at[i], R.gc_r.at[i])

    x1f = R.x1f
    x1f[t] = pick(h1).astype(bf16)

    def tile_out(tiles, which):
        for mate in mates:
            cp(tiles.at[t], tiles.at[t], S_FIRST, R.fi_r.at[which], mate).start()

    tile_out(x1f, 1)
    loop(blocks - 2, x1_out)

    for one in loads[3:]:
        one.wait()
    arrived(R.bias1.at[0:3], R.bi_r.at[0])
    arrived(R.wf1.at[0:2], R.wc_r.at[0])
    act, slope = R.act, R.slope

    def gelu(u):
        cdf = 0.5 * (1.0 + lax.erf(u * (1.0 / math.sqrt(2.0))))
        pdf = jnp.exp(-0.5 * u * u) * (1.0 / math.sqrt(2.0 * math.pi))
        return (u * cdf).astype(bf16), (cdf + u * pdf).astype(bf16)

    wide = R.wide
    act_own = R.da

    def nth(j):
        return jnp.where(j == 0, t, jnp.where(j == 1, t1, jnp.where(j == 2, t2, t3)))

    def own_in(j):
        q = nth(j)
        u = dot(x1[:, t].reshape(own, width), wfs[0][q]) + R.bias1[q, 0:1]
        a, sl = gelu(u)
        R.slope_own[q] = sl
        act_own[:, q] = a.reshape(blocks, PIECE, width)

    def own_out(j):
        q = nth(j)
        wide[...] += dot(act_own[:, q].reshape(own, width), wfs[1][q])

    def x1_on(i):
        ag1(x1.at[i, t2], S_X1, R.gy_r.at[i], R.gc_r.at[i])

    def quarter_fwd(i):
        arrived(x1.at[i, 0:2], R.gc_r.at[i])
        u = dot(x1[i].reshape(BLK, width), wfs[0][t]) + R.bias1[t, 0:1]
        a, sl = gelu(u)
        act[blk(i)] = a
        slope[blk(i)] = sl

    def own_step(s):
        own_in(s)
        at_step(
            s, {0: wb[5], 1: both(wb[6], lambda: arrived(R.wf1.at[0], R.wf_r.at[0])), 2: wb[7]}
        )

    loop(4, own_step)
    wide[...] = jnp.zeros((own, width), f32)

    def out_step(s):
        at_step(s, {3: lambda: arrived(R.wf2.at[0], R.wf_r.at[1])})
        own_out(s)

    loop(4, out_step)

    low_out = R.low

    def second_norm(j):
        at = pl.ds(pl.multiple_of(j * PIECE, PIECE), PIECE)
        n, rstd, out = norm_fwd(h1[at] + wide[at] + vec.fb, vec.g2, vec.n2b)
        n2[at] = n
        rstd2[at] = jnp.broadcast_to(rstd, (PIECE, 128))
        h1[at] = out
        low_out[j] = out.astype(bf16)

    loop(blocks, second_norm)

    firsts = R.firsts
    stage = R.stage
    stage[...] = jnp.zeros((16, width), f32)
    firsts[t] = pick(h1).astype(bf16)
    tile_out(firsts, 0)
    loop(blocks, x1_out, blocks - 2)

    sums = R.sums
    sums[...] = jnp.zeros((16, width), f32)
    up, dv2, df, da = R.up, R.n2, R.df, R.da
    dv1 = R.h1
    dfl, dal = R.dfl, R.dal
    near = blocks // 2

    def colsum(v):
        return jnp.sum(v, axis=0, keepdims=True)

    tile_n1, tile_n2 = pick(n1), pick(n2)
    tile_r1, tile_r2 = pick(rstd1)[:, 0:1], pick(rstd2)[:, 0:1]
    tile_up = pick_low(up.reshape(own, width))

    def norm2_back(dy, n, rstd):
        sums[0:1] += colsum(dy * n)
        sums[1:2] += colsum(dy)
        dv = norm_bwd(dy, n, rstd, vec.g2)
        low = dv.astype(bf16)
        sums[2:3] += colsum(low.astype(f32))
        return dv, low

    def norm1_back(dy, n, rstd):
        sums[3:4] += colsum(dy * n)
        sums[4:5] += colsum(dy)
        dv = norm_bwd(dy, n, rstd, vec.g1)
        low = dv.astype(bf16)
        sums[5:6] += colsum(low.astype(f32))
        return dv, low

    def second_back(i):
        at = piece_at(i)
        row = lax.broadcasted_iota(jnp.int32, (PIECE, 1), 0)
        is_query = jnp.where(i >= slots, 1, 0)
        late = jnp.where(row == 0, jnp.maximum(is_query, 1 - c), jnp.where(row == 32, is_query, 0))
        dy = jnp.where(late == 0, up[i].astype(f32), 0.0)
        dv, low = norm2_back(dy, n2[at], rstd2[at][:, 0:1])
        dv2[at] = dv
        df[i, t] = low

    def halves(p):
        return pl.ds(p * near, near)

    for p in range(2):
        loop((p + 1) * near, second_back, p * near)
        ag0(df.at[halves(p), t], S_DF, R.fy_r.at[p], R.fc_r.at[p])
    wide[...] = dv2[...]

    def own_bwd(q):
        dg = dot_t(df[:, t].reshape(own, width), wfs[1][q])
        du = (dg * R.slope_own[q].astype(f32)).astype(bf16)
        wide[...] += dot_t(du, wfs[0][q])

    def first_back(i):
        at = piece_at(i)
        dv, low = norm1_back(wide[at], n1[at], rstd1[at][:, 0:1])
        dv1[at] = dv
        da[i, t] = low

    def df_on(p):
        ag1(df.at[halves(p), t2], S_DF, R.fy_r.at[p], R.fc_r.at[p])

    def da_on(p):
        ag1(da.at[halves(p), t2], S_DA, R.ay_r.at[p], R.ac_r.at[p])

    def here(full, p, sem):
        arrived(full.at[halves(p), 0:2], sem.at[p])

    du_all = slope

    def quarter_bwd(i):
        dg = dot_t(df[i].reshape(BLK, width), wfs[1][t])
        du = (dg * slope[blk(i)].astype(f32)).astype(bf16)
        sums[8:9] += colsum(du.astype(f32))
        du_all[blk(i)] = du

    loop(2, own_bwd)

    arrived(firsts.at[0:3], R.fi_r.at[0])
    hw = width // 2
    pack = R.pack
    pack[...] = jnp.zeros((16, hw + 128), f32)
    cand_rows = [firsts[0].astype(f32), firsts[2].astype(f32)]
    for k in range(2):
        pack[3 * k : 3 * k + 3, 0:hw] = cand_rows[k][6:9, 0:hw]
        pack[8 + 3 * k : 11 + 3 * k, 0:hw] = cand_rows[k][6:9, hw:width]
    for s in range(slots):
        pack[3 + s : 4 + s, hw : hw + 128] = jnp.zeros((1, 128), f32) + R.bucket[s].astype(f32)
    pack[6:8, hw : hw + 128] = jnp.ones((2, 128), f32)
    mail = R.mail
    mail[dp] = pack[...].astype(bf16)
    loop(n_dp, lambda k: cp(mail.at[dp], mail.at[dp], S_MAIL, R.dp_r.at[0], (dp_at(k), t)).start(), 1)

    qe = R.qe
    qe[...] = jnp.zeros(qe.shape, f32)
    for tt in range(4):
        qe[8 * tt : 8 * tt + 6, 0:width] = firsts[tt].astype(f32)[0:6]
    lane_e = lax.broadcasted_iota(jnp.int32, (32, 128), 1)
    qe[:, width : width + 128] = jnp.where(lane_e == 0, DEAD, 0.0)
    row_q = lax.broadcasted_iota(jnp.int32, (32, 1), 0)
    target_at = jnp.full((32, 1), -1, jnp.int32)
    for tt in range(4):
        for b in range(blocks - slots):
            for k in range(2):
                pos = R.positive[b * 8 + tt * 2 + k]
                slot = lax.div(pos, 2)
                at = lax.div(slot, slots) * 8 + lax.rem(pos, 2) * 3 + lax.rem(slot, slots)
                target_at = jnp.where(row_q == 8 * tt + 2 * b + k, at, target_at)

    loop(4, own_bwd, 2)
    loop(blocks, first_back)

    def da_out(p):
        ag0(da.at[halves(p), t], S_DA, R.ay_r.at[p], R.ac_r.at[p])

    arrived(mail.at[1:], R.dp_r.at[0])
    pe = R.pe

    def unpack(n):
        got = mail[n].astype(f32)
        at = pl.ds(pl.multiple_of(n * 8, 8), 8)
        pe[at, 0:hw] = got[0:8, 0:hw]
        pe[at, hw:width] = got[8:16, 0:hw]
        pe[at, width : width + 128] = got[0:8, hw : hw + 128]

    loop(n_dp, unpack)
    pe_low = pe[...].astype(bf16)
    qe_low = qe[...].astype(bf16)
    z = dot_t(qe_low, pe_low) * loss_scale
    peak = jnp.max(z, axis=1, keepdims=True)
    total = peak + jnp.log(jnp.sum(jnp.exp(z - peak), axis=1, keepdims=True))
    target = lax.broadcasted_iota(jnp.int32, (32, cands), 1) == target_at
    live = target_at >= 0
    picked = jnp.sum(jnp.where(target, z, 0.0), axis=1, keepdims=True)
    ce = jnp.where(live, total - picked, 0.0)
    loss = jnp.sum(ce, axis=0, keepdims=True)
    dz = jnp.where(live, jnp.exp(z - total) - jnp.where(target, 1.0, 0.0), 0.0).astype(bf16)
    dqe = R.dqe
    dqe[...] = dot(dz, pe_low[:, 0:width]) * loss_scale
    dpe = R.dpe
    dpe[...] = (dot_l(dz, qe_low[:, 0:width]) * loss_scale).reshape(n_dp, 8, width)
    back = R.back

    @pl.when(c == 0)
    def _():
        loop(n_dp, lambda k: cp(dpe.at[dp_at(k)], back.at[dp], S_BACK, R.dp_r.at[1], (dp_at(k), t)).start(), 1)

    back[dp] = dpe[dp]

    loop(blocks, x1_on)
    loop(blocks - 2, quarter_fwd)
    df_on(0)
    loop(blocks, quarter_fwd, blocks - 2)
    arrived(x1f.at[0:3], R.fi_r.at[1])
    x1_late = x1f[...].reshape(64, width)
    act_late, slope_late = gelu(dot(x1_late, wfs[0][t]) + R.bias1[t, 0:1])
    R.act_late[...] = act_late

    @pl.when(c == 0)
    def _():
        arrived(back.at[1:], R.dp_r.at[1])
        stage[0:8] = back[0]

        def add(n):
            stage[0:8] += back[n]

        loop(n_dp, add, 1)

    mine_q = dqe[pl.ds(pl.multiple_of(t * 8, 8), 8)]
    row_l = lax.broadcasted_iota(jnp.int32, (16, 1), 0)
    for s in range(slots):
        stage[8 + s : 9 + s] = jnp.where(y == 0, stage[s : s + 1], stage[3 + s : 4 + s])
    grad_late = jnp.concatenate([mine_q[0:6], stage[8 : 8 + slots], jnp.zeros((16 - 6 - slots, width), f32)], axis=0)
    is_late = (row_l < 6) | ((row_l < 6 + slots) & (c == 0))
    dv2_late, low = norm2_back(jnp.where(is_late, tile_up + grad_late, 0.0), tile_n2, tile_r2)
    dfl[t] = low
    tile_out(dfl, 2)
    da_out(0)

    grads = (R.ga1, R.ga2, R.ga3)
    outs = (R.o1, R.o2, R.o3)

    def to_owner(d, s):
        return from_here(1 - d, 4 - s)

    def ring_send(k, d, src, idx):
        cp(src, rb.at[k, d, idx], S_RING, R.rr_r.at[k, idx], ring_to[d]).start()

    def ring_start(k):
        for d in range(2):
            ring_send(k, d, grads[k].at[unit(to_owner(d, 0), d)], 0)
            ring_send(k, d, grads[k].at[unit(to_owner(d, 1), 1 - d)], 4)

    def ring_add(k, s, lead):
        idx = s - 1 if lead else s + 2
        arrived(rb.at[k, :, idx], R.rr_r.at[k, idx])
        for d in range(2):
            slot = rb.at[k, d, idx]
            mine = grads[k][unit(to_owner(d, s), d if lead else 1 - d)]
            slot[...] = (slot[...].astype(f32) + mine.astype(f32)).astype(bf16)
            ring_send(k, d, slot, idx + 1)

    def gather_send(k, d, src, at, idx):
        cp(src, outs[k].at[at], S_GATHER, R.rg_r.at[k, idx], ring_to[d]).start()

    def ring_turn(k):
        for idx in (3, 6):
            arrived(rb.at[k, :, idx], R.rr_r.at[k, idx])
        for a in range(2):
            mine = grads[k][unit(r, a)].astype(f32)
            rb[k, a, 3] = (rb[k, a, 3].astype(f32) + rb[k, 1 - a, 6].astype(f32) + mine).astype(bf16)
        if groups > 1:

            def swap(a, g):
                at = (k * 2 + a) * (groups - 1) + g - 1
                dev = (lax.rem(group + g, groups) * RING + place, t)
                return pltpu.make_async_remote_copy(
                    src_ref=rb.at[k, a, 3], dst_ref=R.gb.at[at], send_sem=R.gr_s.at[at], recv_sem=R.gr_r.at[at],
                    device_id=dev, device_id_type=MESH,
                )

            both = [(a, g) for a in range(2) for g in range(1, groups)]
            for a, g in both:
                swap(a, g).start()
            for a, g in both:
                swap(a, g).wait()
            for a in range(2):
                tot = rb[k, a, 3].astype(f32)
                for g in range(1, groups):
                    tot = tot + R.gb[(k * 2 + a) * (groups - 1) + g - 1].astype(f32)
                rb[k, a, 3] = tot.astype(bf16)
        for d in range(2):
            gather_send(k, d, rb.at[k, d, 3], unit(r, d), 0)
            gather_send(k, d, rb.at[k, 1 - d, 3], unit(r, 1 - d), 4)
        for a in range(2):
            pltpu.make_async_copy(rb.at[k, a, 3], outs[k].at[unit(r, a)], R.ss.at[S_LOCAL]).start()

    def gather_on(k, s, lead):
        idx = s - 1 if lead else s + 3
        arrived(rb.at[k, :, 0], R.rg_r.at[k, idx])
        if s < (4 if lead else 3):
            for d in range(2):
                at = unit(from_here(d, s), d if lead else 1 - d)
                gather_send(k, d, outs[k].at[at], at, idx + 1)

    def ring_jobs(k):
        return [
            lambda: ring_add(k, 1, True), lambda: ring_add(k, 2, False), lambda: ring_add(k, 2, True),
            lambda: ring_add(k, 3, False), lambda: ring_add(k, 3, True), lambda: ring_turn(k),
            lambda: gather_on(k, 1, True), lambda: gather_on(k, 1, False), lambda: gather_on(k, 2, True),
            lambda: gather_on(k, 2, False), lambda: gather_on(k, 3, True), lambda: gather_on(k, 3, False),
            lambda: gather_on(k, 4, True),
        ]

    half_rows = rows // 2

    def flat(full, p):
        return full[halves(p)].reshape(half_rows, width)

    def rows_of(p):
        return pl.ds(p * half_rows, half_rows)

    def grad2(p):
        def one(j):
            at = pl.ds(pl.multiple_of(j * BLK, BLK), BLK)
            new = dot_l(act[rows_of(p), at], flat(df, p))
            if p == 1:
                new = new + grads[1][at].astype(f32) + dot_l(R.act_late[:, at], dfl[...].reshape(64, width))
            grads[1][at] = new.astype(bf16)

        loop(quarter // BLK, one)

    def grad1(p):
        def one(j):
            at = pl.ds(pl.multiple_of(j * BLK, BLK), BLK)
            new = dot_l(flat(x1, p), du_all[rows_of(p), at])
            if p == 1:
                new = new + grads[0][:, at].astype(f32) + dot_l(x1f[...].reshape(64, width), R.du_late[:, at])
            grads[0][:, at] = new.astype(bf16)

        loop(quarter // BLK, one)

    here(df, 0, R.fc_r)
    grad2(0)
    df_on(1)
    loop(near, quarter_bwd)
    arrived(dfl.at[0:3], R.fi_r.at[2])
    here(df, 1, R.fc_r)
    grad2(1)
    ring_start(1)

    dg_late = dot_t(dfl[...].reshape(64, width), wfs[1][t])
    du_late = (dg_late * slope_late.astype(f32)).astype(bf16)
    sums[8:9] += colsum(du_late.astype(f32))
    R.du_late[...] = du_late
    parts = R.parts
    parts[...] = dot_t(du_late, wfs[0][t]).astype(bf16).reshape(4, 16, width)
    for tt, mate in zip((t1, t2, t3), mates):
        cp(parts.at[tt], R.parts_in.at[t], S_PART, R.fi_r.at[4], mate).start()
    loop(blocks, quarter_bwd, near)
    jobs1, jobs0, jobs2 = ring_jobs(1), ring_jobs(0), ring_jobs(2)
    grad1(0)
    jobs1[0]()
    da_on(0)
    arrived(dfl.at[0:3], R.fi_r.at[4])
    late_sum = dv2_late + parts[t].astype(f32)
    for tt in (t1, t2, t3):
        late_sum = late_sum + R.parts_in[tt].astype(f32)
    dv1_late, low = norm1_back(jnp.where(is_late, late_sum, 0.0), tile_n1, tile_r1)
    for j, at in enumerate(first_at):
        dv1[at : at + 1] += dv1_late[j : j + 1]
    dal[t] = low
    tile_out(dal, 3)
    da_out(1)
    sums[6:7] = jnp.where(t == 0, loss, 0.0) + jnp.zeros((1, width), f32)
    tsum = R.tsum
    tsum[t] = sums[0:8]
    for mate in mates:
        cp(tsum.at[t], tsum.at[t], S_TSUM, R.ts_r.at[0], mate).start()
    grad1(1)
    ring_start(0)
    jobs1[1]()
    jobs1[2]()
    arrived(dal.at[0:3], R.fi_r.at[3])
    here(da, 0, R.ac_r)

    dq_all, dk_all, dv_all = R.q, R.k, R.v

    def attend_back(i):
        da_i = da_all[blk(i)]
        dc = dot_t(da_i, wo[...]).astype(bf16)
        q = R.q[blk(i)]
        k = R.k[blk(i)]
        v = R.v[blk(i)]
        dq = jnp.zeros((BLK, local_width), f32)
        dk = jnp.zeros((BLK, local_width), f32)
        dv = jnp.zeros((BLK, local_width), f32)
        for h in range(heads):
            dch = dc * head_b[h]
            p = R.pb[i, h]
            pf = p.astype(f32)
            dp_h = dot_t(dch, v)
            ds = (pf * (dp_h - jnp.sum(pf * dp_h, axis=-1, keepdims=True))).astype(bf16)
            dq = dq + dot(ds, k) * head_f[h]
            dk = dk + dot_l(ds, q * head_b[h])
            dv = dv + dot_l(p, dch)
        dq = (dq * head_scale).astype(bf16)
        dk = (dk * head_scale).astype(bf16)
        dv = dv.astype(bf16)
        dq_all[blk(i)] = dq
        dk_all[blk(i)] = dk
        dv_all[blk(i)] = dv
        sums[9:10, 0:local_width] += colsum(dq.astype(f32))
        sums[10:11, 0:local_width] += colsum(dv.astype(f32))
        part[...] = dot(dq, wqkv[0]) + dot(dk, wqkv[1]) + dot(dv, wqkv[2])

    gin = R.grad_in

    def gin1(i):
        arrived(got1.at[i], R.rc_r.at[1, i])
        mine = dv1[piece_at(i)]
        for yy in range(2):
            has = jnp.where(y == yy, 1.0, 0.0).astype(f32)
            send2[i, yy] = (keep[i, yy].astype(f32) + got1[i, yy].astype(f32) + mine * has).astype(bf16)
        cp(send2.at[i], got2.at[i], S_Y1, R.ry_r.at[1, i], ypeer).start()

    def gin2(i):
        arrived(got2.at[i], R.ry_r.at[1, i])
        for yy in range(2):
            got2[i, yy] = (send2[i, yy].astype(f32) + got2[i, yy].astype(f32)).astype(bf16)
            dst = gin.at[i, 2 * yy + c]
            pltpu.make_async_copy(got2.at[i, yy], dst, R.ss.at[S_GLOCAL]).start()
            cp(got2.at[i, yy], dst, S_GCORE, R.go_r.at[0], core).start()

    sent(send1, S_CORE0)
    sent(send2.at[:, 0], S_Y0)
    tile_row = lax.broadcasted_iota(jnp.int32, (16, 1), 0)
    da_all = act

    def late_rows(i):
        da_all[blk(i)] = da[i].reshape(BLK, width)
        for tt in range(4):
            tile = dal[tt].astype(f32)
            for k in range(2):
                row = jnp.where(i >= slots, 0.0, tile[6:7]) if k == 0 else jnp.zeros((1, width), f32)
                for b in range(blocks - slots):
                    row = row + jnp.where(i == slots + b, tile[2 * b + k : 2 * b + k + 1], 0.0)
                if k == 0:
                    for s in range(1, slots):
                        row = jnp.where(i == s, tile[6 + s : 7 + s], row)
                at = pl.ds(pl.multiple_of(i * BLK + tt * PIECE + 32 * k, 16), 16)
                old = da_all[at].astype(f32)
                da_all[at] = (old + jnp.where(tile_row == 0, row, 0.0)).astype(bf16)

    def back_step(s):
        at_step(s, {2: lambda: da_on(1), 3: lambda: here(da, 1, R.ac_r)})
        late_rows(s)
        attend_back(s)
        rs0(1, s)

        @pl.when(s >= 1)
        def _():
            gin1(s - 1)

        at_step(s, dict(enumerate(jobs1[3 : 3 + blocks])))
        at_step(s, dict(enumerate(jobs0[: blocks - 1], 1)))

    loop(blocks, back_step)

    out = R.layer_out
    out_own = pltpu.make_async_copy(low_out, out.at[:, t], R.ss.at[S_OUTL])
    out_own.start()
    cp(low_out, out.at[:, t], S_OUT, R.lo_r.at[0], ypeer).start()
    cp(low_out, out.at[:, t], S_OUT, R.lo_r.at[1], core).start()

    late1, late0 = jobs1[3 + blocks :], jobs0[blocks - 1 :]
    late = [job for pair in zip(late0, late1) for job in pair] + late0[len(late1) :]
    late[0]()
    late[1]()
    grads[2][0:local_width] = dot_l(dq_all[...], hid[...]).astype(bf16)
    grads[2][local_width : 2 * local_width] = dot_l(dk_all[...], hid[...]).astype(bf16)
    grads[2][2 * local_width : 3 * local_width] = dot_l(dv_all[...], hid[...]).astype(bf16)
    grads[2][3 * local_width : 4 * local_width] = dot_l(R.ctx[...], da_all[...]).astype(bf16)
    ring_start(2)

    arrived(tsum.at[0:3], R.ts_r.at[0])
    sums[0:8] = tsum[0] + tsum[1] + tsum[2] + tsum[3]
    loss_low = sums[6:7].astype(bf16).astype(f32)
    sums[7:8] = sums[6:7] - loss_low
    vmail = R.vmail
    vmail[dp] = sums[...].astype(bf16)
    loop(n_dp, lambda k: cp(vmail.at[dp], vmail.at[dp], S_VEC, R.dp_r.at[2], (dp_at(k), t)).start(), 1)

    def vec_total():
        arrived(vmail.at[1:], R.dp_r.at[2])
        sums[...] = vmail[0].astype(f32)

        def vec_add(n):
            sums[...] += vmail[n].astype(f32)

        loop(n_dp, vec_add, 1)
        R.vec_out[...] = sums[...]
        R.firsts_out[...] = firsts[...]

    def out_on():
        arrived(x1.at[:, 0], R.lo_r.at[0])
        cp(out.at[:, t2], out.at[:, t2], S_OUT, R.lo_r.at[1], core).start()

    extra = [lambda: gin1(blocks - 1)] + [lambda i=i: gin2(i) for i in range(blocks)] + [vec_total]
    extra += [lambda: None, out_on]
    for i in range(max(len(jobs2), len(late) - 2, len(extra))):
        for jobs in (late[2:], jobs2, extra):
            if i < len(jobs):
                jobs[i]()

    arrived(x1.at[:, 0:2], R.lo_r.at[1])
    arrived(send1, R.go_r.at[0])

    out_own.wait()
    sent(x1.at[0, 0:3], S_SHARE)
    sent(R.wf1.at[0:2], S_WCORE)
    sent(rb.at[0:2], S_WRING)
    sent(R.wf1.at[0:2], S_WON)
    sent(R.bias1.at[0:3], S_BIAS)
    sent(send1, S_CORE1)
    sent(send2, S_Y1)
    for kind in (S_X1, S_DF, S_DA, S_OUT):
        sent(x1.at[:, 0:3], kind)
    sent(x1.at[0, 0:3], S_FIRST)
    sent(dfl.at[0:3], S_PART)
    sent(mail.at[1:], S_MAIL)
    sent(vmail.at[1:], S_VEC)
    sent(tsum.at[0:3], S_TSUM)

    @pl.when(c == 0)
    def _():
        sent(back.at[1:], S_BACK)

    sent(rb, S_RING)
    sent(rb, S_GATHER)
    sent(send1, S_GCORE)
    pltpu.make_async_copy(rb.at[0, 0, 0:6], rb.at[0, 0, 0:6], R.ss.at[S_LOCAL]).wait()
    pltpu.make_async_copy(send1, send1, R.ss.at[S_GLOCAL]).wait()


def run_layer(n_dp, ins, dims):
    rows, width, slots, queries, local_width = dims
    blocks = rows // BLK
    heads = local_width // HEAD_DIM
    own = blocks * PIECE
    groups = n_dp // RING
    share = width // RING // 2
    dma = pltpu.SemaphoreType.DMA
    vm = pltpu.VMEM
    any_ = pl.BlockSpec(memory_space=pl.ANY)
    vmem = pl.BlockSpec(memory_space=pltpu.VMEM)
    smem = pl.BlockSpec(memory_space=pltpu.SMEM)
    ins_at = dict(
        hid_in=any_, mask=vmem, bucket=smem, positive=smem, wqkv_in=any_, qv_bias=vmem, wo_in=any_, ob=vmem, g1=vmem,
        n1b=vmem, w1=any_, b1=vmem, w2=any_, fb=vmem, g2=vmem, n2b=vmem, upstream=any_,
    )
    pieces = (blocks, 4, PIECE, width)
    pairs = (blocks, 2, PIECE, width)
    outs = dict(
        layer_out=(any_, pieces, bf16),
        grad_in=(any_, (blocks, 4, PIECE, width), bf16),
        o1=(any_, (width, width), bf16),
        o2=(any_, (width, width), bf16),
        o3=(any_, (width, width), bf16),
        vec_out=(vmem, (16, width), f32),
        firsts_out=(vmem, (4, 16, width), bf16),
    )
    scratch = dict(
        hid=vm((rows, width), bf16),
        wqkv=vm((3, local_width, width), bf16),
        wo=vm((local_width, width), bf16),
        wf1=vm((4, width, width), bf16),
        wf2=vm((4, width, width), bf16),
        up=vm((blocks, PIECE, width), bf16),
        bias1=vm((4, 8, width), f32),
        part=vm((BLK, width), f32),
        keep=vm(pairs, bf16),
        send1=vm(pairs, bf16),
        got1=vm(pairs, bf16),
        send2=vm(pairs, bf16),
        got2=vm(pairs, bf16),
        q=vm((rows, local_width), bf16),
        k=vm((rows, local_width), bf16),
        v=vm((rows, local_width), bf16),
        ctx=vm((rows, local_width), bf16),
        pb=vm((blocks, heads, BLK, BLK), bf16),
        x1=vm((blocks, 4, PIECE, width), bf16),
        x1f=vm((4, 16, width), bf16),
        dfl=vm((4, 16, width), bf16),
        dal=vm((4, 16, width), bf16),
        parts=vm((4, 16, width), bf16),
        parts_in=vm((4, 16, width), bf16),
        act_late=vm((64, width), bf16),
        du_late=vm((64, width), bf16),
        h1=vm((own, width), f32),
        n1=vm((own, width), f32),
        n2=vm((own, width), f32),
        rstd1=vm((own, 128), f32),
        rstd2=vm((own, 128), f32),
        act=vm((rows, width), bf16),
        slope=vm((rows, width), bf16),
        wide=vm((own, width), f32),
        slope_own=vm((4, own, width), bf16),
        low=vm((blocks, PIECE, width), bf16),
        firsts=vm((4, 16, width), bf16),
        stage=vm((16, width), f32),
        pack=vm((16, width // 2 + 128), f32),
        mail=vm((n_dp, 16, width // 2 + 128), bf16),
        qe=vm((32, width + 128), f32),
        pe=vm((n_dp * 8, width + 128), f32),
        dqe=vm((32, width), f32),
        dpe=vm((n_dp, 8, width), f32),
        back=vm((n_dp, 8, width), f32),
        sums=vm((16, width), f32),
        tsum=vm((4, 8, width), f32),
        vmail=vm((n_dp, 16, width), bf16),
        df=vm(pieces, bf16),
        da=vm(pieces, bf16),
        ga1=vm((width, width), bf16),
        ga2=vm((width, width), bf16),
        ga3=vm((width, width), bf16),
        rb=vm((3, 2, RING - 1, share, width), bf16),
        load_sem=dma((6,)),
        ss=dma((25,)),
        wc_r=dma((1,)), wy_r=dma((2,)), wf_r=dma((2,)), wr_r=dma((2, 7)), bi_r=dma((1,)),
        rc_r=dma((2, blocks)), ry_r=dma((2, blocks)),
        gy_r=dma((blocks,)), gc_r=dma((blocks,)),
        fy_r=dma((2,)), fc_r=dma((2,)), ay_r=dma((2,)), ac_r=dma((2,)),
        fi_r=dma((5,)), lo_r=dma((2,)), dp_r=dma((3,)), ts_r=dma((1,)),
        rr_r=dma((3, 7)), rg_r=dma((3, 7)), go_r=dma((1,)),
    )
    if groups > 1:
        n = 6 * (groups - 1)
        scratch.update(gb=vm((n, share, width), bf16), gr_s=dma((n,)), gr_r=dma((n,)))
    names = [*ins_at, *outs, *scratch]

    def kernel(*refs):
        layer_kernel(n_dp, dims, names, *refs)

    return pl.pallas_call(
        kernel,
        name="layer",
        out_shape=[jax.ShapeDtypeStruct(shape, kind) for _, shape, kind in outs.values()],
        in_specs=list(ins_at.values()),
        out_specs=[spec for spec, _, _ in outs.values()],
        scratch_shapes=list(scratch.values()),
        compiler_params=pltpu.CompilerParams(
            collective_id=0, has_side_effects=True, vmem_limit_bytes=64 * 2**20
        ),
    )(*[ins[n] for n in ins_at])


def run_finish(lout, gin, o1, o2, o3, sums, firsts, slots, queries, local_width, n_dp):
    rows, width = lout.shape
    steps = 3
    shapes = (
        ((rows, width), bf16), ((queries, width), bf16), ((2 * slots, width), bf16), ((1, 1), f32),
        ((rows, width), f32), ((3 * local_width, width), f32), ((2, local_width), f32), ((local_width, width), f32),
        ((width,), f32), ((width,), f32), ((width,), f32), ((width, width), f32), ((width,), f32),
        ((width, width), f32), ((width,), f32), ((width,), f32), ((width,), f32),
    )
    big = (0, 4, 5, 7, 11, 13)

    def whole(shape):
        return pl.BlockSpec(shape, lambda i: (0,) * len(shape))

    def cut(count, offset=0):
        return pl.BlockSpec((count // steps, width), lambda i: (i + offset, 0))

    def kernel(lout, gin, o1, o2, o3a, o3b, sums, firsts, *outs):
        outs[0][...] = lout[...]
        outs[4][...] = gin[...].astype(f32)
        outs[5][...] = o3a[...].astype(f32)
        outs[7][...] = o3b[...].astype(f32)
        outs[11][...] = o1[...].astype(f32)
        outs[13][...] = o2[...].astype(f32)

        @pl.when(pl.program_id(0) == 0)
        def _():
            tiles = [firsts[k].astype(f32) for k in range(4)]
            query = [tiles[q % 8 // 2][2 * (q // 8) + q % 2 : 2 * (q // 8) + q % 2 + 1] for q in range(queries)]
            outs[1][...] = jnp.concatenate(query, axis=0).astype(bf16)
            passage = [tiles[2 * (p % 2)][6 + p // 2 : 7 + p // 2] for p in range(2 * slots)]
            outs[2][...] = jnp.concatenate(passage, axis=0).astype(bf16)
            outs[3][...] = (sums[6:7, 0:1] + sums[7:8, 0:1]) * (1.0 / (queries * n_dp))
            outs[6][...] = sums[9:11, 0:local_width]
            for at, row in ((8, 5), (9, 3), (10, 4), (12, 8), (14, 2), (15, 0), (16, 1)):
                outs[at][...] = sums[row : row + 1].reshape(width)

    specs = [whole(shape) for shape, _ in shapes]
    for at in big:
        specs[at] = cut(shapes[at][0][0])
    return pl.pallas_call(
        kernel,
        name="finish",
        grid=(steps,),
        out_shape=[jax.ShapeDtypeStruct(shape, kind) for shape, kind in shapes],
        in_specs=[
            cut(rows), cut(rows), cut(width), cut(width), cut(3 * local_width),
            cut(local_width, 3 * local_width // (local_width // steps)), whole((16, width)), whole((4, 16, width)),
        ],
        out_specs=specs,
    )(lout, gin, o1, o2, o3, o3, sums, firsts)


def local(
    hidden_in, token_mask, bucket, positive, qkv_weight, qv_bias, out_weight, out_bias, norm1_gain, norm1_bias,
    ffn_in, ffn_in_bias, ffn_out, ffn_out_bias, norm2_gain, norm2_bias, upstream,
):
    rows, width = hidden_in.shape
    blocks = rows // BLK
    slots = bucket.shape[0]
    queries = positive.shape[0]
    local_width = qkv_weight.shape[2]
    n_dp = lax.axis_size("dp")
    ins = dict(
        hid_in=hidden_in, mask=token_mask, bucket=bucket, positive=positive, wqkv_in=qkv_weight.transpose(0, 2, 1),
        qv_bias=qv_bias, wo_in=out_weight, ob=out_bias, g1=norm1_gain, n1b=norm1_bias, w1=ffn_in, b1=ffn_in_bias,
        w2=ffn_out, fb=ffn_out_bias, g2=norm2_gain, n2b=norm2_bias,
        upstream=upstream.reshape(blocks, 4, PIECE, width),
    )
    lout, gin, o1, o2, o3, sums, firsts = run_layer(n_dp, ins, (rows, width, slots, queries, local_width))
    lout, gin = lout.reshape(rows, width), gin.reshape(rows, width)
    outs = run_finish(lout, gin, o1, o2, o3, sums, firsts, slots, queries, local_width, n_dp)
    lout, query, passage, loss, gin, qkv, qv, gout, gob, gg1, gn1b, gf1, gb1, gf2, gfb, gg2, gn2b = outs
    qkv = qkv.reshape(3, local_width, width).transpose(0, 2, 1)
    return (
        lout, query, passage, loss.reshape(()), gin, qkv, qv, gout, gob, gg1, gn1b, gf1, gb1, gf2, gfb, gg2, gn2b
    )


def solution(mesh):
    one, two = P("dp"), P("dp", None)
    col, row = P(None, "tensor"), P("tensor", None)
    return jax.shard_map(
        local,
        mesh=mesh,
        in_specs=(
            two, one, one, one, P(None, None, "tensor"), col, row, P(), P(), P(), col, P("tensor"), row, P(), P(), P(),
            two,
        ),
        out_specs=(
            two, two, two, P(), two, P(None, None, "tensor"), col, row, P(), P(), P(), col, P("tensor"), row, P(), P(),
            P(),
        ),
        check_vma=False,
    )
```

```python
import math
from types import SimpleNamespace

import jax
import jax.numpy as jnp
from jax import lax
from jax.experimental import pallas as pl
from jax.experimental.pallas import tpu as pltpu
from jax.sharding import PartitionSpec as P

f32 = jnp.float32
bf16 = jnp.bfloat16
MESH = pl.DeviceIdType.MESH

HEAD_DIM = 64
SLOT_LEN = 256
QRY_LEN = 32
NORM_EPS = 1e-12
BLK = 256
PIECE = 64
RING = 8
DEAD = -1e30


def dot(a, b):
    return lax.dot_general(a, b, (((1,), (0,)), ((), ())), preferred_element_type=f32)


def dot_t(a, b):
    return lax.dot_general(a, b, (((1,), (1,)), ((), ())), preferred_element_type=f32)


def dot_l(a, b):
    return lax.dot_general(a, b, (((0,), (0,)), ((), ())), preferred_element_type=f32)


def loop(n, body, lo=0):
    def step(i, carry):
        body(i)
        return carry

    lax.fori_loop(lo, n, step, 0)


def layer_kernel(n_dp, dims, names, *refs):
    R = SimpleNamespace(**dict(zip(names, refs)))
    rows, width, slots, queries, local_width = dims
    blocks = rows // BLK
    heads = local_width // HEAD_DIM
    groups = n_dp // RING
    cands = 8 * n_dp
    loss_scale = 2.0 / math.sqrt(width)
    quarter = width
    own = blocks * PIECE

    dp = lax.axis_index("dp")
    t = lax.axis_index("tensor")
    y = lax.div(t, 2)
    c = lax.rem(t, 2)
    t1 = 2 * y + (1 - c)
    t2 = 2 * (1 - y) + c
    t3 = 2 * (1 - y) + (1 - c)
    core = (dp, t1)
    ypeer = (dp, t2)
    mates = ((dp, t1), (dp, t2), (dp, t3))

    group = lax.div(dp, RING)
    place = lax.rem(dp, RING)

    def place_of(r):
        return jnp.where(r < 4, 2 * r, 2 * (7 - r) + 1)

    r = jnp.where(lax.rem(place, 2) == 0, lax.div(place, 2), 7 - lax.div(place, 2))
    ring_to = (
        (group * RING + place_of(lax.rem(r + 1, RING)), t),
        (group * RING + place_of(lax.rem(r + RING - 1, RING)), t),
    )

    def dp_at(k):
        return lax.rem(dp + k, n_dp)

    (S_SHARE, S_WCORE, S_WRING, S_WON, S_BIAS, S_CORE0, S_Y0, S_CORE1, S_Y1, S_X1, S_FIRST, S_DF, S_DA, S_OUT, S_MAIL,
     S_BACK, S_VEC, S_TSUM, S_RING, S_GATHER, S_LOCAL, S_GLOCAL, S_GCORE, S_OUTL, S_PART, S_VSHARE) = range(26)

    def cp(src, dst, kind, rsem, dev):
        return pltpu.make_async_remote_copy(
            src_ref=src, dst_ref=dst, send_sem=R.ss.at[kind], recv_sem=rsem, device_id=dev, device_id_type=MESH
        )

    def arrived(ref, rsem):
        cp(ref, ref, S_SHARE, rsem, core).wait_recv()

    def sent(ref, kind):
        cp(ref, ref, kind, R.wc_r.at[0], core).wait_send()

    loads = [
        pltpu.make_async_copy(R.wqkv_in, R.wqkv, R.load_sem.at[0]),
        pltpu.make_async_copy(R.hid_in, R.hid, R.load_sem.at[1]),
        pltpu.make_async_copy(R.wo_in, R.wo, R.load_sem.at[2]),
        pltpu.make_async_copy(R.w1, R.wf1.at[t], R.load_sem.at[3]),
        pltpu.make_async_copy(R.w2, R.wf2.at[t], R.load_sem.at[4]),
        pltpu.make_async_copy(R.upstream.at[:, t], R.up, R.load_sem.at[5]),
    ]
    for one in loads:
        one.start()

    barrier = pltpu.get_barrier_semaphore()
    for mate in mates:
        pl.semaphore_signal(barrier, inc=1, device_id=mate, device_id_type=MESH)

    def greet(k):
        pl.semaphore_signal(barrier, inc=1, device_id=(dp_at(k), t), device_id_type=MESH)

    loop(n_dp, greet, 1)
    pl.semaphore_wait(barrier, 3 + n_dp - 1)

    share = quarter // RING
    half = share // 2
    wfs = (R.wf1, R.wf2)
    wins = (R.w1, R.w2)
    rb = R.rb

    def unit(chunk, sub):
        return pl.ds(pl.multiple_of(chunk * share + sub * half, half), half)

    def from_here(d, s):
        return lax.rem(r - s + 2 * RING, RING) if d == 0 else lax.rem(r + s + 2 * RING, RING)

    def w_share(k):
        at = pl.ds(pl.multiple_of(r * share, share), share)
        return cp(wins[k].at[at], wfs[k].at[t, at], S_SHARE, R.wy_r.at[k], ypeer)

    def w_send(k, at, d, idx):
        ref = wfs[k].at[t2, at]
        cp(ref, ref, S_WRING, R.wr_r.at[k, idx], ring_to[d]).start()

    def w_on(k, at):
        ref = wfs[k].at[t2, at]
        cp(ref, ref, S_WON, R.wf_r.at[k], core).start()

    def w_start(k):
        at = pl.ds(pl.multiple_of(r * share, share), share)
        arrived(wfs[k].at[t2, at], R.wy_r.at[k])
        for d in range(2):
            w_send(k, unit(r, d), d, 0)
            w_send(k, unit(r, 1 - d), d, 4)
        w_on(k, at)

    def w_pass(k, s, lead):
        idx = s - 1 if lead else s + 3
        arrived(rb.at[0, :, 0], R.wr_r.at[k, idx])
        for d in range(2):
            at = unit(from_here(d, s), d if lead else 1 - d)
            if s < (4 if lead else 3):
                w_send(k, at, d, idx + 1)
            w_on(k, at)

    def w_jobs(k):
        return [lambda: w_start(k)] + [
            lambda s=s, lead=lead: w_pass(k, s, lead)
            for s, lead in ((1, True), (1, False), (2, True), (2, False), (3, True), (3, False), (4, True))
        ]

    wa, wb = w_jobs(0), w_jobs(1)

    for k in range(2):
        w_share(k).start()
    for k in range(2):
        cp(wins[k], wfs[k].at[t], S_WCORE, R.wc_r.at[0], core).start()
    R.bias1[t] = jnp.broadcast_to(R.b1[...].astype(f32).reshape(1, quarter), (8, quarter))
    for mate in mates:
        cp(R.bias1.at[t], R.bias1.at[t], S_BIAS, R.bi_r.at[0], mate).start()

    part = R.part
    keep, send1, got1, send2, got2 = R.keep, R.send1, R.got1, R.send2, R.got2

    def rs0(e, i):
        for yy in range(2):
            mine = pl.ds(pl.multiple_of((2 * yy + c) * PIECE, PIECE), PIECE)
            other = pl.ds(pl.multiple_of((2 * yy + 1 - c) * PIECE, PIECE), PIECE)
            keep[i, yy] = part[mine].astype(bf16)
            send1[i, yy] = part[other].astype(bf16)
        cp(send1.at[i], got1.at[i], (S_CORE0, S_CORE1)[e], R.rc_r.at[e, i], core).start()

    def rs1(i):
        arrived(got1.at[i], R.rc_r.at[0, i])
        send2[i, 0] = (keep[i, 1 - y].astype(f32) + got1[i, 1 - y].astype(f32)).astype(bf16)
        cp(send2.at[i, 0], got2.at[i, 0], S_Y0, R.ry_r.at[0, i], ypeer).start()

    def rs2(i):
        arrived(got2.at[i, 0], R.ry_r.at[0, i])
        return keep[i, y].astype(f32) + got1[i, y].astype(f32) + got2[i, 0].astype(f32)

    def ag0(mine, kind, ysem, csem):
        cp(mine, mine, kind, ysem, ypeer).start()
        cp(mine, mine, kind, csem, core).start()

    def ag1(theirs, kind, ysem, csem):
        arrived(theirs, ysem)
        cp(theirs, theirs, kind, csem, core).start()

    def ag2(first, second, csem):
        arrived(first, csem)

    hid, wqkv, wo = R.hid, R.wqkv, R.wo
    lane = lax.broadcasted_iota(jnp.int32, (1, local_width), 1)
    head_f = [jnp.where(lax.shift_right_logical(lane, 6) == h, 1.0, 0.0).astype(f32) for h in range(heads)]
    head_b = [m.astype(bf16) for m in head_f]
    q_bias = R.qv_bias[0:1].astype(f32)
    v_bias = R.qv_bias[1:2].astype(f32)
    head_scale = 1.0 / math.sqrt(HEAD_DIM)

    def allowed_of(i):
        row = lax.broadcasted_iota(jnp.int32, (BLK, 1), 0)
        col = lax.broadcasted_iota(jnp.int32, (1, BLK), 1)
        split = 1 - R.bucket[jnp.minimum(i, slots - 1)]
        is_query = jnp.where(i >= slots, 1, 0)

        def seg(at):
            in_query = lax.shift_right_logical(at, 5)
            in_slot = lax.shift_right_logical(at, 7) * split
            return in_query * is_query + in_slot * (1 - is_query)

        return (seg(row) == seg(col)) & (R.mask[blk(i)].reshape(1, BLK) == 1)

    def blk(i):
        return pl.ds(pl.multiple_of(i * BLK, BLK), BLK)

    def attend(i):
        h_in = hid[blk(i)]
        q = (dot_t(h_in, wqkv[0]) + q_bias).astype(bf16)
        k = dot_t(h_in, wqkv[1]).astype(bf16)
        v = (dot_t(h_in, wqkv[2]) + v_bias).astype(bf16)
        R.q[blk(i)] = q
        R.k[blk(i)] = k
        R.v[blk(i)] = v
        allowed = allowed_of(i)
        context = jnp.zeros((BLK, local_width), f32)
        for h in range(heads):
            s = jnp.where(allowed, dot_t(q * head_b[h], k) * head_scale, DEAD)
            e = jnp.exp(s - jnp.max(s, axis=-1, keepdims=True))
            p = (e / jnp.sum(e, axis=-1, keepdims=True)).astype(bf16)
            R.pb[i, h] = p
            context = context + dot(p, v) * head_f[h]
        low = context.astype(bf16)
        R.ctx[blk(i)] = low
        part[...] = dot(low, wo[...])

    def norm_fwd(v, gain, bias):
        centre = v - jnp.mean(v, axis=-1, keepdims=True)
        rstd = lax.rsqrt(jnp.mean(centre * centre, axis=-1, keepdims=True) + NORM_EPS)
        n = centre * rstd
        return n, rstd, n * gain + bias

    def norm_bwd(dy, n, rstd, gain):
        e = dy * gain
        return (e - jnp.mean(e, axis=-1, keepdims=True) - n * jnp.mean(e * n, axis=-1, keepdims=True)) * rstd

    def vec_of(ref):
        return ref[...].astype(f32).reshape(1, width)

    vec = SimpleNamespace(
        ob=vec_of(R.ob), g1=vec_of(R.g1), n1b=vec_of(R.n1b), fb=vec_of(R.fb), g2=vec_of(R.g2), n2b=vec_of(R.n2b)
    )
    first_at = [(slots + b) * PIECE + 32 * k for b in range(blocks - slots) for k in range(2)]
    first_at += [s * PIECE for s in range(slots)]

    def pick(ref):
        rows_of = [ref[at : at + 1] for at in first_at]
        return jnp.concatenate(rows_of + [jnp.zeros((16 - len(first_at), ref.shape[1]), f32)], axis=0)

    def pick_low(ref):
        rows_of = [ref[at : at + 16].astype(f32)[0:1] for at in first_at]
        return jnp.concatenate(rows_of + [jnp.zeros((16 - len(first_at), ref.shape[1]), f32)], axis=0)

    x1 = R.x1
    h1, n1, n2 = R.h1, R.n1, R.n2
    rstd1, rstd2 = R.rstd1, R.rstd2

    def own_rows(i):
        return pl.ds(pl.multiple_of(i * BLK + t * PIECE, PIECE), PIECE)

    def piece_at(i):
        return pl.ds(pl.multiple_of(i * PIECE, PIECE), PIECE)

    def first_norm(i):
        v = hid[own_rows(i)].astype(f32) + rs2(i) + vec.ob
        n, rstd, out = norm_fwd(v, vec.g1, vec.n1b)
        n1[piece_at(i)] = n
        rstd1[piece_at(i)] = jnp.broadcast_to(rstd, (PIECE, 128))
        h1[piece_at(i)] = out
        x1[i, t] = out.astype(bf16)
        ag0(x1.at[i, t], S_X1, R.gy_r.at[i], R.gc_r.at[i])

    def at_step(s, jobs):
        for i, job in jobs.items():
            pl.when(s == i)(job)

    def both(*jobs):
        def run():
            for job in jobs:
                job()

        return run

    def fwd_step(s):
        attend(s)
        rs0(0, s)

        @pl.when(s >= 1)
        def _():
            rs1(s - 1)

        at_step(s, {1: wa[0], 4: both(wa[1], wb[0]), 5: wa[2]})

    for one in loads[:3]:
        one.wait()
    loop(blocks, fwd_step)
    rs1(blocks - 1)

    wa[3]()

    def norm_step(s):
        first_norm(s)
        at_step(s, {0: wb[1], 1: wa[4], 2: both(wb[2], wa[5]), 3: wb[3], 4: both(wa[6], wb[4]), 5: wa[7]})

    loop(blocks, norm_step)
    x1f = R.x1f
    x1f[t] = pick(h1).astype(bf16)

    def tile_out(tiles, which):
        for mate in mates:
            cp(tiles.at[t], tiles.at[t], S_FIRST, R.fi_r.at[which], mate).start()

    tile_out(x1f, 1)

    for one in loads[3:]:
        one.wait()
    arrived(R.bias1.at[0:3], R.bi_r.at[0])
    arrived(R.wf1.at[0:2], R.wc_r.at[0])
    act, slope = R.act, R.slope

    def gelu(u):
        cdf = 0.5 * (1.0 + lax.erf(u * (1.0 / math.sqrt(2.0))))
        pdf = jnp.exp(-0.5 * u * u) * (1.0 / math.sqrt(2.0 * math.pi))
        return (u * cdf).astype(bf16), (cdf + u * pdf).astype(bf16)

    wide = R.wide
    act_own = R.da

    def nth(j):
        return jnp.where(j == 0, t, jnp.where(j == 1, t1, jnp.where(j == 2, t2, t3)))

    def own_in(j):
        q = nth(j)
        u = dot(x1[:, t].reshape(own, width), wfs[0][q]) + R.bias1[q, 0:1]
        a, sl = gelu(u)
        R.slope_own[q] = sl
        act_own[:, q] = a.reshape(blocks, PIECE, width)

    def own_out(j):
        q = nth(j)
        wide[...] += dot(act_own[:, q].reshape(own, width), wfs[1][q])

    def x1_on(i):
        ag1(x1.at[i, t2], S_X1, R.gy_r.at[i], R.gc_r.at[i])

    def quarter_fwd(i):
        arrived(x1.at[i, 0:2], R.gc_r.at[i])
        u = dot(x1[i].reshape(BLK, width), wfs[0][t]) + R.bias1[t, 0:1]
        a, sl = gelu(u)
        act[blk(i)] = a
        slope[blk(i)] = sl

    def own_step(s):
        own_in(s)
        at_step(
            s, {0: wb[5], 2: both(wb[6], lambda: arrived(R.wf1.at[0], R.wf_r.at[0]))}
        )

    loop(4, own_step)
    wide[...] = jnp.zeros((own, width), f32)

    def out_step(s):
        at_step(s, {2: wb[7], 3: lambda: arrived(R.wf2.at[0], R.wf_r.at[1])})
        own_out(s)

    loop(4, out_step)

    low_out = R.low

    def second_norm(j):
        at = pl.ds(pl.multiple_of(j * PIECE, PIECE), PIECE)
        n, rstd, out = norm_fwd(h1[at] + wide[at] + vec.fb, vec.g2, vec.n2b)
        n2[at] = n
        rstd2[at] = jnp.broadcast_to(rstd, (PIECE, 128))
        h1[at] = out
        low_out[j] = out.astype(bf16)

    loop(blocks, second_norm)

    firsts = R.firsts
    stage = R.stage
    stage[...] = jnp.zeros((16, width), f32)
    firsts[t] = pick(h1).astype(bf16)
    tile_out(firsts, 0)

    sums = R.sums
    sums[...] = jnp.zeros((16, width), f32)
    up, dv2, df, da = R.up, R.n2, R.df, R.da
    dv1 = R.h1
    dfl, dal = R.dfl, R.dal
    near = blocks // 2

    def colsum(v):
        return jnp.sum(v, axis=0, keepdims=True)

    tile_n1, tile_n2 = pick(n1), pick(n2)
    tile_r1, tile_r2 = pick(rstd1)[:, 0:1], pick(rstd2)[:, 0:1]
    tile_up = pick_low(up.reshape(own, width))

    def norm2_back(dy, n, rstd):
        sums[0:1] += colsum(dy * n)
        sums[1:2] += colsum(dy)
        dv = norm_bwd(dy, n, rstd, vec.g2)
        low = dv.astype(bf16)
        sums[2:3] += colsum(low.astype(f32))
        return dv, low

    def norm1_back(dy, n, rstd):
        sums[3:4] += colsum(dy * n)
        sums[4:5] += colsum(dy)
        dv = norm_bwd(dy, n, rstd, vec.g1)
        low = dv.astype(bf16)
        sums[5:6] += colsum(low.astype(f32))
        return dv, low

    def second_back(i):
        at = piece_at(i)
        row = lax.broadcasted_iota(jnp.int32, (PIECE, 1), 0)
        is_query = jnp.where(i >= slots, 1, 0)
        late = jnp.where(row == 0, jnp.maximum(is_query, 1 - c), jnp.where(row == 32, is_query, 0))
        dy = jnp.where(late == 0, up[i].astype(f32), 0.0)
        dv, low = norm2_back(dy, n2[at], rstd2[at][:, 0:1])
        dv2[at] = dv
        df[i, t] = low

    def halves(p):
        return pl.ds(p * near, near)

    for p in range(2):
        loop((p + 1) * near, second_back, p * near)
        ag0(df.at[halves(p), t], S_DF, R.fy_r.at[p], R.fc_r.at[p])
    wide[...] = dv2[...]

    def own_bwd(q):
        dg = dot_t(df[:, t].reshape(own, width), wfs[1][q])
        du = (dg * R.slope_own[q].astype(f32)).astype(bf16)
        wide[...] += dot_t(du, wfs[0][q])

    def first_back(i):
        at = piece_at(i)
        dv, low = norm1_back(wide[at], n1[at], rstd1[at][:, 0:1])
        dv1[at] = dv
        da[i, t] = low

    def df_on(p):
        ag1(df.at[halves(p), t2], S_DF, R.fy_r.at[p], R.fc_r.at[p])

    def da_on(p):
        ag1(da.at[halves(p), t2], S_DA, R.ay_r.at[p], R.ac_r.at[p])

    def here(full, p, sem):
        arrived(full.at[halves(p), 0:2], sem.at[p])

    du_all = slope

    def quarter_bwd(i):
        dg = dot_t(df[i].reshape(BLK, width), wfs[1][t])
        du = (dg * slope[blk(i)].astype(f32)).astype(bf16)
        sums[8:9] += colsum(du.astype(f32))
        du_all[blk(i)] = du

    loop(2, own_bwd)

    arrived(firsts.at[0:3], R.fi_r.at[0])
    hw = width // 2
    pack = R.pack
    pack[...] = jnp.zeros((16, hw + 128), f32)
    cand_rows = [firsts[0].astype(f32), firsts[2].astype(f32)]
    for k in range(2):
        pack[3 * k : 3 * k + 3, 0:hw] = cand_rows[k][6:9, 0:hw]
        pack[8 + 3 * k : 11 + 3 * k, 0:hw] = cand_rows[k][6:9, hw:width]
    for s in range(slots):
        pack[3 + s : 4 + s, hw : hw + 128] = jnp.zeros((1, 128), f32) + R.bucket[s].astype(f32)
    pack[6:8, hw : hw + 128] = jnp.ones((2, 128), f32)
    mail = R.mail
    mail[dp] = pack[...].astype(bf16)
    loop(n_dp, lambda k: cp(mail.at[dp], mail.at[dp], S_MAIL, R.dp_r.at[0], (dp_at(k), t)).start(), 1)

    qe = R.qe
    qe[...] = jnp.zeros(qe.shape, f32)
    for tt in range(4):
        qe[8 * tt : 8 * tt + 6, 0:width] = firsts[tt].astype(f32)[0:6]
    lane_e = lax.broadcasted_iota(jnp.int32, (32, 128), 1)
    qe[:, width : width + 128] = jnp.where(lane_e == 0, DEAD, 0.0)
    row_q = lax.broadcasted_iota(jnp.int32, (32, 1), 0)
    target_at = jnp.full((32, 1), -1, jnp.int32)
    for tt in range(4):
        for b in range(blocks - slots):
            for k in range(2):
                pos = R.positive[b * 8 + tt * 2 + k]
                slot = lax.div(pos, 2)
                at = lax.div(slot, slots) * 8 + lax.rem(pos, 2) * 3 + lax.rem(slot, slots)
                target_at = jnp.where(row_q == 8 * tt + 2 * b + k, at, target_at)

    loop(4, own_bwd, 2)
    loop(blocks, first_back)

    def da_out(p):
        ag0(da.at[halves(p), t], S_DA, R.ay_r.at[p], R.ac_r.at[p])

    arrived(mail.at[1:], R.dp_r.at[0])
    pe = R.pe

    def unpack(n):
        got = mail[n].astype(f32)
        at = pl.ds(pl.multiple_of(n * 8, 8), 8)
        pe[at, 0:hw] = got[0:8, 0:hw]
        pe[at, hw:width] = got[8:16, 0:hw]
        pe[at, width : width + 128] = got[0:8, hw : hw + 128]

    loop(n_dp, unpack)
    pe_low = pe[...].astype(bf16)
    qe_low = qe[...].astype(bf16)
    z = dot_t(qe_low, pe_low) * loss_scale
    peak = jnp.max(z, axis=1, keepdims=True)
    total = peak + jnp.log(jnp.sum(jnp.exp(z - peak), axis=1, keepdims=True))
    target = lax.broadcasted_iota(jnp.int32, (32, cands), 1) == target_at
    live = target_at >= 0
    picked = jnp.sum(jnp.where(target, z, 0.0), axis=1, keepdims=True)
    ce = jnp.where(live, total - picked, 0.0)
    loss = jnp.sum(ce, axis=0, keepdims=True)
    dz = jnp.where(live, jnp.exp(z - total) - jnp.where(target, 1.0, 0.0), 0.0).astype(bf16)
    dqe = R.dqe
    dqe[...] = dot(dz, pe_low[:, 0:width]) * loss_scale
    dpe = R.dpe
    dpe[...] = (dot_l(dz, qe_low[:, 0:width]) * loss_scale).reshape(n_dp, 8, width)
    back = R.back

    @pl.when(c == 0)
    def _():
        loop(n_dp, lambda k: cp(dpe.at[dp_at(k)], back.at[dp], S_BACK, R.dp_r.at[1], (dp_at(k), t)).start(), 1)

    back[dp] = dpe[dp]

    loop(blocks, x1_on)
    loop(blocks - 2, quarter_fwd)
    df_on(0)
    loop(blocks, quarter_fwd, blocks - 2)
    arrived(x1f.at[0:3], R.fi_r.at[1])
    x1_late = x1f[...].reshape(64, width)
    act_late, slope_late = gelu(dot(x1_late, wfs[0][t]) + R.bias1[t, 0:1])
    R.act_late[...] = act_late

    @pl.when(c == 0)
    def _():
        arrived(back.at[1:], R.dp_r.at[1])
        stage[0:8] = back[0]

        def add(n):
            stage[0:8] += back[n]

        loop(n_dp, add, 1)

    mine_q = dqe[pl.ds(pl.multiple_of(t * 8, 8), 8)]
    row_l = lax.broadcasted_iota(jnp.int32, (16, 1), 0)
    for s in range(slots):
        stage[8 + s : 9 + s] = jnp.where(y == 0, stage[s : s + 1], stage[3 + s : 4 + s])
    grad_late = jnp.concatenate([mine_q[0:6], stage[8 : 8 + slots], jnp.zeros((16 - 6 - slots, width), f32)], axis=0)
    is_late = (row_l < 6) | ((row_l < 6 + slots) & (c == 0))
    dv2_late, low = norm2_back(jnp.where(is_late, tile_up + grad_late, 0.0), tile_n2, tile_r2)
    dfl[t] = low
    tile_out(dfl, 2)
    da_out(0)

    grads = (R.ga1, R.ga2, R.ga3)
    outs = (R.o1, R.o2, R.o3)

    def to_owner(d, s):
        return from_here(1 - d, 4 - s)

    def ring_send(k, d, src, idx):
        cp(src, rb.at[k, d, idx], S_RING, R.rr_r.at[k, idx], ring_to[d]).start()

    def ring_start(k):
        for d in range(2):
            ring_send(k, d, grads[k].at[unit(to_owner(d, 0), d)], 0)
            ring_send(k, d, grads[k].at[unit(to_owner(d, 1), 1 - d)], 4)

    def ring_add(k, s, lead):
        idx = s - 1 if lead else s + 2
        arrived(rb.at[k, :, idx], R.rr_r.at[k, idx])
        for d in range(2):
            slot = rb.at[k, d, idx]
            mine = grads[k][unit(to_owner(d, s), d if lead else 1 - d)]
            slot[...] = (slot[...].astype(f32) + mine.astype(f32)).astype(bf16)
            ring_send(k, d, slot, idx + 1)

    def gather_send(k, d, src, at, idx):
        cp(src, outs[k].at[at], S_GATHER, R.rg_r.at[k, idx], ring_to[d]).start()

    def ring_turn(k):
        for idx in (3, 6):
            arrived(rb.at[k, :, idx], R.rr_r.at[k, idx])
        for a in range(2):
            mine = grads[k][unit(r, a)].astype(f32)
            rb[k, a, 3] = (rb[k, a, 3].astype(f32) + rb[k, 1 - a, 6].astype(f32) + mine).astype(bf16)
        if groups > 1:

            def swap(a, g):
                at = (k * 2 + a) * (groups - 1) + g - 1
                dev = (lax.rem(group + g, groups) * RING + place, t)
                return pltpu.make_async_remote_copy(
                    src_ref=rb.at[k, a, 3], dst_ref=R.gb.at[at], send_sem=R.gr_s.at[at], recv_sem=R.gr_r.at[at],
                    device_id=dev, device_id_type=MESH,
                )

            both = [(a, g) for a in range(2) for g in range(1, groups)]
            for a, g in both:
                swap(a, g).start()
            for a, g in both:
                swap(a, g).wait()
            for a in range(2):
                tot = rb[k, a, 3].astype(f32)
                for g in range(1, groups):
                    tot = tot + R.gb[(k * 2 + a) * (groups - 1) + g - 1].astype(f32)
                rb[k, a, 3] = tot.astype(bf16)
        for d in range(2):
            gather_send(k, d, rb.at[k, d, 3], unit(r, d), 0)
            gather_send(k, d, rb.at[k, 1 - d, 3], unit(r, 1 - d), 4)
        for a in range(2):
            pltpu.make_async_copy(rb.at[k, a, 3], outs[k].at[unit(r, a)], R.ss.at[S_LOCAL]).start()

    def gather_on(k, s, lead):
        idx = s - 1 if lead else s + 3
        arrived(rb.at[k, :, 0], R.rg_r.at[k, idx])
        if s < (4 if lead else 3):
            for d in range(2):
                at = unit(from_here(d, s), d if lead else 1 - d)
                gather_send(k, d, outs[k].at[at], at, idx + 1)

    def ring_jobs(k):
        return [
            lambda: ring_add(k, 1, True), lambda: ring_add(k, 2, False), lambda: ring_add(k, 2, True),
            lambda: ring_add(k, 3, False), lambda: ring_add(k, 3, True), lambda: ring_turn(k),
            lambda: gather_on(k, 1, True), lambda: gather_on(k, 1, False), lambda: gather_on(k, 2, True),
            lambda: gather_on(k, 2, False), lambda: gather_on(k, 3, True), lambda: gather_on(k, 3, False),
            lambda: gather_on(k, 4, True),
        ]

    half_rows = rows // 2

    def flat(full, p):
        return full[halves(p)].reshape(half_rows, width)

    def rows_of(p):
        return pl.ds(p * half_rows, half_rows)

    def grad2(p):
        def one(j):
            at = pl.ds(pl.multiple_of(j * BLK, BLK), BLK)
            new = dot_l(act[rows_of(p), at], flat(df, p))
            if p == 1:
                new = new + grads[1][at].astype(f32) + dot_l(R.act_late[:, at], dfl[...].reshape(64, width))
            grads[1][at] = new.astype(bf16)

        loop(quarter // BLK, one)

    def grad1(p):
        def one(j):
            at = pl.ds(pl.multiple_of(j * BLK, BLK), BLK)
            new = dot_l(flat(x1, p), du_all[rows_of(p), at])
            if p == 1:
                new = new + grads[0][:, at].astype(f32) + dot_l(x1f[...].reshape(64, width), R.du_late[:, at])
            grads[0][:, at] = new.astype(bf16)

        loop(quarter // BLK, one)

    here(df, 0, R.fc_r)
    grad2(0)
    df_on(1)
    loop(near, quarter_bwd)
    arrived(dfl.at[0:3], R.fi_r.at[2])
    here(df, 1, R.fc_r)
    grad2(1)
    ring_start(1)

    dg_late = dot_t(dfl[...].reshape(64, width), wfs[1][t])
    du_late = (dg_late * slope_late.astype(f32)).astype(bf16)
    sums[8:9] += colsum(du_late.astype(f32))
    R.du_late[...] = du_late
    parts = R.parts
    parts[...] = dot_t(du_late, wfs[0][t]).astype(bf16).reshape(4, 16, width)
    for tt, mate in zip((t1, t2, t3), mates):
        cp(parts.at[tt], R.parts_in.at[t], S_PART, R.fi_r.at[4], mate).start()
    loop(blocks, quarter_bwd, near)
    jobs1, jobs0, jobs2 = ring_jobs(1), ring_jobs(0), ring_jobs(2)
    grad1(0)
    jobs1[0]()
    da_on(0)
    arrived(dfl.at[0:3], R.fi_r.at[4])
    late_sum = dv2_late + parts[t].astype(f32)
    for tt in (t1, t2, t3):
        late_sum = late_sum + R.parts_in[tt].astype(f32)
    dv1_late, low = norm1_back(jnp.where(is_late, late_sum, 0.0), tile_n1, tile_r1)
    for j, at in enumerate(first_at):
        dv1[at : at + 1] += dv1_late[j : j + 1]
    dal[t] = low
    tile_out(dal, 3)
    da_out(1)
    sums[6:7] = jnp.where(t == 0, loss, 0.0) + jnp.zeros((1, width), f32)
    tsum = R.tsum
    tsum[t] = sums[0:8]
    for mate in mates:
        cp(tsum.at[t], tsum.at[t], S_TSUM, R.ts_r.at[0], mate).start()
    grad1(1)
    ring_start(0)
    jobs1[1]()
    jobs1[2]()
    arrived(dal.at[0:3], R.fi_r.at[3])
    here(da, 0, R.ac_r)

    dq_all, dk_all, dv_all = R.q, R.k, R.v

    def attend_back(i):
        da_i = da_all[blk(i)]
        dc = dot_t(da_i, wo[...]).astype(bf16)
        q = R.q[blk(i)]
        k = R.k[blk(i)]
        v = R.v[blk(i)]
        dq = jnp.zeros((BLK, local_width), f32)
        dk = jnp.zeros((BLK, local_width), f32)
        dv = jnp.zeros((BLK, local_width), f32)
        for h in range(heads):
            dch = dc * head_b[h]
            p = R.pb[i, h]
            pf = p.astype(f32)
            dp_h = dot_t(dch, v)
            ds = (pf * (dp_h - jnp.sum(pf * dp_h, axis=-1, keepdims=True))).astype(bf16)
            dq = dq + dot(ds, k) * head_f[h]
            dk = dk + dot_l(ds, q * head_b[h])
            dv = dv + dot_l(p, dch)
        dq = (dq * head_scale).astype(bf16)
        dk = (dk * head_scale).astype(bf16)
        dv = dv.astype(bf16)
        dq_all[blk(i)] = dq
        dk_all[blk(i)] = dk
        dv_all[blk(i)] = dv
        sums[9:10, 0:local_width] += colsum(dq.astype(f32))
        sums[10:11, 0:local_width] += colsum(dv.astype(f32))
        part[...] = dot(dq, wqkv[0]) + dot(dk, wqkv[1]) + dot(dv, wqkv[2])

    gin = R.grad_in

    def gin1(i):
        arrived(got1.at[i], R.rc_r.at[1, i])
        mine = dv1[piece_at(i)]
        for yy in range(2):
            has = jnp.where(y == yy, 1.0, 0.0).astype(f32)
            send2[i, yy] = (keep[i, yy].astype(f32) + got1[i, yy].astype(f32) + mine * has).astype(bf16)
        cp(send2.at[i], got2.at[i], S_Y1, R.ry_r.at[1, i], ypeer).start()

    def gin2(i):
        arrived(got2.at[i], R.ry_r.at[1, i])
        for yy in range(2):
            got2[i, yy] = (send2[i, yy].astype(f32) + got2[i, yy].astype(f32)).astype(bf16)
            dst = gin.at[i, 2 * yy + c]
            pltpu.make_async_copy(got2.at[i, yy], dst, R.ss.at[S_GLOCAL]).start()
            cp(got2.at[i, yy], dst, S_GCORE, R.go_r.at[0], core).start()

    sent(send1, S_CORE0)
    sent(send2.at[:, 0], S_Y0)
    tile_row = lax.broadcasted_iota(jnp.int32, (16, 1), 0)
    da_all = act

    def late_rows(i):
        da_all[blk(i)] = da[i].reshape(BLK, width)
        for tt in range(4):
            tile = dal[tt].astype(f32)
            for k in range(2):
                row = jnp.where(i >= slots, 0.0, tile[6:7]) if k == 0 else jnp.zeros((1, width), f32)
                for b in range(blocks - slots):
                    row = row + jnp.where(i == slots + b, tile[2 * b + k : 2 * b + k + 1], 0.0)
                if k == 0:
                    for s in range(1, slots):
                        row = jnp.where(i == s, tile[6 + s : 7 + s], row)
                at = pl.ds(pl.multiple_of(i * BLK + tt * PIECE + 32 * k, 16), 16)
                old = da_all[at].astype(f32)
                da_all[at] = (old + jnp.where(tile_row == 0, row, 0.0)).astype(bf16)

    def back_step(s):
        at_step(s, {2: lambda: da_on(1), 3: lambda: here(da, 1, R.ac_r)})
        late_rows(s)
        attend_back(s)
        rs0(1, s)

        @pl.when(s >= 1)
        def _():
            gin1(s - 1)

        at_step(s, {1: both(jobs1[3]), 2: both(jobs1[4]), 3: both(jobs1[5]), 4: both(jobs1[6]), 5: both(jobs1[7])})
        at_step(s, {1: both(jobs0[0]), 2: both(jobs0[1]), 3: both(jobs0[2]), 4: both(jobs0[3]), 5: both(jobs0[4])})

    loop(blocks, back_step)

    out = R.layer_out
    out_own = pltpu.make_async_copy(low_out, out.at[:, t], R.ss.at[S_OUTL])
    out_own.start()
    cp(low_out, out.at[:, t], S_OUT, R.lo_r.at[0], ypeer).start()
    cp(low_out, out.at[:, t], S_OUT, R.lo_r.at[1], core).start()

    late1, late0 = jobs1[8:], jobs0[5:]
    late = [job for pair in zip(late0, late1) for job in pair] + late0[len(late1) :]
    grads[2][0:local_width] = dot_l(dq_all[...], hid[...]).astype(bf16)
    grads[2][local_width : 2 * local_width] = dot_l(dk_all[...], hid[...]).astype(bf16)
    grads[2][2 * local_width : 3 * local_width] = dot_l(dv_all[...], hid[...]).astype(bf16)
    grads[2][3 * local_width : 4 * local_width] = dot_l(R.ctx[...], da_all[...]).astype(bf16)
    ring_start(2)

    arrived(tsum.at[0:3], R.ts_r.at[0])
    sums[0:8] = tsum[0] + tsum[1] + tsum[2] + tsum[3]
    loss_low = sums[6:7].astype(bf16).astype(f32)
    sums[7:8] = sums[6:7] - loss_low
    vmail = R.vmail
    vpack = R.vpack
    third = width // 3
    vpack[...] = jnp.zeros((16, third), f32)
    for j in range(2):
        row = jnp.zeros((1, width), f32)
        for tt in range(4):
            row = row + jnp.where(t == tt, sums[2 * tt + j : 2 * tt + j + 1], 0.0)
        for p in range(3):
            vpack[3 * j + p : 3 * j + p + 1] = row[:, p * third : (p + 1) * third]
    for p in range(3):
        vpack[6 + p : 7 + p] = sums[8:9, p * third : (p + 1) * third]
    vpack[9:11] = sums[9:11, 0:third]
    vmail[dp] = vpack[...].astype(bf16)
    loop(n_dp, lambda k: cp(vmail.at[dp], vmail.at[dp], S_VEC, R.dp_r.at[2], (dp_at(k), t)).start(), 1)

    def vec_total():
        arrived(vmail.at[1:], R.dp_r.at[2])
        vpack[...] = vmail[0].astype(f32)

        def vec_add(n):
            vpack[...] += vmail[n].astype(f32)

        loop(n_dp, vec_add, 1)
        R.vshare[t] = vpack[0:8]
        for mate in mates:
            cp(R.vshare.at[t], R.vshare.at[t], S_VSHARE, R.vs_r.at[0], mate).start()

    def vec_out():
        arrived(R.vshare.at[0:3], R.vs_r.at[0])
        R.vec_out[...] = jnp.zeros((16, width), f32)
        for p in range(3):
            at = slice(p * third, (p + 1) * third)
            for tt in range(4):
                for j in range(2):
                    R.vec_out[2 * tt + j : 2 * tt + j + 1, at] = R.vshare[tt, 3 * j + p : 3 * j + p + 1]
            R.vec_out[8:9, at] = vpack[6 + p : 7 + p]
        R.vec_out[9:11, 0:third] = vpack[9:11]
        R.firsts_out[...] = firsts[...]

    def out_on():
        arrived(x1.at[:, 0], R.lo_r.at[0])
        cp(out.at[:, t2], out.at[:, t2], S_OUT, R.lo_r.at[1], core).start()

    extra = [lambda: gin1(blocks - 1)] + [lambda i=i: gin2(i) for i in range(blocks)] + [vec_total]
    extra += [lambda: None, out_on, vec_out]
    for i in range(max(len(jobs2), len(late), len(extra))):
        for jobs in (late, jobs2, extra):
            if i < len(jobs):
                jobs[i]()

    arrived(x1.at[:, 0:2], R.lo_r.at[1])
    arrived(send1, R.go_r.at[0])

    out_own.wait()
    sent(x1.at[0, 0:3], S_SHARE)
    sent(R.wf1.at[0:2], S_WCORE)
    sent(rb.at[0:2], S_WRING)
    sent(R.wf1.at[0:2], S_WON)
    sent(R.bias1.at[0:3], S_BIAS)
    sent(send1, S_CORE1)
    sent(send2, S_Y1)
    for kind in (S_X1, S_DF, S_DA, S_OUT):
        sent(x1.at[:, 0:3], kind)
    sent(x1.at[0, 0:3], S_FIRST)
    sent(dfl.at[0:3], S_PART)
    sent(mail.at[1:], S_MAIL)
    sent(vmail.at[1:], S_VEC)
    sent(R.vshare.at[0:3], S_VSHARE)
    sent(tsum.at[0:3], S_TSUM)

    @pl.when(c == 0)
    def _():
        sent(back.at[1:], S_BACK)

    sent(rb, S_RING)
    sent(rb, S_GATHER)
    sent(send1, S_GCORE)
    pltpu.make_async_copy(rb.at[0, 0, 0:6], rb.at[0, 0, 0:6], R.ss.at[S_LOCAL]).wait()
    pltpu.make_async_copy(send1, send1, R.ss.at[S_GLOCAL]).wait()


def run_layer(n_dp, ins, dims):
    rows, width, slots, queries, local_width = dims
    blocks = rows // BLK
    heads = local_width // HEAD_DIM
    own = blocks * PIECE
    groups = n_dp // RING
    share = width // RING // 2
    dma = pltpu.SemaphoreType.DMA
    vm = pltpu.VMEM
    any_ = pl.BlockSpec(memory_space=pl.ANY)
    vmem = pl.BlockSpec(memory_space=pltpu.VMEM)
    smem = pl.BlockSpec(memory_space=pltpu.SMEM)
    ins_at = dict(
        hid_in=any_, mask=vmem, bucket=smem, positive=smem, wqkv_in=any_, qv_bias=vmem, wo_in=any_, ob=vmem, g1=vmem,
        n1b=vmem, w1=any_, b1=vmem, w2=any_, fb=vmem, g2=vmem, n2b=vmem, upstream=any_,
    )
    pieces = (blocks, 4, PIECE, width)
    pairs = (blocks, 2, PIECE, width)
    outs = dict(
        layer_out=(any_, pieces, bf16),
        grad_in=(any_, (blocks, 4, PIECE, width), bf16),
        o1=(any_, (width, width), bf16),
        o2=(any_, (width, width), bf16),
        o3=(any_, (width, width), bf16),
        vec_out=(vmem, (16, width), f32),
        firsts_out=(vmem, (4, 16, width), bf16),
    )
    scratch = dict(
        hid=vm((rows, width), bf16),
        wqkv=vm((3, local_width, width), bf16),
        wo=vm((local_width, width), bf16),
        wf1=vm((4, width, width), bf16),
        wf2=vm((4, width, width), bf16),
        up=vm((blocks, PIECE, width), bf16),
        bias1=vm((4, 8, width), f32),
        part=vm((BLK, width), f32),
        keep=vm(pairs, bf16),
        send1=vm(pairs, bf16),
        got1=vm(pairs, bf16),
        send2=vm(pairs, bf16),
        got2=vm(pairs, bf16),
        q=vm((rows, local_width), bf16),
        k=vm((rows, local_width), bf16),
        v=vm((rows, local_width), bf16),
        ctx=vm((rows, local_width), bf16),
        pb=vm((blocks, heads, BLK, BLK), bf16),
        x1=vm((blocks, 4, PIECE, width), bf16),
        x1f=vm((4, 16, width), bf16),
        dfl=vm((4, 16, width), bf16),
        dal=vm((4, 16, width), bf16),
        parts=vm((4, 16, width), bf16),
        parts_in=vm((4, 16, width), bf16),
        act_late=vm((64, width), bf16),
        du_late=vm((64, width), bf16),
        h1=vm((own, width), f32),
        n1=vm((own, width), f32),
        n2=vm((own, width), f32),
        rstd1=vm((own, 128), f32),
        rstd2=vm((own, 128), f32),
        act=vm((rows, width), bf16),
        slope=vm((rows, width), bf16),
        wide=vm((own, width), f32),
        slope_own=vm((4, own, width), bf16),
        low=vm((blocks, PIECE, width), bf16),
        firsts=vm((4, 16, width), bf16),
        stage=vm((16, width), f32),
        pack=vm((16, width // 2 + 128), f32),
        mail=vm((n_dp, 16, width // 2 + 128), bf16),
        qe=vm((32, width + 128), f32),
        pe=vm((n_dp * 8, width + 128), f32),
        dqe=vm((32, width), f32),
        dpe=vm((n_dp, 8, width), f32),
        back=vm((n_dp, 8, width), f32),
        sums=vm((16, width), f32),
        tsum=vm((4, 8, width), f32),
        vmail=vm((n_dp, 16, width // 3), bf16),
        vpack=vm((16, width // 3), f32),
        vshare=vm((4, 8, width // 3), f32),
        df=vm(pieces, bf16),
        da=vm(pieces, bf16),
        ga1=vm((width, width), bf16),
        ga2=vm((width, width), bf16),
        ga3=vm((width, width), bf16),
        rb=vm((3, 2, RING - 1, share, width), bf16),
        load_sem=dma((6,)),
        ss=dma((26,)),
        wc_r=dma((1,)), wy_r=dma((2,)), wf_r=dma((2,)), wr_r=dma((2, 7)), bi_r=dma((1,)),
        rc_r=dma((2, blocks)), ry_r=dma((2, blocks)),
        gy_r=dma((blocks,)), gc_r=dma((blocks,)),
        fy_r=dma((2,)), fc_r=dma((2,)), ay_r=dma((2,)), ac_r=dma((2,)),
        fi_r=dma((5,)), vs_r=dma((1,)), lo_r=dma((2,)), dp_r=dma((3,)), ts_r=dma((1,)),
        rr_r=dma((3, 7)), rg_r=dma((3, 7)), go_r=dma((1,)),
    )
    if groups > 1:
        n = 6 * (groups - 1)
        scratch.update(gb=vm((n, share, width), bf16), gr_s=dma((n,)), gr_r=dma((n,)))
    names = [*ins_at, *outs, *scratch]

    def kernel(*refs):
        layer_kernel(n_dp, dims, names, *refs)

    return pl.pallas_call(
        kernel,
        name="layer",
        out_shape=[jax.ShapeDtypeStruct(shape, kind) for _, shape, kind in outs.values()],
        in_specs=list(ins_at.values()),
        out_specs=[spec for spec, _, _ in outs.values()],
        scratch_shapes=list(scratch.values()),
        compiler_params=pltpu.CompilerParams(
            collective_id=0, has_side_effects=True, vmem_limit_bytes=64 * 2**20
        ),
    )(*[ins[n] for n in ins_at])


def run_finish(lout, gin, o1, o2, o3, sums, firsts, slots, queries, local_width, n_dp):
    rows, width = lout.shape
    steps = 2
    shapes = (
        ((rows, width), bf16), ((queries, width), bf16), ((2 * slots, width), bf16), ((1, 1), f32),
        ((rows, width), f32), ((3 * local_width, width), f32), ((2, local_width), f32), ((local_width, width), f32),
        ((width,), f32), ((width,), f32), ((width,), f32), ((width, width), f32), ((width,), f32),
        ((width, width), f32), ((width,), f32), ((width,), f32), ((width,), f32),
    )
    big = (0, 4, 5, 7, 11, 13)

    def whole(shape):
        return pl.BlockSpec(shape, lambda i: (0,) * len(shape))

    def cut(count, offset=0):
        return pl.BlockSpec((count // steps, width), lambda i: (i + offset, 0))

    def kernel(lout, gin, o1, o2, o3a, o3b, sums, firsts, *outs):
        outs[0][...] = lout[...]
        outs[4][...] = gin[...].astype(f32)
        outs[5][...] = o3a[...].astype(f32)
        outs[7][...] = o3b[...].astype(f32)
        outs[11][...] = o1[...].astype(f32)
        outs[13][...] = o2[...].astype(f32)

        @pl.when(pl.program_id(0) == 0)
        def _():
            tiles = [firsts[k].astype(f32) for k in range(4)]
            query = [tiles[q % 8 // 2][2 * (q // 8) + q % 2 : 2 * (q // 8) + q % 2 + 1] for q in range(queries)]
            outs[1][...] = jnp.concatenate(query, axis=0).astype(bf16)
            passage = [tiles[2 * (p % 2)][6 + p // 2 : 7 + p // 2] for p in range(2 * slots)]
            outs[2][...] = jnp.concatenate(passage, axis=0).astype(bf16)
            outs[3][...] = (sums[6:7, 0:1] + sums[7:8, 0:1]) * (1.0 / (queries * n_dp))
            outs[6][...] = sums[9:11, 0:local_width]
            for at, row in ((8, 5), (9, 3), (10, 4), (12, 8), (14, 2), (15, 0), (16, 1)):
                outs[at][...] = sums[row : row + 1].reshape(width)

    specs = [whole(shape) for shape, _ in shapes]
    for at in big:
        specs[at] = cut(shapes[at][0][0])
    return pl.pallas_call(
        kernel,
        name="finish",
        grid=(steps,),
        out_shape=[jax.ShapeDtypeStruct(shape, kind) for shape, kind in shapes],
        in_specs=[
            cut(rows), cut(rows), cut(width), cut(width), cut(3 * local_width),
            cut(local_width, 3 * local_width // (local_width // steps)), whole((16, width)), whole((4, 16, width)),
        ],
        out_specs=specs,
    )(lout, gin, o1, o2, o3, o3, sums, firsts)


def local(
    hidden_in, token_mask, bucket, positive, qkv_weight, qv_bias, out_weight, out_bias, norm1_gain, norm1_bias,
    ffn_in, ffn_in_bias, ffn_out, ffn_out_bias, norm2_gain, norm2_bias, upstream,
):
    rows, width = hidden_in.shape
    blocks = rows // BLK
    slots = bucket.shape[0]
    queries = positive.shape[0]
    local_width = qkv_weight.shape[2]
    n_dp = lax.axis_size("dp")
    ins = dict(
        hid_in=hidden_in, mask=token_mask, bucket=bucket, positive=positive, wqkv_in=qkv_weight.transpose(0, 2, 1),
        qv_bias=qv_bias, wo_in=out_weight, ob=out_bias, g1=norm1_gain, n1b=norm1_bias, w1=ffn_in, b1=ffn_in_bias,
        w2=ffn_out, fb=ffn_out_bias, g2=norm2_gain, n2b=norm2_bias,
        upstream=upstream.reshape(blocks, 4, PIECE, width),
    )
    lout, gin, o1, o2, o3, sums, firsts = run_layer(n_dp, ins, (rows, width, slots, queries, local_width))
    lout, gin = lout.reshape(rows, width), gin.reshape(rows, width)
    outs = run_finish(lout, gin, o1, o2, o3, sums, firsts, slots, queries, local_width, n_dp)
    lout, query, passage, loss, gin, qkv, qv, gout, gob, gg1, gn1b, gf1, gb1, gf2, gfb, gg2, gn2b = outs
    qkv = qkv.reshape(3, local_width, width).transpose(0, 2, 1)
    return (
        lout, query, passage, loss.reshape(()), gin, qkv, qv, gout, gob, gg1, gn1b, gf1, gb1, gf2, gfb, gg2, gn2b
    )


def solution(mesh):
    one, two = P("dp"), P("dp", None)
    col, row = P(None, "tensor"), P("tensor", None)
    return jax.shard_map(
        local,
        mesh=mesh,
        in_specs=(
            two, one, one, one, P(None, None, "tensor"), col, row, P(), P(), P(), col, P("tensor"), row, P(), P(), P(),
            two,
        ),
        out_specs=(
            two, two, two, P(), two, P(None, None, "tensor"), col, row, P(), P(), P(), col, P("tensor"), row, P(), P(),
            P(),
        ),
        check_vma=False,
    )
```

```python
import math
from types import SimpleNamespace

import jax
import jax.numpy as jnp
from jax import lax
from jax.experimental import pallas as pl
from jax.experimental.pallas import tpu as pltpu
from jax.sharding import PartitionSpec as P

f32 = jnp.float32
bf16 = jnp.bfloat16
MESH = pl.DeviceIdType.MESH

HEAD_DIM = 64
SLOT_LEN = 256
QRY_LEN = 32
NORM_EPS = 1e-12
BLK = 256
PIECE = 64
RING = 8
DEAD = -1e30


def dot(a, b):
    return lax.dot_general(a, b, (((1,), (0,)), ((), ())), preferred_element_type=f32)


def dot_t(a, b):
    return lax.dot_general(a, b, (((1,), (1,)), ((), ())), preferred_element_type=f32)


def dot_l(a, b):
    return lax.dot_general(a, b, (((0,), (0,)), ((), ())), preferred_element_type=f32)


def loop(n, body, lo=0):
    def step(i, carry):
        body(i)
        return carry

    lax.fori_loop(lo, n, step, 0)


def layer_kernel(n_dp, dims, names, *refs):
    R = SimpleNamespace(**dict(zip(names, refs)))
    rows, width, slots, queries, local_width = dims
    blocks = rows // BLK
    heads = local_width // HEAD_DIM
    groups = n_dp // RING
    cands = 8 * n_dp
    loss_scale = 2.0 / math.sqrt(width)
    quarter = width
    own = blocks * PIECE

    dp = lax.axis_index("dp")
    t = lax.axis_index("tensor")
    y = lax.div(t, 2)
    c = lax.rem(t, 2)
    t1 = 2 * y + (1 - c)
    t2 = 2 * (1 - y) + c
    t3 = 2 * (1 - y) + (1 - c)
    core = (dp, t1)
    ypeer = (dp, t2)
    mates = ((dp, t1), (dp, t2), (dp, t3))

    group = lax.div(dp, RING)
    place = lax.rem(dp, RING)

    def place_of(r):
        return jnp.where(r < 4, 2 * r, 2 * (7 - r) + 1)

    r = jnp.where(lax.rem(place, 2) == 0, lax.div(place, 2), 7 - lax.div(place, 2))
    ring_to = (
        (group * RING + place_of(lax.rem(r + 1, RING)), t),
        (group * RING + place_of(lax.rem(r + RING - 1, RING)), t),
    )

    def dp_at(k):
        return lax.rem(dp + k, n_dp)

    (S_SHARE, S_WCORE, S_WRING, S_WON, S_BIAS, S_CORE0, S_Y0, S_CORE1, S_Y1, S_X1, S_FIRST, S_DF, S_DA, S_OUT, S_MAIL,
     S_BACK, S_VEC, S_TSUM, S_RING, S_GATHER, S_LOCAL, S_GLOCAL, S_GCORE, S_OUTL, S_PART, S_VSHARE) = range(26)

    def cp(src, dst, kind, rsem, dev):
        return pltpu.make_async_remote_copy(
            src_ref=src, dst_ref=dst, send_sem=R.ss.at[kind], recv_sem=rsem, device_id=dev, device_id_type=MESH
        )

    def arrived(ref, rsem):
        cp(ref, ref, S_SHARE, rsem, core).wait_recv()

    def sent(ref, kind):
        cp(ref, ref, kind, R.wc_r.at[0], core).wait_send()

    loads = [
        pltpu.make_async_copy(R.wqkv_in, R.wqkv, R.load_sem.at[0]),
        pltpu.make_async_copy(R.hid_in, R.hid, R.load_sem.at[1]),
        pltpu.make_async_copy(R.wo_in, R.wo, R.load_sem.at[2]),
        pltpu.make_async_copy(R.w1, R.wf1.at[t], R.load_sem.at[3]),
        pltpu.make_async_copy(R.w2, R.wf2.at[t], R.load_sem.at[4]),
        pltpu.make_async_copy(R.upstream.at[:, t], R.up, R.load_sem.at[5]),
    ]
    for one in loads:
        one.start()

    barrier = pltpu.get_barrier_semaphore()
    for mate in mates:
        pl.semaphore_signal(barrier, inc=1, device_id=mate, device_id_type=MESH)

    def greet(k):
        pl.semaphore_signal(barrier, inc=1, device_id=(dp_at(k), t), device_id_type=MESH)

    loop(n_dp, greet, 1)
    pl.semaphore_wait(barrier, 3 + n_dp - 1)

    share = quarter // RING
    half = share // 2
    wfs = (R.wf1, R.wf2)
    wins = (R.w1, R.w2)
    rb = R.rb

    def unit(chunk, sub):
        return pl.ds(pl.multiple_of(chunk * share + sub * half, half), half)

    def from_here(d, s):
        return lax.rem(r - s + 2 * RING, RING) if d == 0 else lax.rem(r + s + 2 * RING, RING)

    def w_share(k):
        at = pl.ds(pl.multiple_of(r * share, share), share)
        return cp(wins[k].at[at], wfs[k].at[t, at], S_SHARE, R.wy_r.at[k], ypeer)

    def w_send(k, at, d, idx):
        ref = wfs[k].at[t2, at]
        cp(ref, ref, S_WRING, R.wr_r.at[k, idx], ring_to[d]).start()

    def w_on(k, at):
        ref = wfs[k].at[t2, at]
        cp(ref, ref, S_WON, R.wf_r.at[k], core).start()

    def w_start(k):
        at = pl.ds(pl.multiple_of(r * share, share), share)
        arrived(wfs[k].at[t2, at], R.wy_r.at[k])
        for d in range(2):
            w_send(k, unit(r, d), d, 0)
            w_send(k, unit(r, 1 - d), d, 4)
        w_on(k, at)

    def w_pass(k, s, lead):
        idx = s - 1 if lead else s + 3
        arrived(rb.at[0, :, 0], R.wr_r.at[k, idx])
        for d in range(2):
            at = unit(from_here(d, s), d if lead else 1 - d)
            if s < (4 if lead else 3):
                w_send(k, at, d, idx + 1)
            w_on(k, at)

    def w_jobs(k):
        return [lambda: w_start(k)] + [
            lambda s=s, lead=lead: w_pass(k, s, lead)
            for s, lead in ((1, True), (1, False), (2, True), (2, False), (3, True), (3, False), (4, True))
        ]

    wa, wb = w_jobs(0), w_jobs(1)

    for k in range(2):
        w_share(k).start()
    for k in range(2):
        cp(wins[k], wfs[k].at[t], S_WCORE, R.wc_r.at[0], core).start()
    R.bias1[t] = jnp.broadcast_to(R.b1[...].astype(f32).reshape(1, quarter), (8, quarter))
    for mate in mates:
        cp(R.bias1.at[t], R.bias1.at[t], S_BIAS, R.bi_r.at[0], mate).start()

    part = R.part
    keep, send1, got1, send2, got2 = R.keep, R.send1, R.got1, R.send2, R.got2

    def rs0(e, i):
        for yy in range(2):
            mine = pl.ds(pl.multiple_of((2 * yy + c) * PIECE, PIECE), PIECE)
            other = pl.ds(pl.multiple_of((2 * yy + 1 - c) * PIECE, PIECE), PIECE)
            keep[i, yy] = part[mine].astype(bf16)
            send1[i, yy] = part[other].astype(bf16)
        cp(send1.at[i], got1.at[i], (S_CORE0, S_CORE1)[e], R.rc_r.at[e, i], core).start()

    def rs1(i):
        arrived(got1.at[i], R.rc_r.at[0, i])
        send2[i, 0] = (keep[i, 1 - y].astype(f32) + got1[i, 1 - y].astype(f32)).astype(bf16)
        cp(send2.at[i, 0], got2.at[i, 0], S_Y0, R.ry_r.at[0, i], ypeer).start()

    def rs2(i):
        arrived(got2.at[i, 0], R.ry_r.at[0, i])
        return keep[i, y].astype(f32) + got1[i, y].astype(f32) + got2[i, 0].astype(f32)

    def ag0(mine, kind, ysem, csem):
        cp(mine, mine, kind, ysem, ypeer).start()
        cp(mine, mine, kind, csem, core).start()

    def ag1(theirs, kind, ysem, csem):
        arrived(theirs, ysem)
        cp(theirs, theirs, kind, csem, core).start()

    def ag2(first, second, csem):
        arrived(first, csem)

    hid, wqkv, wo = R.hid, R.wqkv, R.wo
    lane = lax.broadcasted_iota(jnp.int32, (1, local_width), 1)
    head_f = [jnp.where(lax.shift_right_logical(lane, 6) == h, 1.0, 0.0).astype(f32) for h in range(heads)]
    head_b = [m.astype(bf16) for m in head_f]
    q_bias = R.qv_bias[0:1].astype(f32)
    v_bias = R.qv_bias[1:2].astype(f32)
    head_scale = 1.0 / math.sqrt(HEAD_DIM)

    def allowed_of(i):
        row = lax.broadcasted_iota(jnp.int32, (BLK, 1), 0)
        col = lax.broadcasted_iota(jnp.int32, (1, BLK), 1)
        split = 1 - R.bucket[jnp.minimum(i, slots - 1)]
        is_query = jnp.where(i >= slots, 1, 0)

        def seg(at):
            in_query = lax.shift_right_logical(at, 5)
            in_slot = lax.shift_right_logical(at, 7) * split
            return in_query * is_query + in_slot * (1 - is_query)

        return (seg(row) == seg(col)) & (R.mask[blk(i)].reshape(1, BLK) == 1)

    def blk(i):
        return pl.ds(pl.multiple_of(i * BLK, BLK), BLK)

    def attend(i):
        h_in = hid[blk(i)]
        q = (dot_t(h_in, wqkv[0]) + q_bias).astype(bf16)
        k = dot_t(h_in, wqkv[1]).astype(bf16)
        v = (dot_t(h_in, wqkv[2]) + v_bias).astype(bf16)
        R.q[blk(i)] = q
        R.k[blk(i)] = k
        R.v[blk(i)] = v
        allowed = allowed_of(i)
        context = jnp.zeros((BLK, local_width), f32)
        for h in range(heads):
            s = jnp.where(allowed, dot_t(q * head_b[h], k) * head_scale, DEAD)
            e = jnp.exp(s - jnp.max(s, axis=-1, keepdims=True))
            p = (e / jnp.sum(e, axis=-1, keepdims=True)).astype(bf16)
            R.pb[i, h] = p
            context = context + dot(p, v) * head_f[h]
        low = context.astype(bf16)
        R.ctx[blk(i)] = low
        part[...] = dot(low, wo[...])

    def norm_fwd(v, gain, bias):
        centre = v - jnp.mean(v, axis=-1, keepdims=True)
        rstd = lax.rsqrt(jnp.mean(centre * centre, axis=-1, keepdims=True) + NORM_EPS)
        n = centre * rstd
        return n, rstd, n * gain + bias

    def norm_bwd(dy, n, rstd, gain):
        e = dy * gain
        return (e - jnp.mean(e, axis=-1, keepdims=True) - n * jnp.mean(e * n, axis=-1, keepdims=True)) * rstd

    def vec_of(ref):
        return ref[...].astype(f32).reshape(1, width)

    vec = SimpleNamespace(
        ob=vec_of(R.ob), g1=vec_of(R.g1), n1b=vec_of(R.n1b), fb=vec_of(R.fb), g2=vec_of(R.g2), n2b=vec_of(R.n2b)
    )
    first_at = [(slots + b) * PIECE + 32 * k for b in range(blocks - slots) for k in range(2)]
    first_at += [s * PIECE for s in range(slots)]

    def pick(ref):
        rows_of = [ref[at : at + 1] for at in first_at]
        return jnp.concatenate(rows_of + [jnp.zeros((16 - len(first_at), ref.shape[1]), f32)], axis=0)

    def pick_low(ref):
        rows_of = [ref[at : at + 16].astype(f32)[0:1] for at in first_at]
        return jnp.concatenate(rows_of + [jnp.zeros((16 - len(first_at), ref.shape[1]), f32)], axis=0)

    x1 = R.x1
    h1, n1, n2 = R.h1, R.n1, R.n2
    rstd1, rstd2 = R.rstd1, R.rstd2

    def own_rows(i):
        return pl.ds(pl.multiple_of(i * BLK + t * PIECE, PIECE), PIECE)

    def piece_at(i):
        return pl.ds(pl.multiple_of(i * PIECE, PIECE), PIECE)

    def first_norm(i):
        v = hid[own_rows(i)].astype(f32) + rs2(i) + vec.ob
        n, rstd, out = norm_fwd(v, vec.g1, vec.n1b)
        n1[piece_at(i)] = n
        rstd1[piece_at(i)] = jnp.broadcast_to(rstd, (PIECE, 128))
        h1[piece_at(i)] = out
        x1[i, t] = out.astype(bf16)
        ag0(x1.at[i, t], S_X1, R.gy_r.at[i], R.gc_r.at[i])

    def at_step(s, jobs):
        for i, job in jobs.items():
            pl.when(s == i)(job)

    def both(*jobs):
        def run():
            for job in jobs:
                job()

        return run

    def fwd_step(s):
        attend(s)
        rs0(0, s)

        @pl.when(s >= 1)
        def _():
            rs1(s - 1)

        at_step(s, {1: wa[0], 4: both(wa[1], wb[0]), 5: wa[2]})

    for one in loads[:3]:
        one.wait()
    loop(blocks, fwd_step)
    rs1(blocks - 1)

    wa[3]()

    def norm_step(s):
        first_norm(s)
        at_step(s, {0: wb[1], 1: wa[4], 2: both(wb[2], wa[5]), 3: wb[3], 4: both(wa[6], wb[4]), 5: wa[7]})

    loop(blocks, norm_step)
    x1f = R.x1f
    x1f[t] = pick(h1).astype(bf16)

    def tile_out(tiles, which):
        for mate in mates:
            cp(tiles.at[t], tiles.at[t], S_FIRST, R.fi_r.at[which], mate).start()

    tile_out(x1f, 1)

    for one in loads[3:]:
        one.wait()
    arrived(R.bias1.at[0:3], R.bi_r.at[0])
    arrived(R.wf1.at[0:2], R.wc_r.at[0])
    act, slope = R.act, R.slope

    def gelu(u):
        cdf = 0.5 * (1.0 + lax.erf(u * (1.0 / math.sqrt(2.0))))
        pdf = jnp.exp(-0.5 * u * u) * (1.0 / math.sqrt(2.0 * math.pi))
        return (u * cdf).astype(bf16), (cdf + u * pdf).astype(bf16)

    wide = R.wide
    act_own = R.da

    def nth(j):
        return jnp.where(j == 0, t, jnp.where(j == 1, t1, jnp.where(j == 2, t2, t3)))

    def own_in(j):
        q = nth(j)
        u = dot(x1[:, t].reshape(own, width), wfs[0][q]) + R.bias1[q, 0:1]
        a, sl = gelu(u)
        R.slope_own[q] = sl
        act_own[:, q] = a.reshape(blocks, PIECE, width)

    def own_out(j):
        q = nth(j)
        wide[...] += dot(act_own[:, q].reshape(own, width), wfs[1][q])

    def x1_on(i):
        ag1(x1.at[i, t2], S_X1, R.gy_r.at[i], R.gc_r.at[i])

    def quarter_fwd(i):
        arrived(x1.at[i, 0:2], R.gc_r.at[i])
        u = dot(x1[i].reshape(BLK, width), wfs[0][t]) + R.bias1[t, 0:1]
        a, sl = gelu(u)
        act[blk(i)] = a
        slope[blk(i)] = sl

    def own_step(s):
        own_in(s)
        at_step(
            s, {0: wb[5], 2: both(wb[6], lambda: arrived(R.wf1.at[0], R.wf_r.at[0]))}
        )

    loop(4, own_step)
    wide[...] = jnp.zeros((own, width), f32)

    def out_step(s):
        at_step(s, {2: wb[7], 3: lambda: arrived(R.wf2.at[0], R.wf_r.at[1])})
        own_out(s)

    loop(4, out_step)

    low_out = R.low

    def second_norm(j):
        at = pl.ds(pl.multiple_of(j * PIECE, PIECE), PIECE)
        n, rstd, out = norm_fwd(h1[at] + wide[at] + vec.fb, vec.g2, vec.n2b)
        n2[at] = n
        rstd2[at] = jnp.broadcast_to(rstd, (PIECE, 128))
        h1[at] = out
        low_out[j] = out.astype(bf16)

    loop(blocks, second_norm)

    firsts = R.firsts
    stage = R.stage
    stage[...] = jnp.zeros((16, width), f32)
    firsts[t] = pick(h1).astype(bf16)
    tile_out(firsts, 0)

    sums = R.sums
    sums[...] = jnp.zeros((16, width), f32)
    up, dv2, df, da = R.up, R.n2, R.df, R.da
    dv1 = R.h1
    dfl, dal = R.dfl, R.dal
    near = blocks // 2

    def colsum(v):
        return jnp.sum(v, axis=0, keepdims=True)

    tile_n1, tile_n2 = pick(n1), pick(n2)
    tile_r1, tile_r2 = pick(rstd1)[:, 0:1], pick(rstd2)[:, 0:1]
    tile_up = pick_low(up.reshape(own, width))

    def norm2_back(dy, n, rstd):
        sums[0:1] += colsum(dy * n)
        sums[1:2] += colsum(dy)
        dv = norm_bwd(dy, n, rstd, vec.g2)
        low = dv.astype(bf16)
        sums[2:3] += colsum(low.astype(f32))
        return dv, low

    def norm1_back(dy, n, rstd):
        sums[3:4] += colsum(dy * n)
        sums[4:5] += colsum(dy)
        dv = norm_bwd(dy, n, rstd, vec.g1)
        low = dv.astype(bf16)
        sums[5:6] += colsum(low.astype(f32))
        return dv, low

    def second_back(i):
        at = piece_at(i)
        row = lax.broadcasted_iota(jnp.int32, (PIECE, 1), 0)
        is_query = jnp.where(i >= slots, 1, 0)
        late = jnp.where(row == 0, jnp.maximum(is_query, 1 - c), jnp.where(row == 32, is_query, 0))
        dy = jnp.where(late == 0, up[i].astype(f32), 0.0)
        dv, low = norm2_back(dy, n2[at], rstd2[at][:, 0:1])
        dv2[at] = dv
        df[i, t] = low

    def halves(p):
        return pl.ds(p * near, near)

    for p in range(2):
        loop((p + 1) * near, second_back, p * near)
        ag0(df.at[halves(p), t], S_DF, R.fy_r.at[p], R.fc_r.at[p])
    wide[...] = dv2[...]

    def own_bwd(q):
        dg = dot_t(df[:, t].reshape(own, width), wfs[1][q])
        du = (dg * R.slope_own[q].astype(f32)).astype(bf16)
        wide[...] += dot_t(du, wfs[0][q])

    def first_back(i):
        at = piece_at(i)
        dv, low = norm1_back(wide[at], n1[at], rstd1[at][:, 0:1])
        dv1[at] = dv
        da[i, t] = low

    def df_on(p):
        ag1(df.at[halves(p), t2], S_DF, R.fy_r.at[p], R.fc_r.at[p])

    def da_on(p):
        ag1(da.at[halves(p), t2], S_DA, R.ay_r.at[p], R.ac_r.at[p])

    def here(full, p, sem):
        arrived(full.at[halves(p), 0:2], sem.at[p])

    du_all = slope

    def quarter_bwd(i):
        dg = dot_t(df[i].reshape(BLK, width), wfs[1][t])
        du = (dg * slope[blk(i)].astype(f32)).astype(bf16)
        sums[8:9] += colsum(du.astype(f32))
        du_all[blk(i)] = du

    loop(2, own_bwd)

    arrived(firsts.at[0:3], R.fi_r.at[0])
    hw = width // 2
    pack = R.pack
    pack[...] = jnp.zeros((16, hw + 128), f32)
    cand_rows = [firsts[0].astype(f32), firsts[2].astype(f32)]
    for k in range(2):
        pack[3 * k : 3 * k + 3, 0:hw] = cand_rows[k][6:9, 0:hw]
        pack[8 + 3 * k : 11 + 3 * k, 0:hw] = cand_rows[k][6:9, hw:width]
    for s in range(slots):
        pack[3 + s : 4 + s, hw : hw + 128] = jnp.zeros((1, 128), f32) + R.bucket[s].astype(f32)
    pack[6:8, hw : hw + 128] = jnp.ones((2, 128), f32)
    mail = R.mail
    mail[dp] = pack[...].astype(bf16)
    loop(n_dp, lambda k: cp(mail.at[dp], mail.at[dp], S_MAIL, R.dp_r.at[0], (dp_at(k), t)).start(), 1)

    qe = R.qe
    qe[...] = jnp.zeros(qe.shape, f32)
    for tt in range(4):
        qe[8 * tt : 8 * tt + 6, 0:width] = firsts[tt].astype(f32)[0:6]
    lane_e = lax.broadcasted_iota(jnp.int32, (32, 128), 1)
    qe[:, width : width + 128] = jnp.where(lane_e == 0, DEAD, 0.0)
    row_q = lax.broadcasted_iota(jnp.int32, (32, 1), 0)
    target_at = jnp.full((32, 1), -1, jnp.int32)
    for tt in range(4):
        for b in range(blocks - slots):
            for k in range(2):
                pos = R.positive[b * 8 + tt * 2 + k]
                slot = lax.div(pos, 2)
                at = lax.div(slot, slots) * 8 + lax.rem(pos, 2) * 3 + lax.rem(slot, slots)
                target_at = jnp.where(row_q == 8 * tt + 2 * b + k, at, target_at)

    loop(4, own_bwd, 2)
    loop(blocks, first_back)

    def da_out(p):
        ag0(da.at[halves(p), t], S_DA, R.ay_r.at[p], R.ac_r.at[p])

    arrived(mail.at[1:], R.dp_r.at[0])
    pe = R.pe

    def unpack(n):
        got = mail[n].astype(f32)
        at = pl.ds(pl.multiple_of(n * 8, 8), 8)
        pe[at, 0:hw] = got[0:8, 0:hw]
        pe[at, hw:width] = got[8:16, 0:hw]
        pe[at, width : width + 128] = got[0:8, hw : hw + 128]

    loop(n_dp, unpack)
    pe_low = pe[...].astype(bf16)
    qe_low = qe[...].astype(bf16)
    z = dot_t(qe_low, pe_low) * loss_scale
    peak = jnp.max(z, axis=1, keepdims=True)
    total = peak + jnp.log(jnp.sum(jnp.exp(z - peak), axis=1, keepdims=True))
    target = lax.broadcasted_iota(jnp.int32, (32, cands), 1) == target_at
    live = target_at >= 0
    picked = jnp.sum(jnp.where(target, z, 0.0), axis=1, keepdims=True)
    ce = jnp.where(live, total - picked, 0.0)
    loss = jnp.sum(ce, axis=0, keepdims=True)
    dz = jnp.where(live, jnp.exp(z - total) - jnp.where(target, 1.0, 0.0), 0.0).astype(bf16)
    dqe = R.dqe
    dqe[...] = dot(dz, pe_low[:, 0:width]) * loss_scale
    dpe = R.dpe
    dpe[...] = (dot_l(dz, qe_low[:, 0:width]) * loss_scale).reshape(n_dp, 8, width)
    back = R.back

    @pl.when(c == 0)
    def _():
        loop(n_dp, lambda k: cp(dpe.at[dp_at(k)], back.at[dp], S_BACK, R.dp_r.at[1], (dp_at(k), t)).start(), 1)

    back[dp] = dpe[dp]

    loop(blocks, x1_on)
    loop(blocks - 2, quarter_fwd)
    df_on(0)
    loop(blocks, quarter_fwd, blocks - 2)
    arrived(x1f.at[0:3], R.fi_r.at[1])
    x1_late = x1f[...].reshape(64, width)
    act_late, slope_late = gelu(dot(x1_late, wfs[0][t]) + R.bias1[t, 0:1])
    R.act_late[...] = act_late

    @pl.when(c == 0)
    def _():
        arrived(back.at[1:], R.dp_r.at[1])
        stage[0:8] = back[0]

        def add(n):
            stage[0:8] += back[n]

        loop(n_dp, add, 1)

    mine_q = dqe[pl.ds(pl.multiple_of(t * 8, 8), 8)]
    row_l = lax.broadcasted_iota(jnp.int32, (16, 1), 0)
    for s in range(slots):
        stage[8 + s : 9 + s] = jnp.where(y == 0, stage[s : s + 1], stage[3 + s : 4 + s])
    grad_late = jnp.concatenate([mine_q[0:6], stage[8 : 8 + slots], jnp.zeros((16 - 6 - slots, width), f32)], axis=0)
    is_late = (row_l < 6) | ((row_l < 6 + slots) & (c == 0))
    dv2_late, low = norm2_back(jnp.where(is_late, tile_up + grad_late, 0.0), tile_n2, tile_r2)
    dfl[t] = low
    tile_out(dfl, 2)
    da_out(0)

    grads = (R.ga1, R.ga2, R.ga3)
    outs = (R.o1, R.o2, R.o3)

    def to_owner(d, s):
        return from_here(1 - d, 4 - s)

    def ring_send(k, d, src, idx):
        cp(src, rb.at[k, d, idx], S_RING, R.rr_r.at[k, idx], ring_to[d]).start()

    def ring_start(k):
        for d in range(2):
            ring_send(k, d, grads[k].at[unit(to_owner(d, 0), d)], 0)
            ring_send(k, d, grads[k].at[unit(to_owner(d, 1), 1 - d)], 4)

    def ring_add(k, s, lead):
        idx = s - 1 if lead else s + 2
        arrived(rb.at[k, :, idx], R.rr_r.at[k, idx])
        for d in range(2):
            slot = rb.at[k, d, idx]
            mine = grads[k][unit(to_owner(d, s), d if lead else 1 - d)]
            slot[...] = (slot[...].astype(f32) + mine.astype(f32)).astype(bf16)
            ring_send(k, d, slot, idx + 1)

    def gather_send(k, d, src, at, idx):
        cp(src, outs[k].at[at], S_GATHER, R.rg_r.at[k, idx], ring_to[d]).start()

    def ring_turn(k):
        for idx in (3, 6):
            arrived(rb.at[k, :, idx], R.rr_r.at[k, idx])
        for a in range(2):
            mine = grads[k][unit(r, a)].astype(f32)
            rb[k, a, 3] = (rb[k, a, 3].astype(f32) + rb[k, 1 - a, 6].astype(f32) + mine).astype(bf16)
        if groups > 1:

            def swap(a, g):
                at = (k * 2 + a) * (groups - 1) + g - 1
                dev = (lax.rem(group + g, groups) * RING + place, t)
                return pltpu.make_async_remote_copy(
                    src_ref=rb.at[k, a, 3], dst_ref=R.gb.at[at], send_sem=R.gr_s.at[at], recv_sem=R.gr_r.at[at],
                    device_id=dev, device_id_type=MESH,
                )

            both = [(a, g) for a in range(2) for g in range(1, groups)]
            for a, g in both:
                swap(a, g).start()
            for a, g in both:
                swap(a, g).wait()
            for a in range(2):
                tot = rb[k, a, 3].astype(f32)
                for g in range(1, groups):
                    tot = tot + R.gb[(k * 2 + a) * (groups - 1) + g - 1].astype(f32)
                rb[k, a, 3] = tot.astype(bf16)
        for d in range(2):
            gather_send(k, d, rb.at[k, d, 3], unit(r, d), 0)
            gather_send(k, d, rb.at[k, 1 - d, 3], unit(r, 1 - d), 4)
        for a in range(2):
            pltpu.make_async_copy(rb.at[k, a, 3], outs[k].at[unit(r, a)], R.ss.at[S_LOCAL]).start()

    def gather_on(k, s, lead):
        idx = s - 1 if lead else s + 3
        arrived(rb.at[k, :, 0], R.rg_r.at[k, idx])
        if s < (4 if lead else 3):
            for d in range(2):
                at = unit(from_here(d, s), d if lead else 1 - d)
                gather_send(k, d, outs[k].at[at], at, idx + 1)

    def ring_jobs(k):
        return [
            lambda: ring_add(k, 1, True), lambda: ring_add(k, 2, False), lambda: ring_add(k, 2, True),
            lambda: ring_add(k, 3, False), lambda: ring_add(k, 3, True), lambda: ring_turn(k),
            lambda: gather_on(k, 1, True), lambda: gather_on(k, 1, False), lambda: gather_on(k, 2, True),
            lambda: gather_on(k, 2, False), lambda: gather_on(k, 3, True), lambda: gather_on(k, 3, False),
            lambda: gather_on(k, 4, True),
        ]

    half_rows = rows // 2

    def flat(full, p):
        return full[halves(p)].reshape(half_rows, width)

    def rows_of(p):
        return pl.ds(p * half_rows, half_rows)

    def grad2(p):
        def one(j):
            at = pl.ds(pl.multiple_of(j * BLK, BLK), BLK)
            new = dot_l(act[rows_of(p), at], flat(df, p))
            if p == 1:
                new = new + grads[1][at].astype(f32) + dot_l(R.act_late[:, at], dfl[...].reshape(64, width))
            grads[1][at] = new.astype(bf16)

        loop(quarter // BLK, one)

    def grad1(p):
        def one(j):
            at = pl.ds(pl.multiple_of(j * BLK, BLK), BLK)
            new = dot_l(flat(x1, p), du_all[rows_of(p), at])
            if p == 1:
                new = new + grads[0][:, at].astype(f32) + dot_l(x1f[...].reshape(64, width), R.du_late[:, at])
            grads[0][:, at] = new.astype(bf16)

        loop(quarter // BLK, one)

    here(df, 0, R.fc_r)
    grad2(0)
    df_on(1)
    loop(near, quarter_bwd)
    arrived(dfl.at[0:3], R.fi_r.at[2])
    here(df, 1, R.fc_r)
    grad2(1)
    ring_start(1)

    dg_late = dot_t(dfl[...].reshape(64, width), wfs[1][t])
    du_late = (dg_late * slope_late.astype(f32)).astype(bf16)
    sums[8:9] += colsum(du_late.astype(f32))
    R.du_late[...] = du_late
    parts = R.parts
    parts[...] = dot_t(du_late, wfs[0][t]).astype(bf16).reshape(4, 16, width)
    for tt, mate in zip((t1, t2, t3), mates):
        cp(parts.at[tt], R.parts_in.at[t], S_PART, R.fi_r.at[4], mate).start()
    loop(blocks, quarter_bwd, near)
    jobs1, jobs0, jobs2 = ring_jobs(1), ring_jobs(0), ring_jobs(2)
    grad1(0)
    jobs1[0]()
    da_on(0)
    arrived(dfl.at[0:3], R.fi_r.at[4])
    late_sum = dv2_late + parts[t].astype(f32)
    for tt in (t1, t2, t3):
        late_sum = late_sum + R.parts_in[tt].astype(f32)
    dv1_late, low = norm1_back(jnp.where(is_late, late_sum, 0.0), tile_n1, tile_r1)
    for j, at in enumerate(first_at):
        dv1[at : at + 1] += dv1_late[j : j + 1]
    dal[t] = low
    tile_out(dal, 3)
    da_out(1)
    sums[6:7] = jnp.where(t == 0, loss, 0.0) + jnp.zeros((1, width), f32)
    tsum = R.tsum
    tsum[t] = sums[0:8]
    for mate in mates:
        cp(tsum.at[t], tsum.at[t], S_TSUM, R.ts_r.at[0], mate).start()
    grad1(1)
    ring_start(0)
    jobs1[1]()
    jobs1[2]()
    arrived(dal.at[0:3], R.fi_r.at[3])
    here(da, 0, R.ac_r)

    dq_all, dk_all, dv_all = R.q, R.k, R.v

    def attend_back(i):
        da_i = da_all[blk(i)]
        dc = dot_t(da_i, wo[...]).astype(bf16)
        q = R.q[blk(i)]
        k = R.k[blk(i)]
        v = R.v[blk(i)]
        dq = jnp.zeros((BLK, local_width), f32)
        dk = jnp.zeros((BLK, local_width), f32)
        dv = jnp.zeros((BLK, local_width), f32)
        for h in range(heads):
            dch = dc * head_b[h]
            p = R.pb[i, h]
            pf = p.astype(f32)
            dp_h = dot_t(dch, v)
            ds = (pf * (dp_h - jnp.sum(pf * dp_h, axis=-1, keepdims=True))).astype(bf16)
            dq = dq + dot(ds, k) * head_f[h]
            dk = dk + dot_l(ds, q * head_b[h])
            dv = dv + dot_l(p, dch)
        dq = (dq * head_scale).astype(bf16)
        dk = (dk * head_scale).astype(bf16)
        dv = dv.astype(bf16)
        dq_all[blk(i)] = dq
        dk_all[blk(i)] = dk
        dv_all[blk(i)] = dv
        sums[9:10, 0:local_width] += colsum(dq.astype(f32))
        sums[10:11, 0:local_width] += colsum(dv.astype(f32))
        part[...] = dot(dq, wqkv[0]) + dot(dk, wqkv[1]) + dot(dv, wqkv[2])

    gin = R.grad_in

    def gin1(i):
        arrived(got1.at[i], R.rc_r.at[1, i])
        mine = dv1[piece_at(i)]
        for yy in range(2):
            has = jnp.where(y == yy, 1.0, 0.0).astype(f32)
            send2[i, yy] = (keep[i, yy].astype(f32) + got1[i, yy].astype(f32) + mine * has).astype(bf16)
        cp(send2.at[i], got2.at[i], S_Y1, R.ry_r.at[1, i], ypeer).start()

    def gin2(i):
        arrived(got2.at[i], R.ry_r.at[1, i])
        for yy in range(2):
            got2[i, yy] = (send2[i, yy].astype(f32) + got2[i, yy].astype(f32)).astype(bf16)
            dst = gin.at[i, 2 * yy + c]
            pltpu.make_async_copy(got2.at[i, yy], dst, R.ss.at[S_GLOCAL]).start()
            cp(got2.at[i, yy], dst, S_GCORE, R.go_r.at[0], core).start()

    sent(send1, S_CORE0)
    sent(send2.at[:, 0], S_Y0)
    tile_row = lax.broadcasted_iota(jnp.int32, (16, 1), 0)
    da_all = act

    def late_rows(i):
        da_all[blk(i)] = da[i].reshape(BLK, width)
        for tt in range(4):
            tile = dal[tt].astype(f32)
            for k in range(2):
                row = jnp.where(i >= slots, 0.0, tile[6:7]) if k == 0 else jnp.zeros((1, width), f32)
                for b in range(blocks - slots):
                    row = row + jnp.where(i == slots + b, tile[2 * b + k : 2 * b + k + 1], 0.0)
                if k == 0:
                    for s in range(1, slots):
                        row = jnp.where(i == s, tile[6 + s : 7 + s], row)
                at = pl.ds(pl.multiple_of(i * BLK + tt * PIECE + 32 * k, 16), 16)
                old = da_all[at].astype(f32)
                da_all[at] = (old + jnp.where(tile_row == 0, row, 0.0)).astype(bf16)

    def back_step(s):
        at_step(s, {2: lambda: da_on(1), 3: lambda: here(da, 1, R.ac_r)})
        late_rows(s)
        attend_back(s)
        rs0(1, s)

        @pl.when(s >= 1)
        def _():
            gin1(s - 1)

        at_step(s, {1: both(jobs1[3]), 2: both(jobs1[4]), 3: both(jobs1[5]), 4: both(jobs1[6]), 5: both(jobs1[7])})
        at_step(s, {1: both(jobs0[0]), 2: both(jobs0[1]), 3: both(jobs0[2]), 4: both(jobs0[3]), 5: both(jobs0[4])})

    loop(blocks, back_step)

    out = R.layer_out
    out_own = pltpu.make_async_copy(low_out, out.at[:, t], R.ss.at[S_OUTL])
    out_own.start()
    cp(low_out, out.at[:, t], S_OUT, R.lo_r.at[0], ypeer).start()
    cp(low_out, out.at[:, t], S_OUT, R.lo_r.at[1], core).start()

    late1, late0 = jobs1[8:], jobs0[5:]
    late = [job for pair in zip(late0, late1) for job in pair] + late0[len(late1) :]
    grads[2][0:local_width] = dot_l(dq_all[...], hid[...]).astype(bf16)
    grads[2][local_width : 2 * local_width] = dot_l(dk_all[...], hid[...]).astype(bf16)
    grads[2][2 * local_width : 3 * local_width] = dot_l(dv_all[...], hid[...]).astype(bf16)
    grads[2][3 * local_width : 4 * local_width] = dot_l(R.ctx[...], da_all[...]).astype(bf16)
    ring_start(2)

    arrived(tsum.at[0:3], R.ts_r.at[0])
    sums[0:8] = tsum[0] + tsum[1] + tsum[2] + tsum[3]
    loss_low = sums[6:7].astype(bf16).astype(f32)
    sums[7:8] = sums[6:7] - loss_low
    vmail = R.vmail
    vpack = R.vpack
    third = width // 3
    vpack[...] = jnp.zeros((16, third), f32)
    for j in range(2):
        row = jnp.zeros((1, width), f32)
        for tt in range(4):
            row = row + jnp.where(t == tt, sums[2 * tt + j : 2 * tt + j + 1], 0.0)
        for p in range(3):
            vpack[3 * j + p : 3 * j + p + 1] = row[:, p * third : (p + 1) * third]
    for p in range(3):
        vpack[6 + p : 7 + p] = sums[8:9, p * third : (p + 1) * third]
    vpack[9:11] = sums[9:11, 0:third]
    vmail[dp] = vpack[...].astype(bf16)
    loop(n_dp, lambda k: cp(vmail.at[dp], vmail.at[dp], S_VEC, R.dp_r.at[2], (dp_at(k), t)).start(), 1)

    def vec_total():
        arrived(vmail.at[1:], R.dp_r.at[2])
        vpack[...] = vmail[0].astype(f32)

        def vec_add(n):
            vpack[...] += vmail[n].astype(f32)

        loop(n_dp, vec_add, 1)
        R.vshare[t] = vpack[0:8]
        for mate in mates:
            cp(R.vshare.at[t], R.vshare.at[t], S_VSHARE, R.vs_r.at[0], mate).start()

    def vec_out():
        arrived(R.vshare.at[0:3], R.vs_r.at[0])
        R.vec_out[...] = jnp.zeros((16, width), f32)
        for p in range(3):
            at = slice(p * third, (p + 1) * third)
            for tt in range(4):
                for j in range(2):
                    R.vec_out[2 * tt + j : 2 * tt + j + 1, at] = R.vshare[tt, 3 * j + p : 3 * j + p + 1]
            R.vec_out[8:9, at] = vpack[6 + p : 7 + p]
        R.vec_out[9:11, 0:third] = vpack[9:11]
        R.firsts_out[...] = firsts[...]

    def out_on():
        arrived(x1.at[:, 0], R.lo_r.at[0])
        cp(out.at[:, t2], out.at[:, t2], S_OUT, R.lo_r.at[1], core).start()

    extra = [lambda: gin1(blocks - 1)] + [lambda i=i: gin2(i) for i in range(blocks)] + [vec_total]
    extra += [lambda: None, out_on, vec_out]
    for i in range(max(len(jobs2), len(late), len(extra))):
        for jobs in (jobs2, late, extra):
            if i < len(jobs):
                jobs[i]()

    arrived(x1.at[:, 0:2], R.lo_r.at[1])
    arrived(send1, R.go_r.at[0])

    out_own.wait()
    sent(x1.at[0, 0:3], S_SHARE)
    sent(R.wf1.at[0:2], S_WCORE)
    sent(rb.at[0:2], S_WRING)
    sent(R.wf1.at[0:2], S_WON)
    sent(R.bias1.at[0:3], S_BIAS)
    sent(send1, S_CORE1)
    sent(send2, S_Y1)
    for kind in (S_X1, S_DF, S_DA, S_OUT):
        sent(x1.at[:, 0:3], kind)
    sent(x1.at[0, 0:3], S_FIRST)
    sent(dfl.at[0:3], S_PART)
    sent(mail.at[1:], S_MAIL)
    sent(vmail.at[1:], S_VEC)
    sent(R.vshare.at[0:3], S_VSHARE)
    sent(tsum.at[0:3], S_TSUM)

    @pl.when(c == 0)
    def _():
        sent(back.at[1:], S_BACK)

    sent(rb, S_RING)
    sent(rb, S_GATHER)
    sent(send1, S_GCORE)
    pltpu.make_async_copy(rb.at[0, 0, 0:6], rb.at[0, 0, 0:6], R.ss.at[S_LOCAL]).wait()
    pltpu.make_async_copy(send1, send1, R.ss.at[S_GLOCAL]).wait()


def run_layer(n_dp, ins, dims):
    rows, width, slots, queries, local_width = dims
    blocks = rows // BLK
    heads = local_width // HEAD_DIM
    own = blocks * PIECE
    groups = n_dp // RING
    share = width // RING // 2
    dma = pltpu.SemaphoreType.DMA
    vm = pltpu.VMEM
    any_ = pl.BlockSpec(memory_space=pl.ANY)
    vmem = pl.BlockSpec(memory_space=pltpu.VMEM)
    smem = pl.BlockSpec(memory_space=pltpu.SMEM)
    ins_at = dict(
        hid_in=any_, mask=vmem, bucket=smem, positive=smem, wqkv_in=any_, qv_bias=vmem, wo_in=any_, ob=vmem, g1=vmem,
        n1b=vmem, w1=any_, b1=vmem, w2=any_, fb=vmem, g2=vmem, n2b=vmem, upstream=any_,
    )
    pieces = (blocks, 4, PIECE, width)
    pairs = (blocks, 2, PIECE, width)
    outs = dict(
        layer_out=(any_, pieces, bf16),
        grad_in=(any_, (blocks, 4, PIECE, width), bf16),
        o1=(any_, (width, width), bf16),
        o2=(any_, (width, width), bf16),
        o3=(any_, (width, width), bf16),
        vec_out=(vmem, (16, width), f32),
        firsts_out=(vmem, (4, 16, width), bf16),
    )
    scratch = dict(
        hid=vm((rows, width), bf16),
        wqkv=vm((3, local_width, width), bf16),
        wo=vm((local_width, width), bf16),
        wf1=vm((4, width, width), bf16),
        wf2=vm((4, width, width), bf16),
        up=vm((blocks, PIECE, width), bf16),
        bias1=vm((4, 8, width), f32),
        part=vm((BLK, width), f32),
        keep=vm(pairs, bf16),
        send1=vm(pairs, bf16),
        got1=vm(pairs, bf16),
        send2=vm(pairs, bf16),
        got2=vm(pairs, bf16),
        q=vm((rows, local_width), bf16),
        k=vm((rows, local_width), bf16),
        v=vm((rows, local_width), bf16),
        ctx=vm((rows, local_width), bf16),
        pb=vm((blocks, heads, BLK, BLK), bf16),
        x1=vm((blocks, 4, PIECE, width), bf16),
        x1f=vm((4, 16, width), bf16),
        dfl=vm((4, 16, width), bf16),
        dal=vm((4, 16, width), bf16),
        parts=vm((4, 16, width), bf16),
        parts_in=vm((4, 16, width), bf16),
        act_late=vm((64, width), bf16),
        du_late=vm((64, width), bf16),
        h1=vm((own, width), f32),
        n1=vm((own, width), f32),
        n2=vm((own, width), f32),
        rstd1=vm((own, 128), f32),
        rstd2=vm((own, 128), f32),
        act=vm((rows, width), bf16),
        slope=vm((rows, width), bf16),
        wide=vm((own, width), f32),
        slope_own=vm((4, own, width), bf16),
        low=vm((blocks, PIECE, width), bf16),
        firsts=vm((4, 16, width), bf16),
        stage=vm((16, width), f32),
        pack=vm((16, width // 2 + 128), f32),
        mail=vm((n_dp, 16, width // 2 + 128), bf16),
        qe=vm((32, width + 128), f32),
        pe=vm((n_dp * 8, width + 128), f32),
        dqe=vm((32, width), f32),
        dpe=vm((n_dp, 8, width), f32),
        back=vm((n_dp, 8, width), f32),
        sums=vm((16, width), f32),
        tsum=vm((4, 8, width), f32),
        vmail=vm((n_dp, 16, width // 3), bf16),
        vpack=vm((16, width // 3), f32),
        vshare=vm((4, 8, width // 3), f32),
        df=vm(pieces, bf16),
        da=vm(pieces, bf16),
        ga1=vm((width, width), bf16),
        ga2=vm((width, width), bf16),
        ga3=vm((width, width), bf16),
        rb=vm((3, 2, RING - 1, share, width), bf16),
        load_sem=dma((6,)),
        ss=dma((26,)),
        wc_r=dma((1,)), wy_r=dma((2,)), wf_r=dma((2,)), wr_r=dma((2, 7)), bi_r=dma((1,)),
        rc_r=dma((2, blocks)), ry_r=dma((2, blocks)),
        gy_r=dma((blocks,)), gc_r=dma((blocks,)),
        fy_r=dma((2,)), fc_r=dma((2,)), ay_r=dma((2,)), ac_r=dma((2,)),
        fi_r=dma((5,)), vs_r=dma((1,)), lo_r=dma((2,)), dp_r=dma((3,)), ts_r=dma((1,)),
        rr_r=dma((3, 7)), rg_r=dma((3, 7)), go_r=dma((1,)),
    )
    if groups > 1:
        n = 6 * (groups - 1)
        scratch.update(gb=vm((n, share, width), bf16), gr_s=dma((n,)), gr_r=dma((n,)))
    names = [*ins_at, *outs, *scratch]

    def kernel(*refs):
        layer_kernel(n_dp, dims, names, *refs)

    return pl.pallas_call(
        kernel,
        name="layer",
        out_shape=[jax.ShapeDtypeStruct(shape, kind) for _, shape, kind in outs.values()],
        in_specs=list(ins_at.values()),
        out_specs=[spec for spec, _, _ in outs.values()],
        scratch_shapes=list(scratch.values()),
        compiler_params=pltpu.CompilerParams(
            collective_id=0, has_side_effects=True, vmem_limit_bytes=64 * 2**20
        ),
    )(*[ins[n] for n in ins_at])


def run_finish(lout, gin, o1, o2, o3, sums, firsts, slots, queries, local_width, n_dp):
    rows, width = lout.shape
    steps = 2
    shapes = (
        ((rows, width), bf16), ((queries, width), bf16), ((2 * slots, width), bf16), ((1, 1), f32),
        ((rows, width), f32), ((3 * local_width, width), f32), ((2, local_width), f32), ((local_width, width), f32),
        ((width,), f32), ((width,), f32), ((width,), f32), ((width, width), f32), ((width,), f32),
        ((width, width), f32), ((width,), f32), ((width,), f32), ((width,), f32),
    )
    big = (0, 4, 5, 7, 11, 13)

    def whole(shape):
        return pl.BlockSpec(shape, lambda i: (0,) * len(shape))

    def cut(count, offset=0):
        return pl.BlockSpec((count // steps, width), lambda i: (i + offset, 0))

    def kernel(lout, gin, o1, o2, o3a, o3b, sums, firsts, *outs):
        outs[0][...] = lout[...]
        outs[4][...] = gin[...].astype(f32)
        outs[5][...] = o3a[...].astype(f32)
        outs[7][...] = o3b[...].astype(f32)
        outs[11][...] = o1[...].astype(f32)
        outs[13][...] = o2[...].astype(f32)

        @pl.when(pl.program_id(0) == 0)
        def _():
            tiles = [firsts[k].astype(f32) for k in range(4)]
            query = [tiles[q % 8 // 2][2 * (q // 8) + q % 2 : 2 * (q // 8) + q % 2 + 1] for q in range(queries)]
            outs[1][...] = jnp.concatenate(query, axis=0).astype(bf16)
            passage = [tiles[2 * (p % 2)][6 + p // 2 : 7 + p // 2] for p in range(2 * slots)]
            outs[2][...] = jnp.concatenate(passage, axis=0).astype(bf16)
            outs[3][...] = (sums[6:7, 0:1] + sums[7:8, 0:1]) * (1.0 / (queries * n_dp))
            outs[6][...] = sums[9:11, 0:local_width]
            for at, row in ((8, 5), (9, 3), (10, 4), (12, 8), (14, 2), (15, 0), (16, 1)):
                outs[at][...] = sums[row : row + 1].reshape(width)

    specs = [whole(shape) for shape, _ in shapes]
    for at in big:
        specs[at] = cut(shapes[at][0][0])
    return pl.pallas_call(
        kernel,
        name="finish",
        grid=(steps,),
        out_shape=[jax.ShapeDtypeStruct(shape, kind) for shape, kind in shapes],
        in_specs=[
            cut(rows), cut(rows), cut(width), cut(width), cut(3 * local_width),
            cut(local_width, 3 * local_width // (local_width // steps)), whole((16, width)), whole((4, 16, width)),
        ],
        out_specs=specs,
    )(lout, gin, o1, o2, o3, o3, sums, firsts)


def local(
    hidden_in, token_mask, bucket, positive, qkv_weight, qv_bias, out_weight, out_bias, norm1_gain, norm1_bias,
    ffn_in, ffn_in_bias, ffn_out, ffn_out_bias, norm2_gain, norm2_bias, upstream,
):
    rows, width = hidden_in.shape
    blocks = rows // BLK
    slots = bucket.shape[0]
    queries = positive.shape[0]
    local_width = qkv_weight.shape[2]
    n_dp = lax.axis_size("dp")
    ins = dict(
        hid_in=hidden_in, mask=token_mask, bucket=bucket, positive=positive, wqkv_in=qkv_weight.transpose(0, 2, 1),
        qv_bias=qv_bias, wo_in=out_weight, ob=out_bias, g1=norm1_gain, n1b=norm1_bias, w1=ffn_in, b1=ffn_in_bias,
        w2=ffn_out, fb=ffn_out_bias, g2=norm2_gain, n2b=norm2_bias,
        upstream=upstream.reshape(blocks, 4, PIECE, width),
    )
    lout, gin, o1, o2, o3, sums, firsts = run_layer(n_dp, ins, (rows, width, slots, queries, local_width))
    lout, gin = lout.reshape(rows, width), gin.reshape(rows, width)
    outs = run_finish(lout, gin, o1, o2, o3, sums, firsts, slots, queries, local_width, n_dp)
    lout, query, passage, loss, gin, qkv, qv, gout, gob, gg1, gn1b, gf1, gb1, gf2, gfb, gg2, gn2b = outs
    qkv = qkv.reshape(3, local_width, width).transpose(0, 2, 1)
    return (
        lout, query, passage, loss.reshape(()), gin, qkv, qv, gout, gob, gg1, gn1b, gf1, gb1, gf2, gfb, gg2, gn2b
    )


def solution(mesh):
    one, two = P("dp"), P("dp", None)
    col, row = P(None, "tensor"), P("tensor", None)
    return jax.shard_map(
        local,
        mesh=mesh,
        in_specs=(
            two, one, one, one, P(None, None, "tensor"), col, row, P(), P(), P(), col, P("tensor"), row, P(), P(), P(),
            two,
        ),
        out_specs=(
            two, two, two, P(), two, P(None, None, "tensor"), col, row, P(), P(), P(), col, P("tensor"), row, P(), P(),
            P(),
        ),
        check_vma=False,
    )
```
